128 devices in a mesh: fsdp: 16 (over y_lo, z, core), tp: 8 (over x, y_hi).
Axes of the slice: x: 4, y: 4 (y_hi: 2, y_lo: 2; y = y_hi * 2 + y_lo), z: 4, core: 2. Of those that a mesh axis runs over, the one named last changes fastest.
Arguments:
- hidden: bfloat16 [2, 1280, 8192], P(None, 'fsdp'), may hold values from -6 to 6
- qkv_rows: float32 [8192, 10240], P(('fsdp', 'tp')), may hold values from -0.0625 to 0.0625
- o_rows: float32 [8192, 8192], P(('fsdp', 'tp')), may hold values from -0.0625 to 0.0625
- block_owner: int32 [2, 128], replicated, may hold values from 0 to 127, each once within a row
- cache: bfloat16 [2, 1280, 256, 1024], P(None, 'fsdp', None, 'tp'), may hold values from -240 to 240
- lengths: int32 [1280], P('fsdp'), may hold values from 32 to 256, as said below
Outputs:
- attended: bfloat16 [2, 1280, 8192], P(None, 'fsdp', 'tp')
The draws below stay inside these ranges and needn't reach their ends.
Inputs may be any that keep to these rules, and one draw needn't show every extreme that they name: Each row of block_owner is a permutation. `lengths`: the first row of each aligned block of 80 rows holds exactly 256 positions.
All inputs are finite; a program needn't handle non-finite values.
Results may differ from the reference program's by a relative error of at most 0.017.
Values may be sent and summed in bfloat16 or wider, within the bound.
No kernel may reach another device: no remote copies, remote signals or barrier semaphores. Data moves between devices by JAX's collectives and lax.ppermute only.
A program may use at most 192 MiB of HBM per device.

```python
import math
import jax
import jax.numpy as jnp
from jax import lax

D = 8192
HQ = 64
HK = 8
HD = 128
ROWS_DEV = 80
CACHE = 256
QW = 8192
QKV = 10240
BLOCKS = 128
ROWS = 1280
N_FSDP = 16
N_TP = 8


def draw_cache(key, part):
    key = jax.random.fold_in(key, 7)
    first = jax.random.fold_in(key, 0)
    base = jnp.clip(jax.random.normal(first, (2, ROWS, CACHE, HK * HD), jnp.float32), -6.0, 6.0)
    return base.astype(jnp.bfloat16)


def draw_lengths(key, part):
    key = jax.random.fold_in(key, 11)
    drawn = jax.random.randint(key, (ROWS,), CACHE // 8, CACHE + 1, jnp.int32)
    first_row = jnp.arange(ROWS, dtype=jnp.int32) % ROWS_DEV == 0
    return jnp.where(first_row, CACHE, drawn).astype(jnp.int32)


def level_of(key, shape, pieces, smallest, top_value):
    factor_of = 1.0
    for axis_at, parts in pieces:
        draws = jax.random.uniform(jax.random.fold_in(jax.random.fold_in(key, 6), axis_at), (parts,), jnp.float32, smallest / len(pieces), top_value / len(pieces))
        factor_of = factor_of * jnp.repeat(jnp.exp(draws), shape[axis_at] // parts).reshape((-1,) + (1,) * (len(shape) - 1 - axis_at))
    return factor_of


def gaussian(own_key, shape, spread, bound, shards=(), held_as=jnp.bfloat16):
    array = jax.random.normal(own_key, shape, jnp.float32) * spread
    if len(shards) > 0:
        array = level_of(own_key, shape, shards, -0.22, 0.18) * array
    return jnp.clip(array, min=-bound, max=bound).astype(held_as)


def setup_inputs(seed: int = 0) -> dict:
    splits = jax.random.split(jax.random.key(seed), 7)
    hidden = gaussian(splits[0], (2, ROWS, D), 1.0, 6.0, ((1, 16),))
    qkv_rows = gaussian(splits[1], (D, QKV), D ** -0.5, 0.0625, ((0, 128),), jnp.float32)
    o_rows = gaussian(splits[2], (D, QW), QW ** -0.5, 0.0625, ((0, 128),), jnp.float32)
    block_owner = jax.vmap(lambda own: jax.random.permutation(own, BLOCKS))(jax.random.split(splits[3], 2)).reshape((2, BLOCKS)).astype(jnp.int32)
    cache = draw_cache(jax.random.fold_in(splits[6], 71), 0)
    lengths = draw_lengths(jax.random.fold_in(splits[6], 71), 0)
    return dict(hidden=hidden, qkv_rows=qkv_rows, o_rows=o_rows, block_owner=block_owner, cache=cache, lengths=lengths)


def placed(stored, owner):
    rows, cols = stored.shape
    blocks = stored.reshape(BLOCKS, rows // BLOCKS, cols)
    return jnp.zeros_like(blocks).at[owner.astype(jnp.int32)].set(blocks).reshape(rows, cols)

def rotary(values, position):
    half = HD // 2
    freq = 1000000.0 ** (-jnp.arange(half, dtype=jnp.float32) * 2.0 / HD)
    angle = position.astype(jnp.float32)[..., None, None] * freq
    cosine = jnp.cos(angle)
    sine = jnp.sin(angle)
    first = values[..., :half]
    second = values[..., half:]
    return jnp.concatenate([first * cosine - second * sine, second * cosine + first * sine], axis=-1)

def attend(query, new_keys, new_vals, keys, vals, lens):
    factor = 1.0 / math.sqrt(HD)
    query = query.astype(jnp.float32)
    old = jnp.einsum('srgjd,rpgd->srgjp', query, keys.astype(jnp.float32)) * factor
    fresh = jnp.einsum('srgjd,trgd->srgjt', query, new_keys.astype(jnp.float32)) * factor
    live = jnp.arange(CACHE)[None, :] < lens[:, None]
    old = jnp.where(live[None, :, None, None, :], old, -jnp.inf)
    seen = jnp.arange(2)[None, :] <= jnp.arange(2)[:, None]
    fresh = jnp.where(seen[:, None, None, None, :], fresh, -jnp.inf)
    top = jnp.maximum(lax.optimization_barrier(jnp.max(old, -1)), lax.optimization_barrier(jnp.max(fresh, -1)))[..., None]
    old_w = jnp.exp(old - top)
    fresh_w = jnp.exp(fresh - top)
    total = lax.optimization_barrier(jnp.sum(old_w, -1, keepdims=True)) + lax.optimization_barrier(jnp.sum(fresh_w, -1, keepdims=True))
    old_p = (old_w / total).astype(jnp.bfloat16)
    fresh_p = (fresh_w / total).astype(jnp.bfloat16)
    mixed = jnp.einsum('srgjp,rpgd->srgjd', old_p.astype(jnp.float32), vals.astype(jnp.float32))
    mixed = mixed + jnp.einsum('srgjt,trgd->srgjd', fresh_p.astype(jnp.float32), new_vals.astype(jnp.float32))
    return mixed.astype(jnp.bfloat16)

def reference(hidden, qkv_rows, o_rows, block_owner, cache, lengths):
    query_cols = HQ * HD
    kv_cols = HK * HD
    w_qkv = placed(qkv_rows.astype(jnp.bfloat16), block_owner[0])
    w_out = placed(o_rows.astype(jnp.bfloat16), block_owner[1])
    per_group = hidden.reshape(2, N_FSDP, ROWS_DEV, D).transpose(1, 0, 2, 3)
    key_group = cache[0].reshape(N_FSDP, ROWS_DEV, CACHE, kv_cols)
    val_group = cache[1].reshape(N_FSDP, ROWS_DEV, CACHE, kv_cols)
    len_group = lengths.reshape(N_FSDP, ROWS_DEV)

    def one_group(items):
        inputs, keys, vals, lens = items
        rows = inputs.shape[1]
        proj = jnp.dot(inputs.reshape(2 * rows, D), w_qkv, preferred_element_type=jnp.float32).reshape(2, rows, -1)
        position = lens[None, :] + jnp.arange(2, dtype=jnp.int32)[:, None]
        query = rotary(proj[..., :query_cols].reshape(2, rows, HQ, HD), position).astype(jnp.bfloat16)
        new_keys = rotary(proj[..., query_cols:query_cols + kv_cols].reshape(2, rows, HK, HD), position).astype(jnp.bfloat16)
        new_vals = proj[..., query_cols + kv_cols:].reshape(2, rows, HK, HD).astype(jnp.bfloat16)
        mixed = attend(query.reshape(2, rows, HK, HQ // HK, HD), new_keys, new_vals, keys.reshape(rows, CACHE, HK, HD), vals.reshape(rows, CACHE, HK, HD), lens)
        mixed = mixed.reshape(2 * rows, HQ * HD)
        span = HQ // N_TP * HD
        total = jnp.zeros((2 * rows, D), jnp.float32)
        for group in range(N_TP):
            piece = mixed[:, group * span:(group + 1) * span]
            term = jnp.dot(piece, w_out[:, group * span:(group + 1) * span].T, preferred_element_type=jnp.float32)
            total = total + lax.optimization_barrier(term.astype(jnp.bfloat16)).astype(jnp.float32)
        return total.astype(jnp.bfloat16).reshape(2, rows, D)
    result = lax.map(one_group, (per_group, key_group, val_group, len_group))
    return result.transpose(1, 0, 2, 3).reshape(2, ROWS, D)
```

```python
import functools
import math

import jax
import jax.numpy as jnp
from jax import lax
from jax.experimental import pallas as pl
from jax.experimental.pallas import tpu as pltpu
from jax.sharding import PartitionSpec as P

HQ = 64
HK = 8
HD = 128
NZ = 4
MIB = 1024 * 1024


def z_shift(value, k):
    pairs = [(f, (f // 8) * 8 + ((f // 2 + k) % NZ) * 2 + f % 2) for f in range(16)]
    return lax.ppermute(value, "fsdp", pairs)


def flip(value, bit):
    return lax.ppermute(value, "fsdp", [(f, f ^ bit) for f in range(16)])


def by_group(array, sections, groups):
    pieces = []
    begin = 0
    for width in sections:
        pieces.append(
            array[:, begin : begin + width].reshape(array.shape[0], groups, width // groups)
        )
        begin = begin + width
    return jnp.concatenate(pieces, axis=2)


def flatten(received):
    return received.reshape(received.shape[0], received.shape[2])


def shuffle_kernel(owner_ref, hidden_ref, *out_refs):
    f = lax.axis_index("fsdp")
    y_lo, z, core = f // 8, lax.rem(f // 2, 4), lax.rem(f, 2)
    rows = hidden_ref.shape[0]
    low = lax.broadcasted_iota(jnp.int32, (rows, 128), 1) < 64

    for k, out_ref in enumerate(out_refs):
        zz = lax.rem(z + k, 4)

        def step(n, carry, zz=zz, out_ref=out_ref):
            q, p = n // 4, lax.rem(n, 4)
            yy = lax.rem(y_lo + lax.rem(q, 2), 2)
            cc = lax.rem(core + q // 2, 2)
            i = yy * 64 + zz * 16 + cc * 8 + 2 * p
            s0, s1 = owner_ref[0, i], owner_ref[0, i + 1]
            a = hidden_ref[:, pl.ds(pl.multiple_of((s0 // 2) * 128, 128), 128)].astype(jnp.float32)
            b = hidden_ref[:, pl.ds(pl.multiple_of((s1 // 2) * 128, 128), 128)].astype(jnp.float32)
            a = pltpu.roll(a, 64 * lax.rem(s0, 2), 1)
            b = pltpu.roll(b, 64 * (1 - lax.rem(s1, 2)), 1)
            out_ref[:, pl.ds(pl.multiple_of(n * 128, 128), 128)] = jnp.where(low, a, b).astype(
                jnp.bfloat16
            )
            return carry

        lax.fori_loop(0, 16, step, 0)


def shuffle(hidden, block_owner):
    rows, width = hidden.shape
    part = jax.ShapeDtypeStruct((rows, width // NZ), jnp.bfloat16)
    return pl.pallas_call(
        shuffle_kernel,
        out_shape=[part] * NZ,
        in_specs=[
            pl.BlockSpec(memory_space=pltpu.SMEM),
            pl.BlockSpec(memory_space=pltpu.VMEM),
        ],
        out_specs=[pl.BlockSpec(memory_space=pltpu.VMEM)] * NZ,
        compiler_params=pltpu.CompilerParams(vmem_limit_bytes=24 * MIB),
        cost_estimate=pl.CostEstimate(
            flops=rows * width * 8, bytes_accessed=4 * rows * width, transcendentals=0
        ),
        name="shuffle",
    )(block_owner, hidden)


def partial_kernel(h0, h1, h2, h3, w0, w1, w2, w3, p0, p1, p2, p3, stacked):
    rows = h0.shape[0]

    @pl.when(pl.program_id(0) == 0)
    def _():
        for k, h in enumerate((h0, h1, h2, h3)):
            stacked[pl.ds(k * rows, rows), :] = h[...]

    depth = w0.shape[0]
    total = jnp.zeros((NZ * rows, w0.shape[1]), jnp.float32)
    for q, w in enumerate((w0, w1, w2, w3)):
        total = total + jnp.dot(
            stacked[:, q * depth : (q + 1) * depth], w[...], preferred_element_type=jnp.float32
        )
    for k, out in enumerate((p0, p1, p2, p3)):
        out[...] = total[k * rows : (k + 1) * rows].astype(out.dtype)


def partials(parts, weights):
    rows, width = parts[0].shape
    depth, cols = weights[0].shape
    tile = 256
    return pl.pallas_call(
        partial_kernel,
        grid=(cols // tile,),
        out_shape=[jax.ShapeDtypeStruct((rows, cols), jnp.float32)]
        + [jax.ShapeDtypeStruct((rows, cols), jnp.bfloat16)] * 3,
        in_specs=[pl.BlockSpec((rows, width), lambda j: (0, 0))] * NZ
        + [pl.BlockSpec((depth, tile), lambda j: (0, j))] * NZ,
        out_specs=[pl.BlockSpec((rows, tile), lambda j: (0, j))] * NZ,
        scratch_shapes=[pltpu.VMEM((NZ * rows, width), jnp.bfloat16)],
        compiler_params=pltpu.CompilerParams(vmem_limit_bytes=32 * MIB),
        cost_estimate=pl.CostEstimate(
            flops=2 * NZ * rows * width * cols,
            bytes_accessed=2 * (NZ * rows * width + width * cols + NZ * rows * cols),
            transcendentals=0,
        ),
        name="partials",
    )(*parts, *weights)


def back_kernel(blocks, owned, owner_ref, mixed_ref, weight_ref, out_ref, place, held, sems):
    t = pl.program_id(0)
    steps = pl.num_programs(0)

    @pl.when(t == 0)
    def _():
        def note(i, carry):
            place[owner_ref[1, i]] = i
            return carry

        lax.fori_loop(0, owner_ref.shape[1], note, 0)

    def fetch(step, slot):
        def one(j, carry):
            source = place[step * blocks + j]
            pltpu.make_async_copy(
                weight_ref.at[pl.ds(pl.multiple_of(source * owned, owned), owned)],
                held.at[slot, pl.ds(pl.multiple_of(j * owned, owned), owned)],
                sems.at[slot],
            ).start()
            return carry

        lax.fori_loop(0, blocks, one, 0)

    slot = lax.rem(t, 2)

    @pl.when(t == 0)
    def _():
        fetch(t, slot)

    @pl.when(t + 1 < steps)
    def _():
        fetch(t + 1, 1 - slot)

    pltpu.make_async_copy(
        weight_ref.at[pl.ds(0, blocks * owned)], held.at[slot], sems.at[slot]
    ).wait()
    out_ref[0] = lax.dot_general(
        mixed_ref[...],
        held[slot],
        (((1,), (1,)), ((), ())),
        preferred_element_type=jnp.float32,
    ).astype(out_ref.dtype)


def project_back(mixed, weight, block_owner, groups):
    rows, depth = mixed.shape
    width = weight.shape[0]
    total = block_owner.shape[1]
    blocks, owned = total // groups, width // total
    return pl.pallas_call(
        functools.partial(back_kernel, blocks, owned),
        grid=(groups,),
        out_shape=jax.ShapeDtypeStruct((groups, rows, width // groups), jnp.bfloat16),
        in_specs=[
            pl.BlockSpec(memory_space=pltpu.SMEM),
            pl.BlockSpec((rows, depth), lambda t: (0, 0)),
            pl.BlockSpec(memory_space=pltpu.HBM),
        ],
        out_specs=pl.BlockSpec((1, rows, width // groups), lambda t: (t, 0, 0)),
        scratch_shapes=[
            pltpu.SMEM((total,), jnp.int32),
            pltpu.VMEM((2, width // groups, depth), jnp.bfloat16),
            pltpu.SemaphoreType.DMA((2,)),
        ],
        compiler_params=pltpu.CompilerParams(vmem_limit_bytes=54 * MIB),
        cost_estimate=pl.CostEstimate(
            flops=2 * rows * depth * width,
            bytes_accessed=2 * (rows * depth + depth * width + rows * width),
            transcendentals=0,
        ),
        name="project_back",
    )(block_owner, mixed, weight)


def rotary(values, position):
    half = HD // 2
    freq = 1000000.0 ** (-jnp.arange(half, dtype=jnp.float32) * 2.0 / HD)
    angle = position.astype(jnp.float32)[..., None, None] * freq
    cosine = jnp.cos(angle)
    sine = jnp.sin(angle)
    first = values[..., :half]
    second = values[..., half:]
    return jnp.concatenate(
        [first * cosine - second * sine, second * cosine + first * sine], axis=-1
    )


def attention(proj, cache, lengths, groups):
    rows = lengths.shape[0]
    heads = HQ // groups
    kv_heads = HK // groups
    query_cols = heads * HD
    kv_cols = kv_heads * HD
    proj = proj.reshape(2, rows, -1)
    position = lengths[None, :] + jnp.arange(2, dtype=jnp.int32)[:, None]
    query = rotary(proj[..., :query_cols].reshape(2, rows, heads, HD), position).astype(
        jnp.bfloat16
    )
    new_keys = rotary(
        proj[..., query_cols : query_cols + kv_cols].reshape(2, rows, kv_heads, HD), position
    ).astype(jnp.bfloat16)
    new_vals = proj[..., query_cols + kv_cols :].reshape(2, rows, kv_heads, HD).astype(jnp.bfloat16)
    query = query.reshape(2, rows, kv_heads, HQ // HK, HD)
    keys = cache[0].reshape(rows, -1, kv_heads, HD)
    vals = cache[1].reshape(rows, -1, kv_heads, HD)
    factor = 1.0 / math.sqrt(HD)
    old = jnp.einsum("srgjd,rpgd->srgjp", query, keys, preferred_element_type=jnp.float32) * factor
    fresh = (
        jnp.einsum("srgjd,trgd->srgjt", query, new_keys, preferred_element_type=jnp.float32)
        * factor
    )
    live = jnp.arange(keys.shape[1])[None, :] < lengths[:, None]
    old = jnp.where(live[None, :, None, None, :], old, -jnp.inf)
    seen = jnp.arange(2)[None, :] <= jnp.arange(2)[:, None]
    fresh = jnp.where(seen[:, None, None, None, :], fresh, -jnp.inf)
    top = jnp.maximum(jnp.max(old, -1), jnp.max(fresh, -1))[..., None]
    old_w = jnp.exp(old - top)
    fresh_w = jnp.exp(fresh - top)
    total = jnp.sum(old_w, -1, keepdims=True) + jnp.sum(fresh_w, -1, keepdims=True)
    old_p = (old_w / total).astype(jnp.bfloat16)
    fresh_p = (fresh_w / total).astype(jnp.bfloat16)
    mixed = jnp.einsum("srgjp,rpgd->srgjd", old_p, vals, preferred_element_type=jnp.float32)
    mixed = mixed + jnp.einsum(
        "srgjt,trgd->srgjd", fresh_p, new_vals, preferred_element_type=jnp.float32
    )
    return mixed.astype(jnp.bfloat16).reshape(2 * rows, query_cols)


def body(hidden, qkv_rows, o_rows, block_owner, cache, lengths):
    groups = lax.axis_size("tp")
    steps, rows, width = hidden.shape
    owned = qkv_rows.shape[0]
    query_cols = HQ * HD
    kv_cols = HK * HD
    qkv_copy = by_group(qkv_rows.astype(jnp.bfloat16), (query_cols, kv_cols, kv_cols), groups)
    out_copy = o_rows.astype(jnp.bfloat16).reshape(owned, groups, query_cols // groups)

    parts = shuffle(hidden.reshape(steps * rows, width), block_owner)
    qkv_copy, out_copy, *parts = lax.optimization_barrier((qkv_copy, out_copy, *parts))
    parts = [parts[0]] + [z_shift(parts[k], k) for k in range(1, NZ)]

    w = flatten(lax.all_to_all(qkv_copy, "tp", split_axis=1, concat_axis=0, tiled=True))
    w_y = flip(w, 8)
    w_c = flip(w, 1)
    w_yc = flip(w_y, 1)
    sums = partials(parts, (w, w_y, w_c, w_yc))
    got_o = lax.all_to_all(out_copy, "tp", split_axis=1, concat_axis=0, tiled=True)
    whole_o = lax.all_gather(flatten(got_o), "fsdp", axis=0, tiled=True)

    proj = sums[0]
    for k in range(1, NZ):
        proj = proj + z_shift(sums[k], -k).astype(jnp.float32)
    mixed = attention(proj, cache, lengths, groups)
    terms = project_back(mixed, whole_o, block_owner, groups)
    terms = lax.all_to_all(terms, "tp", split_axis=0, concat_axis=0, tiled=True)
    summed = jnp.sum(terms.astype(jnp.float32), axis=0).astype(jnp.bfloat16)
    return summed.reshape(steps, rows, width // groups)


def solution(mesh):
    in_specs = (
        P(None, "fsdp", None),
        P(("fsdp", "tp"), None),
        P(("fsdp", "tp"), None),
        P(),
        P(None, "fsdp", None, "tp"),
        P("fsdp"),
    )
    out_specs = P(None, "fsdp", "tp")
    return jax.shard_map(body, mesh=mesh, in_specs=in_specs, out_specs=out_specs, check_vma=False)
```

```python
import functools
import math

import jax
import jax.numpy as jnp
from jax import lax
from jax.experimental import pallas as pl
from jax.experimental.pallas import tpu as pltpu
from jax.sharding import PartitionSpec as P

HQ = 64
HK = 8
HD = 128
NZ = 4
MIB = 1024 * 1024


def z_shift(value, k):
    pairs = [(f, (f // 8) * 8 + ((f // 2 + k) % NZ) * 2 + f % 2) for f in range(16)]
    return lax.ppermute(value, "fsdp", pairs)


def flip(value, bit):
    return lax.ppermute(value, "fsdp", [(f, f ^ bit) for f in range(16)])


def by_group(array, sections, groups):
    pieces = []
    begin = 0
    for width in sections:
        pieces.append(
            array[:, begin : begin + width].reshape(array.shape[0], groups, width // groups)
        )
        begin = begin + width
    return jnp.concatenate(pieces, axis=2)


def flatten(received):
    return received.reshape(received.shape[0], received.shape[2])


def shuffle_kernel(owner_ref, hidden_ref, *out_refs):
    f = lax.axis_index("fsdp")
    y_lo, z, core = f // 8, lax.rem(f // 2, 4), lax.rem(f, 2)
    rows = hidden_ref.shape[0]
    low = lax.broadcasted_iota(jnp.int32, (rows, 128), 1) < 64

    for k, out_ref in enumerate(out_refs):
        zz = lax.rem(z + k, 4)

        def step(n, carry, zz=zz, out_ref=out_ref):
            q, p = n // 4, lax.rem(n, 4)
            yy = lax.rem(y_lo + lax.rem(q, 2), 2)
            cc = lax.rem(core + q // 2, 2)
            i = yy * 64 + zz * 16 + cc * 8 + 2 * p
            s0, s1 = owner_ref[0, i], owner_ref[0, i + 1]
            a = hidden_ref[:, pl.ds(pl.multiple_of((s0 // 2) * 128, 128), 128)].astype(jnp.float32)
            b = hidden_ref[:, pl.ds(pl.multiple_of((s1 // 2) * 128, 128), 128)].astype(jnp.float32)
            a = pltpu.roll(a, 64 * lax.rem(s0, 2), 1)
            b = pltpu.roll(b, 64 * (1 - lax.rem(s1, 2)), 1)
            out_ref[:, pl.ds(pl.multiple_of(n * 128, 128), 128)] = jnp.where(low, a, b).astype(
                jnp.bfloat16
            )
            return carry

        lax.fori_loop(0, 16, step, 0, unroll=4)


def shuffle(hidden, block_owner):
    rows, width = hidden.shape
    part = jax.ShapeDtypeStruct((rows, width // NZ), jnp.bfloat16)
    return pl.pallas_call(
        shuffle_kernel,
        out_shape=[part] * NZ,
        in_specs=[
            pl.BlockSpec(memory_space=pltpu.SMEM),
            pl.BlockSpec(memory_space=pltpu.VMEM),
        ],
        out_specs=[pl.BlockSpec(memory_space=pltpu.VMEM)] * NZ,
        compiler_params=pltpu.CompilerParams(vmem_limit_bytes=24 * MIB),
        cost_estimate=pl.CostEstimate(
            flops=rows * width * 8, bytes_accessed=4 * rows * width, transcendentals=0
        ),
        name="shuffle",
    )(block_owner, hidden)


def partial_kernel(h0, h1, h2, h3, w0, w1, w2, w3, p0, p1, p2, p3, stacked):
    rows = h0.shape[0]

    @pl.when(pl.program_id(0) == 0)
    def _():
        for k, h in enumerate((h0, h1, h2, h3)):
            stacked[pl.ds(k * rows, rows), :] = h[...]

    depth = w0.shape[0]
    total = jnp.zeros((NZ * rows, w0.shape[1]), jnp.float32)
    for q, w in enumerate((w0, w1, w2, w3)):
        total = total + jnp.dot(
            stacked[:, q * depth : (q + 1) * depth], w[...], preferred_element_type=jnp.float32
        )
    for k, out in enumerate((p0, p1, p2, p3)):
        out[...] = total[k * rows : (k + 1) * rows].astype(out.dtype)


def partials(parts, weights):
    rows, width = parts[0].shape
    depth, cols = weights[0].shape
    tile = 256
    return pl.pallas_call(
        partial_kernel,
        grid=(cols // tile,),
        out_shape=[jax.ShapeDtypeStruct((rows, cols), jnp.float32)]
        + [jax.ShapeDtypeStruct((rows, cols), jnp.bfloat16)] * 3,
        in_specs=[pl.BlockSpec((rows, width), lambda j: (0, 0))] * NZ
        + [pl.BlockSpec((depth, tile), lambda j: (0, j))] * NZ,
        out_specs=[pl.BlockSpec((rows, tile), lambda j: (0, j))] * NZ,
        scratch_shapes=[pltpu.VMEM((NZ * rows, width), jnp.bfloat16)],
        compiler_params=pltpu.CompilerParams(vmem_limit_bytes=32 * MIB),
        cost_estimate=pl.CostEstimate(
            flops=2 * NZ * rows * width * cols,
            bytes_accessed=2 * (NZ * rows * width + width * cols + NZ * rows * cols),
            transcendentals=0,
        ),
        name="partials",
    )(*parts, *weights)


def back_kernel(spots, groups, owner_ref, mixed_ref, *refs):
    count = len(spots)
    sources, out_ref, held, placed, sems = refs[:count], *refs[count:]
    f = lax.axis_index("fsdp")
    y_lo, z, core = f // 8, lax.rem(f // 2, NZ), lax.rem(f, 2)
    rows, depth = mixed_ref.shape
    width = held.shape[0]
    owned = width // owner_ref.shape[1]

    copies = []
    begin = 0
    for n, source in enumerate(sources):
        size = source.shape[0]
        copies.append(
            pltpu.make_async_copy(source, held.at[pl.ds(begin, size)], sems.at[n])
        )
        copies[-1].start()
        begin += size
    turned = mixed_ref[...].astype(jnp.float32).T.astype(jnp.bfloat16)

    begin = 0
    for n, (dy, dz, dc, t0) in enumerate(spots):
        size = sources[n].shape[0]
        first = (
            lax.rem(y_lo + dy, 2) * 64 + lax.rem(z + dz, NZ) * 16 + lax.rem(core + dc, 2) * 8 + t0
        )
        copies[n].wait()
        terms = jnp.dot(held[begin : begin + size], turned, preferred_element_type=jnp.float32)
        terms = terms.astype(jnp.bfloat16)
        for b in range(size // owned):
            spot = pl.multiple_of(owner_ref[1, first + b] * owned, owned)
            placed[pl.ds(spot, owned), :] = terms[b * owned : (b + 1) * owned]
        begin += size

    slab = width // groups
    for t in range(groups):
        out_ref[t] = placed[t * slab : (t + 1) * slab].T


def project_back(mixed, sources, spots, block_owner, groups):
    rows, depth = mixed.shape
    width = sum(source.shape[0] for source in sources)
    return pl.pallas_call(
        functools.partial(back_kernel, spots, groups),
        out_shape=jax.ShapeDtypeStruct((groups, rows, width // groups), jnp.bfloat16),
        in_specs=[
            pl.BlockSpec(memory_space=pltpu.SMEM),
            pl.BlockSpec(memory_space=pltpu.VMEM),
        ]
        + [pl.BlockSpec(memory_space=pl.ANY)] * len(sources),
        out_specs=pl.BlockSpec(memory_space=pltpu.VMEM),
        scratch_shapes=[
            pltpu.VMEM((width, depth), jnp.bfloat16),
            pltpu.VMEM((width, rows), jnp.bfloat16),
            pltpu.SemaphoreType.DMA((len(sources),)),
        ],
        compiler_params=pltpu.CompilerParams(vmem_limit_bytes=48 * MIB),
        cost_estimate=pl.CostEstimate(
            flops=2 * rows * depth * width,
            bytes_accessed=2 * (rows * depth + depth * width + rows * width),
            transcendentals=0,
        ),
        name="project_back",
    )(block_owner, mixed, *sources)


def gather_rows(own):
    half = own.shape[0] // 2
    across = flip(own, 8)
    below, above = z_shift(own, 1), z_shift(own, -1)
    far_a, far_b = z_shift(above[:half], -1), z_shift(below[half:], 1)
    across_below, across_above = z_shift(across, 1), z_shift(across, -1)
    across_far_a, across_far_b = flip(far_a, 8), flip(far_b, 8)
    held = [
        (own, (0, 0), 0),
        (across, (1, 0), 0),
        (below, (0, 3), 0),
        (above, (0, 1), 0),
        (far_a, (0, 2), 0),
        (far_b, (0, 2), 4),
        (across_below, (1, 3), 0),
        (across_above, (1, 1), 0),
        (across_far_a, (1, 2), 0),
        (across_far_b, (1, 2), 4),
    ]
    sources = [value for value, _, _ in held] + [flip(value, 1) for value, _, _ in held]
    spots = [(*at, core, t0) for core in (0, 1) for _, at, t0 in held]
    return sources, tuple(spots)


def rotary(values, position):
    half = HD // 2
    freq = 1000000.0 ** (-jnp.arange(half, dtype=jnp.float32) * 2.0 / HD)
    angle = position.astype(jnp.float32)[..., None, None] * freq
    cosine = jnp.cos(angle)
    sine = jnp.sin(angle)
    first = values[..., :half]
    second = values[..., half:]
    return jnp.concatenate(
        [first * cosine - second * sine, second * cosine + first * sine], axis=-1
    )


def attention(proj, cache, lengths, groups):
    rows = lengths.shape[0]
    heads = HQ // groups
    kv_heads = HK // groups
    query_cols = heads * HD
    kv_cols = kv_heads * HD
    proj = proj.reshape(2, rows, -1)
    position = lengths[None, :] + jnp.arange(2, dtype=jnp.int32)[:, None]
    query = rotary(proj[..., :query_cols].reshape(2, rows, heads, HD), position).astype(
        jnp.bfloat16
    )
    new_keys = rotary(
        proj[..., query_cols : query_cols + kv_cols].reshape(2, rows, kv_heads, HD), position
    ).astype(jnp.bfloat16)
    new_vals = proj[..., query_cols + kv_cols :].reshape(2, rows, kv_heads, HD).astype(jnp.bfloat16)
    query = query.reshape(2, rows, kv_heads, HQ // HK, HD)
    keys = cache[0].reshape(rows, -1, kv_heads, HD)
    vals = cache[1].reshape(rows, -1, kv_heads, HD)
    factor = 1.0 / math.sqrt(HD)
    old = jnp.einsum("srgjd,rpgd->srgjp", query, keys, preferred_element_type=jnp.float32) * factor
    fresh = (
        jnp.einsum("srgjd,trgd->srgjt", query, new_keys, preferred_element_type=jnp.float32)
        * factor
    )
    live = jnp.arange(keys.shape[1])[None, :] < lengths[:, None]
    old = jnp.where(live[None, :, None, None, :], old, -jnp.inf)
    seen = jnp.arange(2)[None, :] <= jnp.arange(2)[:, None]
    fresh = jnp.where(seen[:, None, None, None, :], fresh, -jnp.inf)
    top = jnp.maximum(jnp.max(old, -1), jnp.max(fresh, -1))[..., None]
    old_w = jnp.exp(old - top)
    fresh_w = jnp.exp(fresh - top)
    total = jnp.sum(old_w, -1, keepdims=True) + jnp.sum(fresh_w, -1, keepdims=True)
    old_p = (old_w / total).astype(jnp.bfloat16)
    fresh_p = (fresh_w / total).astype(jnp.bfloat16)
    mixed = jnp.einsum("srgjp,rpgd->srgjd", old_p, vals, preferred_element_type=jnp.float32)
    mixed = mixed + jnp.einsum(
        "srgjt,trgd->srgjd", fresh_p, new_vals, preferred_element_type=jnp.float32
    )
    return mixed.astype(jnp.bfloat16).reshape(2 * rows, query_cols)


def body(hidden, qkv_rows, o_rows, block_owner, cache, lengths):
    groups = lax.axis_size("tp")
    steps, rows, width = hidden.shape
    owned = qkv_rows.shape[0]
    query_cols = HQ * HD
    kv_cols = HK * HD
    qkv_copy = by_group(qkv_rows.astype(jnp.bfloat16), (query_cols, kv_cols, kv_cols), groups)
    out_copy = o_rows.astype(jnp.bfloat16).reshape(owned, groups, query_cols // groups)

    parts = shuffle(hidden.reshape(steps * rows, width), block_owner)
    qkv_copy, out_copy, *parts = lax.optimization_barrier((qkv_copy, out_copy, *parts))
    parts = [parts[0]] + [z_shift(parts[k], k) for k in range(1, NZ)]

    w = flatten(lax.all_to_all(qkv_copy, "tp", split_axis=1, concat_axis=0, tiled=True))
    w, out_copy = lax.optimization_barrier((w, out_copy))
    w_y = flip(w, 8)
    w_c = flip(w, 1)
    w_yc = flip(w_y, 1)
    got_o = flatten(lax.all_to_all(out_copy, "tp", split_axis=1, concat_axis=0, tiled=True))
    sums = partials(parts, (w, w_y, w_c, w_yc))
    sources, spots = gather_rows(got_o)

    proj = sums[0]
    for k in range(1, NZ):
        proj = proj + z_shift(sums[k], -k).astype(jnp.float32)
    mixed = attention(proj, cache, lengths, groups)
    terms = project_back(mixed, sources, spots, block_owner, groups)
    terms = lax.all_to_all(terms, "tp", split_axis=0, concat_axis=0, tiled=True)
    summed = jnp.sum(terms.astype(jnp.float32), axis=0).astype(jnp.bfloat16)
    return summed.reshape(steps, rows, width // groups)


def solution(mesh):
    in_specs = (
        P(None, "fsdp", None),
        P(("fsdp", "tp"), None),
        P(("fsdp", "tp"), None),
        P(),
        P(None, "fsdp", None, "tp"),
        P("fsdp"),
    )
    out_specs = P(None, "fsdp", "tp")
    return jax.shard_map(body, mesh=mesh, in_specs=in_specs, out_specs=out_specs, check_vma=False)
```

```python
import functools
import math

import jax
import jax.numpy as jnp
from jax import lax
from jax.experimental import pallas as pl
from jax.experimental.pallas import tpu as pltpu
from jax.sharding import PartitionSpec as P

HQ = 64
HK = 8
HD = 128
NZ = 4
MIB = 1024 * 1024


def z_shift(value, k):
    pairs = [(f, (f // 8) * 8 + ((f // 2 + k) % NZ) * 2 + f % 2) for f in range(16)]
    return lax.ppermute(value, "fsdp", pairs)


def flip(value, bit):
    return lax.ppermute(value, "fsdp", [(f, f ^ bit) for f in range(16)])


def by_group(array, sections, groups):
    pieces = []
    begin = 0
    for width in sections:
        pieces.append(
            array[:, begin : begin + width].reshape(array.shape[0], groups, width // groups)
        )
        begin = begin + width
    return jnp.concatenate(pieces, axis=2)


def flatten(received):
    return received.reshape(received.shape[0], received.shape[2])


def shuffle_kernel(owner_ref, hidden_ref, *out_refs):
    f = lax.axis_index("fsdp")
    y_lo, z, core = f // 8, lax.rem(f // 2, 4), lax.rem(f, 2)
    rows = hidden_ref.shape[0]
    low = lax.broadcasted_iota(jnp.int32, (rows, 128), 1) < 64

    for k, out_ref in enumerate(out_refs):
        zz = lax.rem(z + k, 4)

        def step(n, carry, zz=zz, out_ref=out_ref):
            q, p = n // 4, lax.rem(n, 4)
            yy = lax.rem(y_lo + lax.rem(q, 2), 2)
            cc = lax.rem(core + q // 2, 2)
            i = yy * 64 + zz * 16 + cc * 8 + 2 * p
            s0, s1 = owner_ref[0, i], owner_ref[0, i + 1]
            a = hidden_ref[:, pl.ds(pl.multiple_of((s0 // 2) * 128, 128), 128)].astype(jnp.float32)
            b = hidden_ref[:, pl.ds(pl.multiple_of((s1 // 2) * 128, 128), 128)].astype(jnp.float32)
            a = pltpu.roll(a, 64 * lax.rem(s0, 2), 1)
            b = pltpu.roll(b, 64 * (1 - lax.rem(s1, 2)), 1)
            out_ref[:, pl.ds(pl.multiple_of(n * 128, 128), 128)] = jnp.where(low, a, b).astype(
                jnp.bfloat16
            )
            return carry

        lax.fori_loop(0, 16, step, 0, unroll=4)


def shuffle(hidden, block_owner):
    rows, width = hidden.shape
    part = jax.ShapeDtypeStruct((rows, width // NZ), jnp.bfloat16)
    return pl.pallas_call(
        shuffle_kernel,
        out_shape=[part] * NZ,
        in_specs=[
            pl.BlockSpec(memory_space=pltpu.SMEM),
            pl.BlockSpec(memory_space=pltpu.VMEM),
        ],
        out_specs=[pl.BlockSpec(memory_space=pltpu.VMEM)] * NZ,
        compiler_params=pltpu.CompilerParams(vmem_limit_bytes=24 * MIB),
        cost_estimate=pl.CostEstimate(
            flops=rows * width * 8, bytes_accessed=4 * rows * width, transcendentals=0
        ),
        name="shuffle",
    )(block_owner, hidden)


def partial_kernel(h0, h1, h2, h3, w0, w1, w2, w3, p0, p1, p2, p3, stacked):
    rows = h0.shape[0]

    @pl.when(pl.program_id(0) == 0)
    def _():
        for k, h in enumerate((h0, h1, h2, h3)):
            stacked[pl.ds(k * rows, rows), :] = h[...]

    depth = w0.shape[0]
    total = jnp.zeros((NZ * rows, w0.shape[1]), jnp.float32)
    for q, w in enumerate((w0, w1, w2, w3)):
        total = total + jnp.dot(
            stacked[:, q * depth : (q + 1) * depth], w[...], preferred_element_type=jnp.float32
        )
    for k, out in enumerate((p0, p1, p2, p3)):
        out[...] = total[k * rows : (k + 1) * rows].astype(out.dtype)


def partials(parts, weights):
    rows, width = parts[0].shape
    depth, cols = weights[0].shape
    tile = 256
    return pl.pallas_call(
        partial_kernel,
        grid=(cols // tile,),
        out_shape=[jax.ShapeDtypeStruct((rows, cols), jnp.float32)]
        + [jax.ShapeDtypeStruct((rows, cols), jnp.bfloat16)] * 3,
        in_specs=[pl.BlockSpec((rows, width), lambda j: (0, 0))] * NZ
        + [pl.BlockSpec((depth, tile), lambda j: (0, j))] * NZ,
        out_specs=[pl.BlockSpec((rows, tile), lambda j: (0, j))] * NZ,
        scratch_shapes=[pltpu.VMEM((NZ * rows, width), jnp.bfloat16)],
        compiler_params=pltpu.CompilerParams(vmem_limit_bytes=32 * MIB),
        cost_estimate=pl.CostEstimate(
            flops=2 * NZ * rows * width * cols,
            bytes_accessed=2 * (NZ * rows * width + width * cols + NZ * rows * cols),
            transcendentals=0,
        ),
        name="partials",
    )(*parts, *weights)


def back_kernel(spots, groups, owner_ref, mixed_ref, *refs):
    count = len(spots)
    sources, out_ref, held, placed, sems = refs[:count], *refs[count:]
    f = lax.axis_index("fsdp")
    y_lo, z, core = f // 8, lax.rem(f // 2, NZ), lax.rem(f, 2)
    rows, depth = mixed_ref.shape
    width = held.shape[0]
    owned = width // owner_ref.shape[1]

    copies = []
    begin = 0
    for n, source in enumerate(sources):
        size = source.shape[0]
        copies.append(
            pltpu.make_async_copy(source, held.at[pl.ds(begin, size)], sems.at[n])
        )
        copies[-1].start()
        begin += size
    turned = mixed_ref[...].astype(jnp.float32).T.astype(jnp.bfloat16)

    begin = 0
    for n, (dy, dz, dc, t0) in enumerate(spots):
        size = sources[n].shape[0]
        first = (
            lax.rem(y_lo + dy, 2) * 64 + lax.rem(z + dz, NZ) * 16 + lax.rem(core + dc, 2) * 8 + t0
        )
        copies[n].wait()
        terms = jnp.dot(held[begin : begin + size], turned, preferred_element_type=jnp.float32)
        terms = terms.astype(jnp.bfloat16)
        for b in range(size // owned):
            spot = pl.multiple_of(owner_ref[1, first + b] * owned, owned)
            placed[pl.ds(spot, owned), :] = terms[b * owned : (b + 1) * owned]
        begin += size

    slab = width // groups
    for t in range(groups):
        out_ref[t] = placed[t * slab : (t + 1) * slab].T


def project_back(mixed, sources, spots, block_owner, groups):
    rows, depth = mixed.shape
    width = sum(source.shape[0] for source in sources)
    return pl.pallas_call(
        functools.partial(back_kernel, spots, groups),
        out_shape=jax.ShapeDtypeStruct((groups, rows, width // groups), jnp.bfloat16),
        in_specs=[
            pl.BlockSpec(memory_space=pltpu.SMEM),
            pl.BlockSpec(memory_space=pltpu.VMEM),
        ]
        + [pl.BlockSpec(memory_space=pl.ANY)] * len(sources),
        out_specs=pl.BlockSpec(memory_space=pltpu.VMEM),
        scratch_shapes=[
            pltpu.VMEM((width, depth), jnp.bfloat16),
            pltpu.VMEM((width, rows), jnp.bfloat16),
            pltpu.SemaphoreType.DMA((len(sources),)),
        ],
        compiler_params=pltpu.CompilerParams(vmem_limit_bytes=48 * MIB),
        cost_estimate=pl.CostEstimate(
            flops=2 * rows * depth * width,
            bytes_accessed=2 * (rows * depth + depth * width + rows * width),
            transcendentals=0,
        ),
        name="project_back",
    )(block_owner, mixed, *sources)


def gather_rows(own):
    half = own.shape[0] // 2
    across = flip(own, 8)
    below, above = z_shift(own, 1), z_shift(own, -1)
    far_a, far_b = z_shift(above[:half], -1), z_shift(below[half:], 1)
    across_below, across_above = z_shift(across, 1), z_shift(across, -1)
    across_far_a, across_far_b = flip(far_a, 8), flip(far_b, 8)
    held = [
        (own, (0, 0), 0),
        (across, (1, 0), 0),
        (below, (0, 3), 0),
        (above, (0, 1), 0),
        (far_a, (0, 2), 0),
        (far_b, (0, 2), 4),
        (across_below, (1, 3), 0),
        (across_above, (1, 1), 0),
        (across_far_a, (1, 2), 0),
        (across_far_b, (1, 2), 4),
    ]
    sources = [value for value, _, _ in held] + [flip(value, 1) for value, _, _ in held]
    spots = [(*at, core, t0) for core in (0, 1) for _, at, t0 in held]
    return sources, tuple(spots)


def rotary(values, position):
    half = HD // 2
    freq = 1000000.0 ** (-jnp.arange(half, dtype=jnp.float32) * 2.0 / HD)
    angle = position.astype(jnp.float32)[..., None, None] * freq
    cosine = jnp.cos(angle)
    sine = jnp.sin(angle)
    first = values[..., :half]
    second = values[..., half:]
    return jnp.concatenate(
        [first * cosine - second * sine, second * cosine + first * sine], axis=-1
    )


def attention(proj, cache, lengths, groups):
    rows = lengths.shape[0]
    heads = HQ // groups
    kv_heads = HK // groups
    query_cols = heads * HD
    kv_cols = kv_heads * HD
    proj = proj.reshape(2, rows, -1)
    position = lengths[None, :] + jnp.arange(2, dtype=jnp.int32)[:, None]
    query = rotary(proj[..., :query_cols].reshape(2, rows, heads, HD), position).astype(
        jnp.bfloat16
    )
    new_keys = rotary(
        proj[..., query_cols : query_cols + kv_cols].reshape(2, rows, kv_heads, HD), position
    ).astype(jnp.bfloat16)
    new_vals = proj[..., query_cols + kv_cols :].reshape(2, rows, kv_heads, HD).astype(jnp.bfloat16)
    query = query.reshape(2, rows, kv_heads, HQ // HK, HD)
    keys = cache[0].reshape(rows, -1, kv_heads, HD)
    vals = cache[1].reshape(rows, -1, kv_heads, HD)
    factor = 1.0 / math.sqrt(HD)
    old = jnp.einsum("srgjd,rpgd->srgjp", query, keys, preferred_element_type=jnp.float32) * factor
    fresh = (
        jnp.einsum("srgjd,trgd->srgjt", query, new_keys, preferred_element_type=jnp.float32)
        * factor
    )
    live = jnp.arange(keys.shape[1])[None, :] < lengths[:, None]
    old = jnp.where(live[None, :, None, None, :], old, -jnp.inf)
    seen = jnp.arange(2)[None, :] <= jnp.arange(2)[:, None]
    fresh = jnp.where(seen[:, None, None, None, :], fresh, -jnp.inf)
    top = jnp.maximum(jnp.max(old, -1), jnp.max(fresh, -1))[..., None]
    old_w = jnp.exp(old - top)
    fresh_w = jnp.exp(fresh - top)
    total = jnp.sum(old_w, -1, keepdims=True) + jnp.sum(fresh_w, -1, keepdims=True)
    old_p = (old_w / total).astype(jnp.bfloat16)
    fresh_p = (fresh_w / total).astype(jnp.bfloat16)
    mixed = jnp.einsum("srgjp,rpgd->srgjd", old_p, vals, preferred_element_type=jnp.float32)
    mixed = mixed + jnp.einsum(
        "srgjt,trgd->srgjd", fresh_p, new_vals, preferred_element_type=jnp.float32
    )
    return mixed.astype(jnp.bfloat16).reshape(2 * rows, query_cols)


def body(hidden, qkv_rows, o_rows, block_owner, cache, lengths):
    groups = lax.axis_size("tp")
    steps, rows, width = hidden.shape
    owned = qkv_rows.shape[0]
    query_cols = HQ * HD
    kv_cols = HK * HD
    qkv_copy = by_group(qkv_rows.astype(jnp.bfloat16), (query_cols, kv_cols, kv_cols), groups)
    out_copy = o_rows.astype(jnp.bfloat16).reshape(owned, groups, query_cols // groups)

    parts = shuffle(hidden.reshape(steps * rows, width), block_owner)
    qkv_copy, out_copy, *parts = lax.optimization_barrier((qkv_copy, out_copy, *parts))
    parts = [parts[0]] + [z_shift(parts[k], k) for k in range(1, NZ)]

    w = flatten(lax.all_to_all(qkv_copy, "tp", split_axis=1, concat_axis=0, tiled=True))
    w, out_copy, *parts = lax.optimization_barrier((w, out_copy, *parts))
    w_y = flip(w, 8)
    w_c = flip(w, 1)
    w_yc = flip(w_y, 1)
    got_o = flatten(lax.all_to_all(out_copy, "tp", split_axis=1, concat_axis=0, tiled=True))
    sums = partials(parts, (w, w_y, w_c, w_yc))
    sources, spots = gather_rows(got_o)

    proj = sums[0]
    for k in range(1, NZ):
        proj = proj + z_shift(sums[k], -k).astype(jnp.float32)
    mixed = attention(proj, cache, lengths, groups)
    terms = project_back(mixed, sources, spots, block_owner, groups)
    terms = lax.all_to_all(terms, "tp", split_axis=0, concat_axis=0, tiled=True)
    summed = jnp.sum(terms.astype(jnp.float32), axis=0).astype(jnp.bfloat16)
    return summed.reshape(steps, rows, width // groups)


def solution(mesh):
    in_specs = (
        P(None, "fsdp", None),
        P(("fsdp", "tp"), None),
        P(("fsdp", "tp"), None),
        P(),
        P(None, "fsdp", None, "tp"),
        P("fsdp"),
    )
    out_specs = P(None, "fsdp", "tp")
    return jax.shard_map(body, mesh=mesh, in_specs=in_specs, out_specs=out_specs, check_vma=False)
```

```python
import functools
import math

import jax
import jax.numpy as jnp
from jax import lax
from jax.experimental import pallas as pl
from jax.experimental.pallas import tpu as pltpu
from jax.sharding import PartitionSpec as P

HQ = 64
HK = 8
HD = 128
NZ = 4
GROUP = 8
AHEAD = 4
MIB = 1024 * 1024


def z_shift(value, k):
    pairs = [(f, (f // 8) * 8 + ((f // 2 + k) % NZ) * 2 + f % 2) for f in range(16)]
    return lax.ppermute(value, "fsdp", pairs)


def flip(value, bit):
    return lax.ppermute(value, "fsdp", [(f, f ^ bit) for f in range(16)])


def by_group(array, sections, groups):
    pieces = []
    begin = 0
    for width in sections:
        pieces.append(
            array[:, begin : begin + width].reshape(array.shape[0], groups, width // groups)
        )
        begin = begin + width
    return jnp.concatenate(pieces, axis=2)


def flatten(received):
    return received.reshape(received.shape[0], received.shape[2])


def shuffle_kernel(owner_ref, hidden_ref, *out_refs):
    f = lax.axis_index("fsdp")
    y_lo, z, core = f // 8, lax.rem(f // 2, 4), lax.rem(f, 2)
    rows = hidden_ref.shape[0]
    low = lax.broadcasted_iota(jnp.int32, (rows, 128), 1) < 64

    for k, out_ref in enumerate(out_refs):
        zz = lax.rem(z + k, 4)

        def step(n, carry, zz=zz, out_ref=out_ref):
            q, p = n // 4, lax.rem(n, 4)
            yy = lax.rem(y_lo + lax.rem(q, 2), 2)
            cc = lax.rem(core + q // 2, 2)
            i = yy * 64 + zz * 16 + cc * 8 + 2 * p
            s0, s1 = owner_ref[0, i], owner_ref[0, i + 1]
            a = hidden_ref[:, pl.ds(pl.multiple_of((s0 // 2) * 128, 128), 128)].astype(jnp.float32)
            b = hidden_ref[:, pl.ds(pl.multiple_of((s1 // 2) * 128, 128), 128)].astype(jnp.float32)
            a = pltpu.roll(a, 64 * lax.rem(s0, 2), 1)
            b = pltpu.roll(b, 64 * (1 - lax.rem(s1, 2)), 1)
            out_ref[:, pl.ds(pl.multiple_of(n * 128, 128), 128)] = jnp.where(low, a, b).astype(
                jnp.bfloat16
            )
            return carry

        lax.fori_loop(0, 16, step, 0, unroll=4)


def shuffle(hidden, block_owner):
    rows, width = hidden.shape
    part = jax.ShapeDtypeStruct((rows, width // NZ), jnp.bfloat16)
    return pl.pallas_call(
        shuffle_kernel,
        out_shape=[part] * NZ,
        in_specs=[
            pl.BlockSpec(memory_space=pltpu.SMEM),
            pl.BlockSpec(memory_space=pltpu.VMEM),
        ],
        out_specs=[pl.BlockSpec(memory_space=pltpu.VMEM)] * NZ,
        compiler_params=pltpu.CompilerParams(vmem_limit_bytes=48 * MIB),
        cost_estimate=pl.CostEstimate(
            flops=rows * width * 8, bytes_accessed=4 * rows * width, transcendentals=0
        ),
        name="shuffle",
    )(block_owner, hidden)


def partial_kernel(h0, h1, h2, h3, w0, w1, w2, w3, p0, p1, p2, p3, stacked):
    rows = h0.shape[0]

    @pl.when(pl.program_id(0) == 0)
    def _():
        for k, h in enumerate((h0, h1, h2, h3)):
            stacked[pl.ds(k * rows, rows), :] = h[...]

    depth = w0.shape[0]
    total = jnp.zeros((NZ * rows, w0.shape[1]), jnp.float32)
    for q, w in enumerate((w0, w1, w2, w3)):
        total = total + jnp.dot(
            stacked[:, q * depth : (q + 1) * depth], w[...], preferred_element_type=jnp.float32
        )
    for k, out in enumerate((p0, p1, p2, p3)):
        out[...] = total[k * rows : (k + 1) * rows].astype(out.dtype)


def partials(parts, weights):
    rows, width = parts[0].shape
    depth, cols = weights[0].shape
    tile = 256
    return pl.pallas_call(
        partial_kernel,
        grid=(cols // tile,),
        out_shape=[jax.ShapeDtypeStruct((rows, cols), jnp.float32)]
        + [jax.ShapeDtypeStruct((rows, cols), jnp.bfloat16)] * 3,
        in_specs=[pl.BlockSpec((rows, width), lambda j: (0, 0))] * NZ
        + [pl.BlockSpec((depth, tile), lambda j: (0, j))] * NZ,
        out_specs=[pl.BlockSpec((rows, tile), lambda j: (0, j))] * NZ,
        scratch_shapes=[pltpu.VMEM((NZ * rows, width), jnp.bfloat16)],
        compiler_params=pltpu.CompilerParams(vmem_limit_bytes=48 * MIB),
        cost_estimate=pl.CostEstimate(
            flops=2 * NZ * rows * width * cols,
            bytes_accessed=2 * (NZ * rows * width + width * cols + NZ * rows * cols),
            transcendentals=0,
        ),
        name="partials",
    )(*parts, *weights)


def back_kernel(spots, groups, owner_ref, mixed_ref, *refs):
    count = len(spots)
    sources, out_ref, held, placed, sems = refs[:count], *refs[count:]
    f = lax.axis_index("fsdp")
    y_lo, z, core = f // 8, lax.rem(f // 2, NZ), lax.rem(f, 2)
    rows, depth = mixed_ref.shape
    width = held.shape[0]
    owned = width // owner_ref.shape[1]

    copies = []
    begin = 0
    for n, source in enumerate(sources):
        size = source.shape[0]
        copies.append(
            pltpu.make_async_copy(source, held.at[pl.ds(begin, size)], sems.at[n])
        )
        begin += size
    for copy in copies[:AHEAD]:
        copy.start()
    turned = mixed_ref[...].astype(jnp.float32).T.astype(jnp.bfloat16)

    begin = 0
    for n, (dy, dz, dc, t0) in enumerate(spots):
        size = sources[n].shape[0]
        first = (
            lax.rem(y_lo + dy, 2) * 64 + lax.rem(z + dz, NZ) * 16 + lax.rem(core + dc, 2) * 8 + t0
        )
        copies[n].wait()
        if n + AHEAD < count:
            copies[n + AHEAD].start()
        terms = jnp.dot(held[begin : begin + size], turned, preferred_element_type=jnp.float32)
        terms = terms.astype(jnp.bfloat16)
        for b in range(size // owned):
            spot = pl.multiple_of(owner_ref[1, first + b] * owned, owned)
            placed[pl.ds(spot, owned), :] = terms[b * owned : (b + 1) * owned]
        begin += size

    slab = width // groups
    for t in range(groups):
        out_ref[t] = placed[t * slab : (t + 1) * slab].T


def project_back(mixed, sources, spots, block_owner, groups):
    rows, depth = mixed.shape
    width = sum(source.shape[0] for source in sources)
    return pl.pallas_call(
        functools.partial(back_kernel, spots, groups),
        out_shape=jax.ShapeDtypeStruct((groups, rows, width // groups), jnp.bfloat16),
        in_specs=[
            pl.BlockSpec(memory_space=pltpu.SMEM),
            pl.BlockSpec(memory_space=pltpu.VMEM),
        ]
        + [pl.BlockSpec(memory_space=pl.ANY)] * len(sources),
        out_specs=pl.BlockSpec(memory_space=pltpu.VMEM),
        scratch_shapes=[
            pltpu.VMEM((width, depth), jnp.bfloat16),
            pltpu.VMEM((width, rows), jnp.bfloat16),
            pltpu.SemaphoreType.DMA((len(sources),)),
        ],
        compiler_params=pltpu.CompilerParams(vmem_limit_bytes=48 * MIB),
        cost_estimate=pl.CostEstimate(
            flops=2 * rows * depth * width,
            bytes_accessed=2 * (rows * depth + depth * width + rows * width),
            transcendentals=0,
        ),
        name="project_back",
    )(block_owner, mixed, *sources)


def turns(lengths):
    half = HD // 2
    position = (lengths[None, :] + jnp.arange(2, dtype=jnp.int32)[:, None]).reshape(-1)
    freq = 1000000.0 ** (-jnp.arange(half, dtype=jnp.float32) * 2.0 / HD)
    angle = position.astype(jnp.float32)[:, None] * freq
    cosine, sine = jnp.cos(angle), jnp.sin(angle)
    return jnp.concatenate([cosine, cosine], axis=1), jnp.concatenate([-sine, sine], axis=1)


def attention_kernel(
    lengths_ref, p0, p1, p2, p3, cos_ref, sin_ref, cache_ref, out_ref, query, keys, values, result
):
    step = pl.program_id(0)
    both = p0.shape[0]
    rows = both // 2
    heads = out_ref.shape[1] // HD
    lanes = 2 * heads
    span = GROUP * lanes

    @pl.when(step == 0)
    def _():
        cosine, sine = cos_ref[...], sin_ref[...]

        def part(begin):
            cut = slice(begin * HD, (begin + 1) * HD)
            total = p0[:, cut] + p1[:, cut].astype(jnp.float32)
            return total + p2[:, cut].astype(jnp.float32) + p3[:, cut].astype(jnp.float32)

        def turn(x):
            return x * cosine + pltpu.roll(x, HD // 2, 1) * sine

        for h in range(heads):
            turned = turn(part(h))
            for s in range(2):
                query[pl.ds(s * heads + h, rows, stride=lanes), :] = turned[
                    s * rows : (s + 1) * rows
                ]
        new_keys, new_values = turn(part(heads)), part(heads + 1)
        for g in range(rows // GROUP):
            for t in range(2):
                to = slice((2 * g + t) * GROUP, (2 * g + t + 1) * GROUP)
                begin = t * rows + g * GROUP
                keys[to] = new_keys[begin : begin + GROUP]
                values[to] = new_values[begin : begin + GROUP]

    factor = 1.0 / math.sqrt(HD)
    nt = (((1,), (1,)), ((), ()))
    at = pl.ds(pl.multiple_of(step * span, span), span)
    fresh_at = pl.ds(pl.multiple_of(step * 2 * GROUP, 2 * GROUP), 2 * GROUP)
    q = query[at, :].astype(jnp.bfloat16)
    fresh = (
        lax.dot_general(
            q, keys[fresh_at, :].astype(jnp.bfloat16), nt, preferred_element_type=jnp.float32
        )
        * factor
    )
    of = lax.broadcasted_iota(jnp.int32, fresh.shape, 0)
    new = lax.broadcasted_iota(jnp.int32, fresh.shape, 1)
    seen = (of // lanes == new % GROUP) & (new // GROUP <= (of // heads) % 2)
    fresh = jnp.where(seen, fresh, -jnp.inf)

    held = cache_ref.shape[2]
    place = lax.broadcasted_iota(jnp.int32, (lanes, held), 1)
    pieces = []
    for r in range(GROUP):
        score = lax.dot_general(
            q[r * lanes : (r + 1) * lanes], cache_ref[0, r], nt, preferred_element_type=jnp.float32
        )
        pieces.append(jnp.where(place < lengths_ref[step * GROUP + r], score * factor, -jnp.inf))
    old = jnp.concatenate(pieces, axis=0)
    top = jnp.maximum(
        jnp.max(old, axis=1, keepdims=True), jnp.max(fresh, axis=1, keepdims=True)
    )
    old_w = jnp.exp(old - top)
    fresh_w = jnp.exp(fresh - top)
    total = jnp.sum(old_w, axis=1, keepdims=True) + jnp.sum(fresh_w, axis=1, keepdims=True)
    scale = 1.0 / total
    old_p = (old_w * scale).astype(jnp.bfloat16)
    fresh_p = (fresh_w * scale).astype(jnp.bfloat16)
    mixed = jnp.concatenate(
        [
            jnp.dot(
                old_p[r * lanes : (r + 1) * lanes],
                cache_ref[1, r],
                preferred_element_type=jnp.float32,
            )
            for r in range(GROUP)
        ],
        axis=0,
    )
    mixed = mixed + jnp.dot(
        fresh_p, values[fresh_at, :].astype(jnp.bfloat16), preferred_element_type=jnp.float32
    )
    result[at, :] = mixed

    @pl.when(step == pl.num_programs(0) - 1)
    def _():
        for h in range(heads):
            for s in range(2):
                out_ref[s * rows : (s + 1) * rows, h * HD : (h + 1) * HD] = result[
                    pl.ds(s * heads + h, rows, stride=lanes), :
                ].astype(out_ref.dtype)


def attention(sums, cos, sin, cache, lengths):
    both, cols = sums[0].shape
    rows = both // 2
    width = cols - 2 * HD
    held = cache.shape[2]
    lanes = 2 * width // HD

    def whole(*shape):
        return pl.BlockSpec(shape, lambda g: (0,) * len(shape))

    return pl.pallas_call(
        attention_kernel,
        grid=(rows // GROUP,),
        out_shape=jax.ShapeDtypeStruct((both, width), jnp.bfloat16),
        in_specs=[pl.BlockSpec(memory_space=pltpu.SMEM)]
        + [whole(both, cols)] * NZ
        + [whole(both, HD)] * 2
        + [pl.BlockSpec((2, GROUP, held, HD), lambda g: (0, g, 0, 0))],
        out_specs=whole(both, width),
        scratch_shapes=[
            pltpu.VMEM((rows * lanes, HD), jnp.float32),
            pltpu.VMEM((both, HD), jnp.float32),
            pltpu.VMEM((both, HD), jnp.float32),
            pltpu.VMEM((rows * lanes, HD), jnp.float32),
        ],
        compiler_params=pltpu.CompilerParams(vmem_limit_bytes=48 * MIB),
        cost_estimate=pl.CostEstimate(
            flops=4 * rows * lanes * held * HD,
            bytes_accessed=4 * rows * held * HD,
            transcendentals=rows * lanes * held,
        ),
        name="attention",
    )(lengths, *sums, cos, sin, cache)


def after(values, *first):
    return lax.optimization_barrier((*values, *first))[: len(values)]


def body(hidden, qkv_rows, o_rows, block_owner, cache, lengths):
    groups = lax.axis_size("tp")
    steps, rows, width = hidden.shape
    owned = qkv_rows.shape[0]
    query_cols = HQ * HD
    kv_cols = HK * HD
    cols = (query_cols + 2 * kv_cols) // groups
    copy = jnp.concatenate([qkv_rows.astype(jnp.bfloat16), o_rows.astype(jnp.bfloat16)], axis=1)
    copy = by_group(copy, (query_cols, kv_cols, kv_cols, query_cols), groups)

    cos, sin = turns(lengths)
    parts = shuffle(hidden.reshape(steps * rows, width), block_owner)
    parts = [parts[0]] + [z_shift(parts[k], k) for k in range(1, NZ)]

    both = flatten(lax.all_to_all(copy, "tp", split_axis=1, concat_axis=0, tiled=True))
    both, parts[0], parts[1], parts[3], cos, sin = lax.optimization_barrier(
        (both, parts[0], parts[1], parts[3], cos, sin)
    )
    w, own = both[:, :cols], both[:, cols:]
    half = own.shape[0] // 2

    w_y, w_c = flip(w, 8), flip(w, 1)
    below, above = z_shift(own, 1), z_shift(own, -1)
    own_c = flip(own, 1)
    w_y, below, above, own, parts[2] = lax.optimization_barrier((w_y, below, above, own, parts[2]))
    w_yc = flip(w_y, 1)
    far_a, far_b = z_shift(above[:half], -1), z_shift(below[half:], 1)
    across = flip(own, 8)

    sums = partials(parts, (w, w_y, w_c, w_yc))
    sums = [sums[0]] + [z_shift(sums[k], -k) for k in range(1, NZ)]
    below_c, above_c = after((below, above), sums[0])
    below_c, above_c = flip(below_c, 1), flip(above_c, 1)
    across_n, far_an, far_bn = after((across, far_a, far_b), *sums)
    across_below, across_above = z_shift(across_n, 1), z_shift(across_n, -1)
    across_far_a, across_far_b = flip(far_an, 8), flip(far_bn, 8)
    across_c, far_ac, far_bc = flip(across_n, 1), flip(far_an, 1), flip(far_bn, 1)
    mixed = attention(sums, cos, sin, cache, lengths)

    last = after((across_below, across_above, across_far_a, across_far_b), mixed)
    last_c = [flip(value, 1) for value in last]
    near = ((0, 0), (0, 3), (0, 1), (1, 0), (0, 2), (0, 2), (1, 3), (1, 1), (1, 2), (1, 2))
    begins = (0, 0, 0, 0, 0, 4, 0, 0, 0, 4)
    sources = [own, below, above, across, far_a, far_b, *last]
    sources += [own_c, below_c, above_c, across_c, far_ac, far_bc, *last_c]
    spots = tuple((*at, core, t0) for core in (0, 1) for at, t0 in zip(near, begins))
    order = (0, 10, 1, 2, 11, 12, 3, 13, 4, 5, 14, 15, 6, 7, 8, 9, 16, 17, 18, 19)
    sources, spots = [sources[n] for n in order], tuple(spots[n] for n in order)
    terms = project_back(mixed, sources, spots, block_owner, groups)
    terms = lax.all_to_all(terms, "tp", split_axis=0, concat_axis=0, tiled=True)
    summed = jnp.sum(terms.astype(jnp.float32), axis=0).astype(jnp.bfloat16)
    return summed.reshape(steps, rows, width // groups)


def solution(mesh):
    in_specs = (
        P(None, "fsdp", None),
        P(("fsdp", "tp"), None),
        P(("fsdp", "tp"), None),
        P(),
        P(None, "fsdp", None, "tp"),
        P("fsdp"),
    )
    out_specs = P(None, "fsdp", "tp")
    return jax.shard_map(body, mesh=mesh, in_specs=in_specs, out_specs=out_specs, check_vma=False)
```

```python
import functools
import math

import jax
import jax.numpy as jnp
from jax import lax
from jax.experimental import pallas as pl
from jax.experimental.pallas import tpu as pltpu
from jax.sharding import PartitionSpec as P

HQ = 64
HK = 8
HD = 128
NZ = 4
GROUP = 8
CHUNK = 4
MIB = 1024 * 1024


def z_shift(value, k):
    pairs = [(f, (f // 8) * 8 + ((f // 2 + k) % NZ) * 2 + f % 2) for f in range(16)]
    return lax.ppermute(value, "fsdp", pairs)


def flip(value, bit):
    return lax.ppermute(value, "fsdp", [(f, f ^ bit) for f in range(16)])


def by_group(array, sections, groups):
    pieces = []
    begin = 0
    for width in sections:
        pieces.append(
            array[:, begin : begin + width].reshape(array.shape[0], groups, width // groups)
        )
        begin = begin + width
    return jnp.concatenate(pieces, axis=2)


def flatten(received):
    return received.reshape(received.shape[0], received.shape[2])


def shuffle_kernel(owner_ref, hidden_ref, *out_refs):
    f = lax.axis_index("fsdp")
    y_lo, z, core = f // 8, lax.rem(f // 2, 4), lax.rem(f, 2)
    rows = hidden_ref.shape[0]
    low = lax.broadcasted_iota(jnp.int32, (rows, 128), 1) < 64

    for k, out_ref in enumerate(out_refs):
        zz = lax.rem(z + k, 4)

        def step(n, carry, zz=zz, out_ref=out_ref):
            q, p = n // 4, lax.rem(n, 4)
            yy = lax.rem(y_lo + lax.rem(q, 2), 2)
            cc = lax.rem(core + q // 2, 2)
            i = yy * 64 + zz * 16 + cc * 8 + 2 * p
            s0, s1 = owner_ref[0, i], owner_ref[0, i + 1]
            a = hidden_ref[:, pl.ds(pl.multiple_of((s0 // 2) * 128, 128), 128)].astype(jnp.float32)
            b = hidden_ref[:, pl.ds(pl.multiple_of((s1 // 2) * 128, 128), 128)].astype(jnp.float32)
            a = pltpu.roll(a, 64 * lax.rem(s0, 2), 1)
            b = pltpu.roll(b, 64 * (1 - lax.rem(s1, 2)), 1)
            out_ref[:, pl.ds(pl.multiple_of(n * 128, 128), 128)] = jnp.where(low, a, b).astype(
                jnp.bfloat16
            )
            return carry

        lax.fori_loop(0, 16, step, 0, unroll=4)


def shuffle(hidden, block_owner):
    rows, width = hidden.shape
    part = jax.ShapeDtypeStruct((rows, width // NZ), jnp.bfloat16)
    return pl.pallas_call(
        shuffle_kernel,
        out_shape=[part] * NZ,
        in_specs=[
            pl.BlockSpec(memory_space=pltpu.SMEM),
            pl.BlockSpec(memory_space=pltpu.VMEM),
        ],
        out_specs=[pl.BlockSpec(memory_space=pltpu.VMEM)] * NZ,
        compiler_params=pltpu.CompilerParams(vmem_limit_bytes=48 * MIB),
        cost_estimate=pl.CostEstimate(
            flops=rows * width * 8, bytes_accessed=4 * rows * width, transcendentals=0
        ),
        name="shuffle",
    )(block_owner, hidden)


def partial_kernel(h0, h1, h2, h3, w0, w1, w2, w3, p0, p1, p2, p3, stacked):
    rows = h0.shape[0]

    @pl.when(pl.program_id(0) == 0)
    def _():
        for k, h in enumerate((h0, h1, h2, h3)):
            stacked[pl.ds(k * rows, rows), :] = h[...]

    depth = w0.shape[0]
    total = jnp.zeros((NZ * rows, w0.shape[1]), jnp.float32)
    for q, w in enumerate((w0, w1, w2, w3)):
        total = total + jnp.dot(
            stacked[:, q * depth : (q + 1) * depth], w[...], preferred_element_type=jnp.float32
        )
    for k, out in enumerate((p0, p1, p2, p3)):
        out[...] = total[k * rows : (k + 1) * rows].astype(out.dtype)


def partials(parts, weights):
    rows, width = parts[0].shape
    depth, cols = weights[0].shape
    tile = 256
    return pl.pallas_call(
        partial_kernel,
        grid=(cols // tile,),
        out_shape=[jax.ShapeDtypeStruct((rows, cols), jnp.float32)]
        + [jax.ShapeDtypeStruct((rows, cols), jnp.bfloat16)] * 3,
        in_specs=[pl.BlockSpec((rows, width), lambda j: (0, 0))] * NZ
        + [pl.BlockSpec((depth, tile), lambda j: (0, j))] * NZ,
        out_specs=[pl.BlockSpec((rows, tile), lambda j: (0, j))] * NZ,
        scratch_shapes=[pltpu.VMEM((NZ * rows, width), jnp.bfloat16)],
        compiler_params=pltpu.CompilerParams(vmem_limit_bytes=48 * MIB),
        cost_estimate=pl.CostEstimate(
            flops=2 * NZ * rows * width * cols,
            bytes_accessed=2 * (NZ * rows * width + width * cols + NZ * rows * cols),
            transcendentals=0,
        ),
        name="partials",
    )(*parts, *weights)


def back_kernel(spots, groups, owner_ref, mixed_ref, *refs):
    count = len(spots)
    sources, out_ref, held, placed, goals, sems = refs[:count], *refs[count:]
    f = lax.axis_index("fsdp")
    y_lo, z, core = f // 8, lax.rem(f // 2, NZ), lax.rem(f, 2)
    width = held.shape[0]
    owned = width // owner_ref.shape[1]
    chunk = CHUNK * owned

    n = 0
    for (dy, dz, dc, t0), source in zip(spots, sources):
        first = (
            lax.rem(y_lo + dy, 2) * 64 + lax.rem(z + dz, NZ) * 16 + lax.rem(core + dc, 2) * 8 + t0
        )
        for part in range(source.shape[0] // chunk):
            pltpu.make_async_copy(
                source.at[pl.ds(part * chunk, chunk)], held.at[pl.ds(n * chunk, chunk)], sems.at[n]
            ).start()
            for b in range(CHUNK):
                goals[n * CHUNK + b] = owner_ref[1, first + part * CHUNK + b] * owned
            n += 1
    turned = mixed_ref[...].astype(jnp.float32).T.astype(jnp.bfloat16)

    def multiply(n, carry):
        at = pl.ds(pl.multiple_of(n * chunk, chunk), chunk)
        pltpu.make_async_copy(held.at[at], held.at[at], sems.at[n]).wait()
        terms = jnp.dot(held[at, :], turned, preferred_element_type=jnp.float32)
        terms = terms.astype(jnp.bfloat16)
        for b in range(CHUNK):
            spot = pl.multiple_of(goals[n * CHUNK + b], owned)
            placed[pl.ds(spot, owned), :] = terms[b * owned : (b + 1) * owned]
        return carry

    lax.fori_loop(0, width // chunk, multiply, 0)
    slab = width // groups

    def turn_back(t, carry):
        out_ref[t] = placed[pl.ds(pl.multiple_of(t * slab, slab), slab), :].T
        return carry

    lax.fori_loop(0, groups, turn_back, 0)


def project_back(mixed, sources, spots, block_owner, groups):
    rows, depth = mixed.shape
    width = sum(source.shape[0] for source in sources)
    return pl.pallas_call(
        functools.partial(back_kernel, spots, groups),
        out_shape=jax.ShapeDtypeStruct((groups, rows, width // groups), jnp.bfloat16),
        in_specs=[
            pl.BlockSpec(memory_space=pltpu.SMEM),
            pl.BlockSpec(memory_space=pltpu.VMEM),
        ]
        + [pl.BlockSpec(memory_space=pl.ANY)] * len(sources),
        out_specs=pl.BlockSpec(memory_space=pltpu.VMEM),
        scratch_shapes=[
            pltpu.VMEM((width, depth), jnp.bfloat16),
            pltpu.VMEM((width, rows), jnp.bfloat16),
            pltpu.SMEM((block_owner.shape[1],), jnp.int32),
            pltpu.SemaphoreType.DMA((block_owner.shape[1] // CHUNK,)),
        ],
        compiler_params=pltpu.CompilerParams(vmem_limit_bytes=48 * MIB),
        cost_estimate=pl.CostEstimate(
            flops=2 * rows * depth * width,
            bytes_accessed=2 * (rows * depth + depth * width + rows * width),
            transcendentals=0,
        ),
        name="project_back",
    )(block_owner, mixed, *sources)


def turns(lengths):
    half = HD // 2
    position = (lengths[None, :] + jnp.arange(2, dtype=jnp.int32)[:, None]).reshape(-1)
    freq = 1000000.0 ** (-jnp.arange(half, dtype=jnp.float32) * 2.0 / HD)
    angle = position.astype(jnp.float32)[:, None] * freq
    cosine, sine = jnp.cos(angle), jnp.sin(angle)
    return jnp.concatenate([cosine, cosine], axis=1), jnp.concatenate([-sine, sine], axis=1)


def attention_kernel(
    lengths_ref, p0, p1, p2, p3, cos_ref, sin_ref, cache_ref, out_ref, query, keys, values, result
):
    step = pl.program_id(0)
    both = p0.shape[0]
    rows = both // 2
    heads = out_ref.shape[1] // HD
    lanes = 2 * heads
    span = GROUP * lanes

    @pl.when(step == 0)
    def _():
        cosine, sine = cos_ref[...], sin_ref[...]

        def part(begin):
            cut = slice(begin * HD, (begin + 1) * HD)
            total = p0[:, cut] + p1[:, cut].astype(jnp.float32)
            return total + p2[:, cut].astype(jnp.float32) + p3[:, cut].astype(jnp.float32)

        def turn(x):
            return x * cosine + pltpu.roll(x, HD // 2, 1) * sine

        for h in range(heads):
            turned = turn(part(h))
            for s in range(2):
                query[pl.ds(s * heads + h, rows, stride=lanes), :] = turned[
                    s * rows : (s + 1) * rows
                ]
        new_keys, new_values = turn(part(heads)), part(heads + 1)
        for g in range(rows // GROUP):
            for t in range(2):
                to = slice((2 * g + t) * GROUP, (2 * g + t + 1) * GROUP)
                begin = t * rows + g * GROUP
                keys[to] = new_keys[begin : begin + GROUP]
                values[to] = new_values[begin : begin + GROUP]

    factor = 1.0 / math.sqrt(HD)
    nt = (((1,), (1,)), ((), ()))
    at = pl.ds(pl.multiple_of(step * span, span), span)
    fresh_at = pl.ds(pl.multiple_of(step * 2 * GROUP, 2 * GROUP), 2 * GROUP)
    q = query[at, :].astype(jnp.bfloat16)
    fresh = (
        lax.dot_general(
            q, keys[fresh_at, :].astype(jnp.bfloat16), nt, preferred_element_type=jnp.float32
        )
        * factor
    )
    of = lax.broadcasted_iota(jnp.int32, fresh.shape, 0)
    new = lax.broadcasted_iota(jnp.int32, fresh.shape, 1)
    seen = (of // lanes == new % GROUP) & (new // GROUP <= (of // heads) % 2)
    fresh = jnp.where(seen, fresh, -jnp.inf)

    held = cache_ref.shape[2]
    place = lax.broadcasted_iota(jnp.int32, (lanes, held), 1)
    pieces = []
    for r in range(GROUP):
        score = lax.dot_general(
            q[r * lanes : (r + 1) * lanes], cache_ref[0, r], nt, preferred_element_type=jnp.float32
        )
        pieces.append(jnp.where(place < lengths_ref[step * GROUP + r], score * factor, -jnp.inf))
    old = jnp.concatenate(pieces, axis=0)
    top = jnp.maximum(
        jnp.max(old, axis=1, keepdims=True), jnp.max(fresh, axis=1, keepdims=True)
    )
    old_w = jnp.exp(old - top)
    fresh_w = jnp.exp(fresh - top)
    total = jnp.sum(old_w, axis=1, keepdims=True) + jnp.sum(fresh_w, axis=1, keepdims=True)
    scale = 1.0 / total
    old_p = (old_w * scale).astype(jnp.bfloat16)
    fresh_p = (fresh_w * scale).astype(jnp.bfloat16)
    mixed = jnp.concatenate(
        [
            jnp.dot(
                old_p[r * lanes : (r + 1) * lanes],
                cache_ref[1, r],
                preferred_element_type=jnp.float32,
            )
            for r in range(GROUP)
        ],
        axis=0,
    )
    mixed = mixed + jnp.dot(
        fresh_p, values[fresh_at, :].astype(jnp.bfloat16), preferred_element_type=jnp.float32
    )
    result[at, :] = mixed

    @pl.when(step == pl.num_programs(0) - 1)
    def _():
        for h in range(heads):
            for s in range(2):
                out_ref[s * rows : (s + 1) * rows, h * HD : (h + 1) * HD] = result[
                    pl.ds(s * heads + h, rows, stride=lanes), :
                ].astype(out_ref.dtype)


def attention(sums, cos, sin, cache, lengths):
    both, cols = sums[0].shape
    rows = both // 2
    width = cols - 2 * HD
    held = cache.shape[2]
    lanes = 2 * width // HD

    def whole(*shape):
        return pl.BlockSpec(shape, lambda g: (0,) * len(shape))

    return pl.pallas_call(
        attention_kernel,
        grid=(rows // GROUP,),
        out_shape=jax.ShapeDtypeStruct((both, width), jnp.bfloat16),
        in_specs=[pl.BlockSpec(memory_space=pltpu.SMEM)]
        + [whole(both, cols)] * NZ
        + [whole(both, HD)] * 2
        + [pl.BlockSpec((2, GROUP, held, HD), lambda g: (0, g, 0, 0))],
        out_specs=whole(both, width),
        scratch_shapes=[
            pltpu.VMEM((rows * lanes, HD), jnp.float32),
            pltpu.VMEM((both, HD), jnp.float32),
            pltpu.VMEM((both, HD), jnp.float32),
            pltpu.VMEM((rows * lanes, HD), jnp.float32),
        ],
        compiler_params=pltpu.CompilerParams(vmem_limit_bytes=48 * MIB),
        cost_estimate=pl.CostEstimate(
            flops=4 * rows * lanes * held * HD,
            bytes_accessed=16 * rows * held * HD,
            transcendentals=rows * lanes * held,
        ),
        name="attention",
    )(lengths, *sums, cos, sin, cache)


def after(values, *first):
    return lax.optimization_barrier((*values, *first))[: len(values)]


def body(hidden, qkv_rows, o_rows, block_owner, cache, lengths):
    groups = lax.axis_size("tp")
    steps, rows, width = hidden.shape
    owned = qkv_rows.shape[0]
    query_cols = HQ * HD
    kv_cols = HK * HD
    cols = (query_cols + 2 * kv_cols) // groups
    copy = jnp.concatenate([qkv_rows.astype(jnp.bfloat16), o_rows.astype(jnp.bfloat16)], axis=1)
    copy = by_group(copy, (query_cols, kv_cols, kv_cols, query_cols), groups)

    cos, sin = turns(lengths)
    parts = shuffle(hidden.reshape(steps * rows, width), block_owner)
    parts = [parts[0]] + [z_shift(parts[k], k) for k in range(1, NZ)]

    both = flatten(lax.all_to_all(copy, "tp", split_axis=1, concat_axis=0, tiled=True))
    both, cos, sin, *parts = lax.optimization_barrier((both, cos, sin, *parts))
    w, own = both[:, :cols], both[:, cols:]
    half = own.shape[0] // 2

    w_y, w_c = flip(w, 8), flip(w, 1)
    below, above = z_shift(own, 1), z_shift(own, -1)
    own_c = flip(own, 1)
    w_y, below, above, own, own_c = lax.optimization_barrier((w_y, below, above, own, own_c))
    w_yc = flip(w_y, 1)
    far_a, far_b = z_shift(above[:half], -1), z_shift(below[half:], 1)
    across = flip(own, 8)
    below_c, above_c = flip(below, 1), flip(above, 1)
    w_yc, below_c, above_c = lax.optimization_barrier((w_yc, below_c, above_c))

    sums = partials(parts, (w, w_y, w_c, w_yc))
    sums = [sums[0]] + [z_shift(sums[k], -k) for k in range(1, NZ)]
    across, far_a, far_b = after((across, far_a, far_b), *sums)
    across_below, across_above = z_shift(across, 1), z_shift(across, -1)
    across_far_a, across_far_b = flip(far_a, 8), flip(far_b, 8)
    mixed = attention(sums, cos, sin, cache, lengths)

    across_c, far_ac, far_bc = (flip(v, 1) for v in after((across, far_a, far_b), mixed))
    last = after((across_below, across_above, across_far_a, across_far_b), mixed)
    last_c = [flip(value, 1) for value in last]
    near = ((0, 0), (0, 3), (0, 1), (1, 0), (0, 2), (0, 2), (1, 3), (1, 1), (1, 2), (1, 2))
    begins = (0, 0, 0, 0, 0, 4, 0, 0, 0, 4)
    sources = [own, below, above, across, far_a, far_b, *last]
    sources += [own_c, below_c, above_c, across_c, far_ac, far_bc, *last_c]
    spots = tuple((*at, core, t0) for core in (0, 1) for at, t0 in zip(near, begins))
    order = (0, 10, 1, 2, 11, 12, 3, 13, 4, 5, 14, 15, 6, 7, 8, 9, 16, 17, 18, 19)
    sources, spots = [sources[n] for n in order], tuple(spots[n] for n in order)
    terms = project_back(mixed, sources, spots, block_owner, groups)
    terms = lax.all_to_all(terms, "tp", split_axis=0, concat_axis=0, tiled=True)
    summed = jnp.sum(terms.astype(jnp.float32), axis=0).astype(jnp.bfloat16)
    return summed.reshape(steps, rows, width // groups)


def solution(mesh):
    in_specs = (
        P(None, "fsdp", None),
        P(("fsdp", "tp"), None),
        P(("fsdp", "tp"), None),
        P(),
        P(None, "fsdp", None, "tp"),
        P("fsdp"),
    )
    out_specs = P(None, "fsdp", "tp")
    return jax.shard_map(body, mesh=mesh, in_specs=in_specs, out_specs=out_specs, check_vma=False)
```

```python
import functools
import math

import jax
import jax.numpy as jnp
from jax import lax
from jax.experimental import pallas as pl
from jax.experimental.pallas import tpu as pltpu
from jax.sharding import PartitionSpec as P

HQ = 64
HK = 8
HD = 128
NZ = 4
GROUP = 8
CHUNK = 4
MIB = 1024 * 1024


def z_shift(value, k):
    pairs = [(f, (f // 8) * 8 + ((f // 2 + k) % NZ) * 2 + f % 2) for f in range(16)]
    return lax.ppermute(value, "fsdp", pairs)


def flip(value, bit):
    return lax.ppermute(value, "fsdp", [(f, f ^ bit) for f in range(16)])


def by_group(array, sections, groups):
    pieces = []
    begin = 0
    for width in sections:
        pieces.append(
            array[:, begin : begin + width].reshape(array.shape[0], groups, width // groups)
        )
        begin = begin + width
    return jnp.concatenate(pieces, axis=2)


def flatten(received):
    return received.reshape(received.shape[0], received.shape[2])


def shuffle_kernel(owner_ref, hidden_ref, *out_refs):
    f = lax.axis_index("fsdp")
    y_lo, z, core = f // 8, lax.rem(f // 2, 4), lax.rem(f, 2)
    rows = hidden_ref.shape[0]
    low = lax.broadcasted_iota(jnp.int32, (rows, 128), 1) < 64

    for k, out_ref in enumerate(out_refs):
        zz = lax.rem(z + k, 4)

        def step(n, carry, zz=zz, out_ref=out_ref):
            q, p = n // 4, lax.rem(n, 4)
            yy = lax.rem(y_lo + q // 2, 2)
            cc = lax.rem(core + lax.rem(q, 2), 2)
            i = yy * 64 + zz * 16 + cc * 8 + 2 * p
            s0, s1 = owner_ref[0, i], owner_ref[0, i + 1]
            a = hidden_ref[:, pl.ds(pl.multiple_of((s0 // 2) * 128, 128), 128)].astype(jnp.float32)
            b = hidden_ref[:, pl.ds(pl.multiple_of((s1 // 2) * 128, 128), 128)].astype(jnp.float32)
            a = pltpu.roll(a, 64 * lax.rem(s0, 2), 1)
            b = pltpu.roll(b, 64 * (1 - lax.rem(s1, 2)), 1)
            out_ref[:, pl.ds(pl.multiple_of(n * 128, 128), 128)] = jnp.where(low, a, b).astype(
                jnp.bfloat16
            )
            return carry

        lax.fori_loop(0, 16, step, 0, unroll=4)


def shuffle(hidden, block_owner):
    rows, width = hidden.shape
    part = jax.ShapeDtypeStruct((rows, width // NZ), jnp.bfloat16)
    return pl.pallas_call(
        shuffle_kernel,
        out_shape=[part] * NZ,
        in_specs=[
            pl.BlockSpec(memory_space=pltpu.SMEM),
            pl.BlockSpec(memory_space=pltpu.VMEM),
        ],
        out_specs=[pl.BlockSpec(memory_space=pltpu.VMEM)] * NZ,
        compiler_params=pltpu.CompilerParams(vmem_limit_bytes=14 * MIB),
        cost_estimate=pl.CostEstimate(
            flops=rows * width * 8, bytes_accessed=4 * rows * width, transcendentals=0
        ),
        name="shuffle",
    )(block_owner, hidden)


def partial_kernel(begun, *refs):
    held, weights = refs[:NZ], refs[NZ : NZ + 2]
    totals = refs[NZ + 2 : 2 * NZ + 2] if begun else ()
    *outs, stacked = refs[NZ + 2 + len(totals) :]
    rows = held[0].shape[0]
    depth = weights[0].shape[0]

    @pl.when(pl.program_id(0) == 0)
    def _():
        for k, h in enumerate(held):
            stacked[pl.ds(k * rows, rows), :] = h[...]

    total = jnp.dot(stacked[:, :depth], weights[0][...], preferred_element_type=jnp.float32)
    total = total + jnp.dot(
        stacked[:, depth:], weights[1][...], preferred_element_type=jnp.float32
    )
    for k, out in enumerate(outs):
        part = total[k * rows : (k + 1) * rows]
        if begun:
            part = part + totals[k][...]
        out[...] = part.astype(out.dtype)


def partials(parts, weights, totals=()):
    rows, width = parts[0].shape
    depth, cols = weights[0].shape
    tile = 256
    begun = len(totals) > 0
    place = 1 if begun else 0
    block = pl.BlockSpec((rows, tile), lambda j: (0, j))
    types = [jnp.float32] + [jnp.bfloat16 if begun else jnp.float32] * (NZ - 1)
    return pl.pallas_call(
        functools.partial(partial_kernel, begun),
        grid=(cols // tile,),
        out_shape=[jax.ShapeDtypeStruct((rows, cols), kind) for kind in types],
        in_specs=[pl.BlockSpec((rows, width // 2), lambda j: (0, place))] * NZ
        + [pl.BlockSpec((depth, tile), lambda j: (0, j))] * 2
        + [block] * len(totals),
        out_specs=[block] * NZ,
        scratch_shapes=[pltpu.VMEM((NZ * rows, width // 2), jnp.bfloat16)],
        compiler_params=pltpu.CompilerParams(vmem_limit_bytes=14 * MIB),
        cost_estimate=pl.CostEstimate(
            flops=NZ * rows * width * cols,
            bytes_accessed=NZ * rows * width + width * cols + 4 * NZ * rows * cols,
            transcendentals=0,
        ),
        name="partials_rest" if begun else "partials",
    )(*parts, *weights, *totals)


def back_kernel(spots, groups, owner_ref, mixed_ref, *refs):
    count = len(spots)
    sources, out_ref, held, placed, goals, sems = refs[:count], *refs[count:]
    f = lax.axis_index("fsdp")
    y_lo, z, core = f // 8, lax.rem(f // 2, NZ), lax.rem(f, 2)
    width = held.shape[0]
    owned = width // owner_ref.shape[1]
    chunk = CHUNK * owned

    n = 0
    for (dy, dz, dc, t0), source in zip(spots, sources):
        first = (
            lax.rem(y_lo + dy, 2) * 64 + lax.rem(z + dz, NZ) * 16 + lax.rem(core + dc, 2) * 8 + t0
        )
        for part in range(source.shape[0] // chunk):
            pltpu.make_async_copy(
                source.at[pl.ds(part * chunk, chunk)], held.at[pl.ds(n * chunk, chunk)], sems.at[n]
            ).start()
            for b in range(CHUNK):
                goals[n * CHUNK + b] = owner_ref[1, first + part * CHUNK + b] * owned
            n += 1
    turned = mixed_ref[...].astype(jnp.float32).T.astype(jnp.bfloat16)

    def multiply(n, carry):
        at = pl.ds(pl.multiple_of(n * chunk, chunk), chunk)
        pltpu.make_async_copy(held.at[at], held.at[at], sems.at[n]).wait()
        terms = jnp.dot(held[at, :], turned, preferred_element_type=jnp.float32)
        terms = terms.astype(jnp.bfloat16)
        for b in range(CHUNK):
            spot = pl.multiple_of(goals[n * CHUNK + b], owned)
            placed[pl.ds(spot, owned), :] = terms[b * owned : (b + 1) * owned]
        return carry

    lax.fori_loop(0, width // chunk, multiply, 0)
    slab = width // groups

    def turn_back(t, carry):
        out_ref[t] = placed[pl.ds(pl.multiple_of(t * slab, slab), slab), :].T
        return carry

    lax.fori_loop(0, groups, turn_back, 0)


def project_back(mixed, sources, spots, block_owner, groups):
    rows, depth = mixed.shape
    width = sum(source.shape[0] for source in sources)
    return pl.pallas_call(
        functools.partial(back_kernel, spots, groups),
        out_shape=jax.ShapeDtypeStruct((groups, rows, width // groups), jnp.bfloat16),
        in_specs=[
            pl.BlockSpec(memory_space=pltpu.SMEM),
            pl.BlockSpec(memory_space=pltpu.VMEM),
        ]
        + [pl.BlockSpec(memory_space=pl.ANY)] * len(sources),
        out_specs=pl.BlockSpec(memory_space=pltpu.VMEM),
        scratch_shapes=[
            pltpu.VMEM((width, depth), jnp.bfloat16),
            pltpu.VMEM((width, rows), jnp.bfloat16),
            pltpu.SMEM((block_owner.shape[1],), jnp.int32),
            pltpu.SemaphoreType.DMA((block_owner.shape[1] // CHUNK,)),
        ],
        compiler_params=pltpu.CompilerParams(vmem_limit_bytes=48 * MIB),
        cost_estimate=pl.CostEstimate(
            flops=2 * rows * depth * width,
            bytes_accessed=2 * (rows * depth + depth * width + rows * width),
            transcendentals=0,
        ),
        name="project_back",
    )(block_owner, mixed, *sources)


def turns(lengths):
    half = HD // 2
    position = (lengths[None, :] + jnp.arange(2, dtype=jnp.int32)[:, None]).reshape(-1)
    freq = 1000000.0 ** (-jnp.arange(half, dtype=jnp.float32) * 2.0 / HD)
    angle = position.astype(jnp.float32)[:, None] * freq
    cosine, sine = jnp.cos(angle), jnp.sin(angle)
    return jnp.concatenate([cosine, cosine], axis=1), jnp.concatenate([-sine, sine], axis=1)


def attention_kernel(
    lengths_ref, p0, p1, p2, p3, cos_ref, sin_ref, cache_ref, out_ref, query, keys, values, result
):
    step = pl.program_id(0)
    both = p0.shape[0]
    rows = both // 2
    heads = out_ref.shape[1] // HD
    lanes = 2 * heads
    span = GROUP * lanes

    @pl.when(step == 0)
    def _():
        cosine, sine = cos_ref[...], sin_ref[...]

        def part(begin):
            cut = slice(begin * HD, (begin + 1) * HD)
            total = p0[:, cut] + p1[:, cut].astype(jnp.float32)
            return total + p2[:, cut].astype(jnp.float32) + p3[:, cut].astype(jnp.float32)

        def turn(x):
            return x * cosine + pltpu.roll(x, HD // 2, 1) * sine

        for h in range(heads):
            turned = turn(part(h))
            for s in range(2):
                query[pl.ds(s * heads + h, rows, stride=lanes), :] = turned[
                    s * rows : (s + 1) * rows
                ]
        new_keys, new_values = turn(part(heads)), part(heads + 1)
        for g in range(rows // GROUP):
            for t in range(2):
                to = slice((2 * g + t) * GROUP, (2 * g + t + 1) * GROUP)
                begin = t * rows + g * GROUP
                keys[to] = new_keys[begin : begin + GROUP]
                values[to] = new_values[begin : begin + GROUP]

    factor = 1.0 / math.sqrt(HD)
    nt = (((1,), (1,)), ((), ()))
    at = pl.ds(pl.multiple_of(step * span, span), span)
    fresh_at = pl.ds(pl.multiple_of(step * 2 * GROUP, 2 * GROUP), 2 * GROUP)
    q = query[at, :].astype(jnp.bfloat16)
    fresh = (
        lax.dot_general(
            q, keys[fresh_at, :].astype(jnp.bfloat16), nt, preferred_element_type=jnp.float32
        )
        * factor
    )
    of = lax.broadcasted_iota(jnp.int32, fresh.shape, 0)
    new = lax.broadcasted_iota(jnp.int32, fresh.shape, 1)
    seen = (of // lanes == new % GROUP) & (new // GROUP <= (of // heads) % 2)
    fresh = jnp.where(seen, fresh, -jnp.inf)

    held = cache_ref.shape[2]
    place = lax.broadcasted_iota(jnp.int32, (lanes, held), 1)
    pieces = []
    for r in range(GROUP):
        score = lax.dot_general(
            q[r * lanes : (r + 1) * lanes], cache_ref[0, r], nt, preferred_element_type=jnp.float32
        )
        pieces.append(jnp.where(place < lengths_ref[step * GROUP + r], score * factor, -jnp.inf))
    old = jnp.concatenate(pieces, axis=0)
    top = jnp.maximum(
        jnp.max(old, axis=1, keepdims=True), jnp.max(fresh, axis=1, keepdims=True)
    )
    old_w = jnp.exp(old - top)
    fresh_w = jnp.exp(fresh - top)
    total = jnp.sum(old_w, axis=1, keepdims=True) + jnp.sum(fresh_w, axis=1, keepdims=True)
    scale = 1.0 / total
    old_p = (old_w * scale).astype(jnp.bfloat16)
    fresh_p = (fresh_w * scale).astype(jnp.bfloat16)
    mixed = jnp.concatenate(
        [
            jnp.dot(
                old_p[r * lanes : (r + 1) * lanes],
                cache_ref[1, r],
                preferred_element_type=jnp.float32,
            )
            for r in range(GROUP)
        ],
        axis=0,
    )
    mixed = mixed + jnp.dot(
        fresh_p, values[fresh_at, :].astype(jnp.bfloat16), preferred_element_type=jnp.float32
    )
    result[at, :] = mixed

    @pl.when(step == pl.num_programs(0) - 1)
    def _():
        for h in range(heads):
            for s in range(2):
                out_ref[s * rows : (s + 1) * rows, h * HD : (h + 1) * HD] = result[
                    pl.ds(s * heads + h, rows, stride=lanes), :
                ].astype(out_ref.dtype)


def attention(sums, cos, sin, cache, lengths):
    both, cols = sums[0].shape
    rows = both // 2
    width = cols - 2 * HD
    held = cache.shape[2]
    lanes = 2 * width // HD

    def whole(*shape):
        return pl.BlockSpec(shape, lambda g: (0,) * len(shape))

    return pl.pallas_call(
        attention_kernel,
        grid=(rows // GROUP,),
        out_shape=jax.ShapeDtypeStruct((both, width), jnp.bfloat16),
        in_specs=[pl.BlockSpec(memory_space=pltpu.SMEM)]
        + [whole(both, cols)] * NZ
        + [whole(both, HD)] * 2
        + [pl.BlockSpec((2, GROUP, held, HD), lambda g: (0, g, 0, 0))],
        out_specs=whole(both, width),
        scratch_shapes=[
            pltpu.VMEM((rows * lanes, HD), jnp.float32),
            pltpu.VMEM((both, HD), jnp.float32),
            pltpu.VMEM((both, HD), jnp.float32),
            pltpu.VMEM((rows * lanes, HD), jnp.float32),
        ],
        compiler_params=pltpu.CompilerParams(vmem_limit_bytes=48 * MIB),
        cost_estimate=pl.CostEstimate(
            flops=4 * rows * lanes * held * HD,
            bytes_accessed=16 * rows * held * HD,
            transcendentals=rows * lanes * held,
        ),
        name="attention",
    )(lengths, *sums, cos, sin, cache)


def after(values, *first):
    return lax.optimization_barrier((*values, *first))[: len(values)]


def body(hidden, qkv_rows, o_rows, block_owner, cache, lengths):
    groups = lax.axis_size("tp")
    steps, rows, width = hidden.shape
    owned = qkv_rows.shape[0]
    query_cols = HQ * HD
    kv_cols = HK * HD
    cols = (query_cols + 2 * kv_cols) // groups
    copy = jnp.concatenate([qkv_rows.astype(jnp.bfloat16), o_rows.astype(jnp.bfloat16)], axis=1)
    copy = by_group(copy, (query_cols, kv_cols, kv_cols, query_cols), groups)

    cos, sin = turns(lengths)
    parts = shuffle(hidden.reshape(steps * rows, width), block_owner)
    parts = [parts[0]] + [z_shift(parts[k], k) for k in range(1, NZ)]

    both = flatten(lax.all_to_all(copy, "tp", split_axis=1, concat_axis=0, tiled=True))
    both, cos, sin, parts[1], parts[3] = lax.optimization_barrier(
        (both, cos, sin, parts[1], parts[3])
    )
    w, own = both[:, :cols], both[:, cols:]
    half = own.shape[0] // 2

    w_y, w_c = flip(w, 8), flip(w, 1)
    own, parts[2] = lax.optimization_barrier((own, parts[2]))
    below, above = z_shift(own, 1), z_shift(own, -1)
    own_c = flip(own, 1)
    begun = partials(parts, (w, w_c))
    w_y, below, above, own, own_c, *begun = lax.optimization_barrier(
        (w_y, below, above, own, own_c, *begun)
    )
    w_yc = flip(w_y, 1)
    far_a, far_b = z_shift(above[:half], -1), z_shift(below[half:], 1)
    across = flip(own, 8)

    sums = partials(parts, (w_y, w_yc), begun)
    sums = [sums[0]] + [z_shift(sums[k], -k) for k in range(1, NZ)]
    across, far_a, far_b, below, above = after((across, far_a, far_b, below, above), *sums)
    across_below, across_above = z_shift(across, 1), z_shift(across, -1)
    across_far_a, across_far_b = flip(far_a, 8), flip(far_b, 8)
    mixed = attention(sums, cos, sin, cache, lengths)

    below_c, above_c, across_c, far_ac, far_bc = (
        flip(value, 1) for value in after((below, above, across, far_a, far_b), mixed)
    )
    last = after((across_below, across_above, across_far_a, across_far_b), mixed)
    last_c = [flip(value, 1) for value in last]
    near = ((0, 0), (0, 3), (0, 1), (1, 0), (0, 2), (0, 2), (1, 3), (1, 1), (1, 2), (1, 2))
    begins = (0, 0, 0, 0, 0, 4, 0, 0, 0, 4)
    sources = [own, below, above, across, far_a, far_b, *last]
    sources += [own_c, below_c, above_c, across_c, far_ac, far_bc, *last_c]
    spots = tuple((*at, core, t0) for core in (0, 1) for at, t0 in zip(near, begins))
    order = (0, 10, 1, 2, 11, 12, 3, 13, 4, 5, 14, 15, 6, 7, 8, 9, 16, 17, 18, 19)
    sources, spots = [sources[n] for n in order], tuple(spots[n] for n in order)
    terms = project_back(mixed, sources, spots, block_owner, groups)
    terms = lax.all_to_all(terms, "tp", split_axis=0, concat_axis=0, tiled=True)
    summed = jnp.sum(terms.astype(jnp.float32), axis=0).astype(jnp.bfloat16)
    return summed.reshape(steps, rows, width // groups)


def solution(mesh):
    in_specs = (
        P(None, "fsdp", None),
        P(("fsdp", "tp"), None),
        P(("fsdp", "tp"), None),
        P(),
        P(None, "fsdp", None, "tp"),
        P("fsdp"),
    )
    out_specs = P(None, "fsdp", "tp")
    return jax.shard_map(body, mesh=mesh, in_specs=in_specs, out_specs=out_specs, check_vma=False)
```

```python
import functools
import math

import jax
import jax.numpy as jnp
from jax import lax
from jax.experimental import pallas as pl
from jax.experimental.pallas import tpu as pltpu
from jax.sharding import PartitionSpec as P

HQ = 64
HK = 8
HD = 128
NZ = 4
GROUP = 8
CHUNK = 256
MIB = 1024 * 1024


def z_shift(value, k):
    pairs = [(f, (f // 8) * 8 + ((f // 2 + k) % NZ) * 2 + f % 2) for f in range(16)]
    return lax.ppermute(value, "fsdp", pairs)


def flip(value, bit):
    return lax.ppermute(value, "fsdp", [(f, f ^ bit) for f in range(16)])


def by_group(array, sections, groups):
    pieces = []
    begin = 0
    for width in sections:
        pieces.append(
            array[:, begin : begin + width].reshape(array.shape[0], groups, width // groups)
        )
        begin = begin + width
    return jnp.concatenate(pieces, axis=2)


def flatten(received):
    return received.reshape(received.shape[0], received.shape[2])


def shuffle_kernel(owner_ref, hidden_ref, *out_refs):
    f = lax.axis_index("fsdp")
    y_lo, z, core = f // 8, lax.rem(f // 2, 4), lax.rem(f, 2)
    rows = hidden_ref.shape[0]
    low = lax.broadcasted_iota(jnp.int32, (rows, 128), 1) < 64

    for k, out_ref in enumerate(out_refs):
        zz = lax.rem(z + k, 4)

        def step(n, carry, zz=zz, out_ref=out_ref):
            q, p = n // 4, lax.rem(n, 4)
            yy = lax.rem(y_lo + q // 2, 2)
            cc = lax.rem(core + lax.rem(q, 2), 2)
            i = yy * 64 + zz * 16 + cc * 8 + 2 * p
            s0, s1 = owner_ref[0, i], owner_ref[0, i + 1]
            a = hidden_ref[:, pl.ds(pl.multiple_of((s0 // 2) * 128, 128), 128)].astype(jnp.float32)
            b = hidden_ref[:, pl.ds(pl.multiple_of((s1 // 2) * 128, 128), 128)].astype(jnp.float32)
            a = pltpu.roll(a, 64 * lax.rem(s0, 2), 1)
            b = pltpu.roll(b, 64 * (1 - lax.rem(s1, 2)), 1)
            out_ref[:, pl.ds(pl.multiple_of(n * 128, 128), 128)] = jnp.where(low, a, b).astype(
                jnp.bfloat16
            )
            return carry

        lax.fori_loop(0, 16, step, 0, unroll=4)


def shuffle(hidden, block_owner):
    rows, width = hidden.shape
    part = jax.ShapeDtypeStruct((rows, width // NZ), jnp.bfloat16)
    return pl.pallas_call(
        shuffle_kernel,
        out_shape=[part] * NZ,
        in_specs=[
            pl.BlockSpec(memory_space=pltpu.SMEM),
            pl.BlockSpec(memory_space=pltpu.VMEM),
        ],
        out_specs=[pl.BlockSpec(memory_space=pltpu.VMEM)] * NZ,
        compiler_params=pltpu.CompilerParams(vmem_limit_bytes=14 * MIB),
        cost_estimate=pl.CostEstimate(
            flops=rows * width * 8, bytes_accessed=4 * rows * width, transcendentals=0
        ),
        name="shuffle",
    )(block_owner, hidden)


def partial_kernel(begun, *refs):
    held, weights = refs[:NZ], refs[NZ : NZ + 2]
    totals = refs[NZ + 2 : 2 * NZ + 2] if begun else ()
    *outs, stacked = refs[NZ + 2 + len(totals) :]
    rows = held[0].shape[0]
    depth = weights[0].shape[0]

    @pl.when(pl.program_id(0) == 0)
    def _():
        for k, h in enumerate(held):
            stacked[pl.ds(k * rows, rows), :] = h[...]

    total = jnp.dot(stacked[:, :depth], weights[0][...], preferred_element_type=jnp.float32)
    total = total + jnp.dot(
        stacked[:, depth:], weights[1][...], preferred_element_type=jnp.float32
    )
    for k, out in enumerate(outs):
        part = total[k * rows : (k + 1) * rows]
        if begun:
            part = part + totals[k][...]
        out[...] = part.astype(out.dtype)


def partials(parts, weights, totals=()):
    rows, width = parts[0].shape
    depth, cols = weights[0].shape
    tile = 256
    begun = len(totals) > 0
    place = 1 if begun else 0
    block = pl.BlockSpec((rows, tile), lambda j: (0, j))
    types = [jnp.float32] + [jnp.bfloat16 if begun else jnp.float32] * (NZ - 1)
    return pl.pallas_call(
        functools.partial(partial_kernel, begun),
        grid=(cols // tile,),
        out_shape=[jax.ShapeDtypeStruct((rows, cols), kind) for kind in types],
        in_specs=[pl.BlockSpec((rows, width // 2), lambda j: (0, place))] * NZ
        + [pl.BlockSpec((depth, tile), lambda j: (0, j))] * 2
        + [block] * len(totals),
        out_specs=[block] * NZ,
        scratch_shapes=[pltpu.VMEM((NZ * rows, width // 2), jnp.bfloat16)],
        compiler_params=pltpu.CompilerParams(vmem_limit_bytes=14 * MIB),
        cost_estimate=pl.CostEstimate(
            flops=NZ * rows * width * cols,
            bytes_accessed=NZ * rows * width + width * cols + 4 * NZ * rows * cols,
            transcendentals=0,
        ),
        name="partials_rest" if begun else "partials",
    )(*parts, *weights, *totals)


def terms_kernel(mixed_ref, *refs):
    *sources, out_ref = refs
    spare = out_ref.shape[1] - mixed_ref.shape[0]
    wide = jnp.pad(mixed_ref[...].astype(jnp.float32), ((0, spare), (0, 0)))
    turned = wide.T.astype(jnp.bfloat16)
    begin = 0
    for source in sources:

        def multiply(n, carry, source=source, begin=begin):
            rows = source[pl.ds(pl.multiple_of(n * CHUNK, CHUNK), CHUNK), :]
            to = pl.ds(pl.multiple_of(begin + n * CHUNK, CHUNK), CHUNK)
            out_ref[to, :] = jnp.dot(rows, turned, preferred_element_type=jnp.float32).astype(
                out_ref.dtype
            )
            return carry

        lax.fori_loop(0, source.shape[0] // CHUNK, multiply, 0)
        begin += source.shape[0]


def terms_of(mixed, sources):
    rows, depth = mixed.shape
    width = sum(source.shape[0] for source in sources)
    lanes = -(-rows // 128) * 128
    vmem = pl.BlockSpec(memory_space=pltpu.VMEM)
    return pl.pallas_call(
        terms_kernel,
        out_shape=jax.ShapeDtypeStruct((width, lanes), jnp.bfloat16),
        in_specs=[vmem] * (1 + len(sources)),
        out_specs=vmem,
        compiler_params=pltpu.CompilerParams(vmem_limit_bytes=20 * MIB),
        cost_estimate=pl.CostEstimate(
            flops=2 * rows * depth * width,
            bytes_accessed=2 * (rows * depth + depth * width + rows * width),
            transcendentals=0,
        ),
        name="terms",
    )(mixed, *sources)


def place_kernel(spots, groups, owner_ref, *refs):
    *pieces, out_ref, placed = refs
    f = lax.axis_index("fsdp")
    y_lo, z, core = f // 8, lax.rem(f // 2, NZ), lax.rem(f, 2)
    width = placed.shape[0]
    owned = width // owner_ref.shape[1]
    for n, dy, dz, dc, t0, blocks, begin in spots:
        first = (
            lax.rem(y_lo + dy, 2) * 64 + lax.rem(z + dz, NZ) * 16 + lax.rem(core + dc, 2) * 8 + t0
        )

        def put(b, carry, n=n, first=first, begin=begin):
            goal = pl.multiple_of(owner_ref[1, first + b] * owned, owned)
            start = pl.multiple_of(begin + b * owned, owned)
            placed[pl.ds(goal, owned), :] = pieces[n][pl.ds(start, owned), :]
            return carry

        lax.fori_loop(0, blocks, put, 0)
    slab = width // groups

    def turn_back(t, carry):
        slab_t = placed[pl.ds(pl.multiple_of(t * slab, slab), slab), :].T
        out_ref[t] = slab_t[: out_ref.shape[1]]
        return carry

    lax.fori_loop(0, groups, turn_back, 0)


def place(pieces, spots, block_owner, groups, rows):
    width = sum(piece.shape[0] for piece in pieces)
    lanes = pieces[0].shape[1]
    vmem = pl.BlockSpec(memory_space=pltpu.VMEM)
    return pl.pallas_call(
        functools.partial(place_kernel, spots, groups),
        out_shape=jax.ShapeDtypeStruct((groups, rows, width // groups), jnp.bfloat16),
        in_specs=[pl.BlockSpec(memory_space=pltpu.SMEM)] + [vmem] * len(pieces),
        out_specs=vmem,
        scratch_shapes=[pltpu.VMEM((width, lanes), jnp.bfloat16)],
        compiler_params=pltpu.CompilerParams(vmem_limit_bytes=20 * MIB),
        cost_estimate=pl.CostEstimate(
            flops=0, bytes_accessed=8 * rows * width, transcendentals=0
        ),
        name="place",
    )(block_owner, *pieces)


def turns(lengths):
    half = HD // 2
    position = (lengths[None, :] + jnp.arange(2, dtype=jnp.int32)[:, None]).reshape(-1)
    freq = 1000000.0 ** (-jnp.arange(half, dtype=jnp.float32) * 2.0 / HD)
    angle = position.astype(jnp.float32)[:, None] * freq
    cosine, sine = jnp.cos(angle), jnp.sin(angle)
    return jnp.concatenate([cosine, cosine], axis=1), jnp.concatenate([-sine, sine], axis=1)


def attention_kernel(
    lengths_ref, p0, p1, p2, p3, cos_ref, sin_ref, cache_ref, out_ref, query, keys, values, result
):
    step = pl.program_id(0)
    both = p0.shape[0]
    rows = both // 2
    heads = out_ref.shape[1] // HD
    lanes = 2 * heads
    span = GROUP * lanes

    @pl.when(step == 0)
    def _():
        cosine, sine = cos_ref[...], sin_ref[...]

        def part(begin):
            cut = slice(begin * HD, (begin + 1) * HD)
            total = p0[:, cut] + p1[:, cut].astype(jnp.float32)
            return total + p2[:, cut].astype(jnp.float32) + p3[:, cut].astype(jnp.float32)

        def turn(x):
            return x * cosine + pltpu.roll(x, HD // 2, 1) * sine

        for h in range(heads):
            turned = turn(part(h))
            for s in range(2):
                query[pl.ds(s * heads + h, rows, stride=lanes), :] = turned[
                    s * rows : (s + 1) * rows
                ]
        new_keys, new_values = turn(part(heads)), part(heads + 1)
        for g in range(rows // GROUP):
            for t in range(2):
                to = slice((2 * g + t) * GROUP, (2 * g + t + 1) * GROUP)
                begin = t * rows + g * GROUP
                keys[to] = new_keys[begin : begin + GROUP]
                values[to] = new_values[begin : begin + GROUP]

    factor = 1.0 / math.sqrt(HD)
    nt = (((1,), (1,)), ((), ()))
    at = pl.ds(pl.multiple_of(step * span, span), span)
    fresh_at = pl.ds(pl.multiple_of(step * 2 * GROUP, 2 * GROUP), 2 * GROUP)
    q = query[at, :].astype(jnp.bfloat16)
    fresh = (
        lax.dot_general(
            q, keys[fresh_at, :].astype(jnp.bfloat16), nt, preferred_element_type=jnp.float32
        )
        * factor
    )
    of = lax.broadcasted_iota(jnp.int32, fresh.shape, 0)
    new = lax.broadcasted_iota(jnp.int32, fresh.shape, 1)
    seen = (of // lanes == new % GROUP) & (new // GROUP <= (of // heads) % 2)
    fresh = jnp.where(seen, fresh, -jnp.inf)

    held = cache_ref.shape[2]
    place = lax.broadcasted_iota(jnp.int32, (lanes, held), 1)
    pieces = []
    for r in range(GROUP):
        score = lax.dot_general(
            q[r * lanes : (r + 1) * lanes], cache_ref[0, r], nt, preferred_element_type=jnp.float32
        )
        pieces.append(jnp.where(place < lengths_ref[step * GROUP + r], score * factor, -jnp.inf))
    old = jnp.concatenate(pieces, axis=0)
    top = jnp.maximum(
        jnp.max(old, axis=1, keepdims=True), jnp.max(fresh, axis=1, keepdims=True)
    )
    old_w = jnp.exp(old - top)
    fresh_w = jnp.exp(fresh - top)
    total = jnp.sum(old_w, axis=1, keepdims=True) + jnp.sum(fresh_w, axis=1, keepdims=True)
    scale = 1.0 / total
    old_p = (old_w * scale).astype(jnp.bfloat16)
    fresh_p = (fresh_w * scale).astype(jnp.bfloat16)
    mixed = jnp.concatenate(
        [
            jnp.dot(
                old_p[r * lanes : (r + 1) * lanes],
                cache_ref[1, r],
                preferred_element_type=jnp.float32,
            )
            for r in range(GROUP)
        ],
        axis=0,
    )
    mixed = mixed + jnp.dot(
        fresh_p, values[fresh_at, :].astype(jnp.bfloat16), preferred_element_type=jnp.float32
    )
    result[at, :] = mixed

    @pl.when(step == pl.num_programs(0) - 1)
    def _():
        for h in range(heads):
            for s in range(2):
                out_ref[s * rows : (s + 1) * rows, h * HD : (h + 1) * HD] = result[
                    pl.ds(s * heads + h, rows, stride=lanes), :
                ].astype(out_ref.dtype)


def attention(sums, cos, sin, cache, lengths):
    both, cols = sums[0].shape
    rows = both // 2
    width = cols - 2 * HD
    held = cache.shape[2]
    lanes = 2 * width // HD

    def whole(*shape):
        return pl.BlockSpec(shape, lambda g: (0,) * len(shape))

    return pl.pallas_call(
        attention_kernel,
        grid=(rows // GROUP,),
        out_shape=jax.ShapeDtypeStruct((both, width), jnp.bfloat16),
        in_specs=[pl.BlockSpec(memory_space=pltpu.SMEM)]
        + [whole(both, cols)] * NZ
        + [whole(both, HD)] * 2
        + [pl.BlockSpec((2, GROUP, held, HD), lambda g: (0, g, 0, 0))],
        out_specs=whole(both, width),
        scratch_shapes=[
            pltpu.VMEM((rows * lanes, HD), jnp.float32),
            pltpu.VMEM((both, HD), jnp.float32),
            pltpu.VMEM((both, HD), jnp.float32),
            pltpu.VMEM((rows * lanes, HD), jnp.float32),
        ],
        compiler_params=pltpu.CompilerParams(vmem_limit_bytes=48 * MIB),
        cost_estimate=pl.CostEstimate(
            flops=4 * rows * lanes * held * HD,
            bytes_accessed=16 * rows * held * HD,
            transcendentals=rows * lanes * held,
        ),
        name="attention",
    )(lengths, *sums, cos, sin, cache)


def after(values, *first):
    return lax.optimization_barrier((*values, *first))[: len(values)]


def body(hidden, qkv_rows, o_rows, block_owner, cache, lengths):
    groups = lax.axis_size("tp")
    steps, rows, width = hidden.shape
    owned = qkv_rows.shape[0]
    query_cols = HQ * HD
    kv_cols = HK * HD
    cols = (query_cols + 2 * kv_cols) // groups
    copy = jnp.concatenate([qkv_rows.astype(jnp.bfloat16), o_rows.astype(jnp.bfloat16)], axis=1)
    copy = by_group(copy, (query_cols, kv_cols, kv_cols, query_cols), groups)

    cos, sin = turns(lengths)
    parts = shuffle(hidden.reshape(steps * rows, width), block_owner)
    parts = [parts[0]] + [z_shift(parts[k], k) for k in range(1, NZ)]

    both = flatten(lax.all_to_all(copy, "tp", split_axis=1, concat_axis=0, tiled=True))
    both, cos, sin, parts[1], parts[3] = lax.optimization_barrier(
        (both, cos, sin, parts[1], parts[3])
    )
    w, own = both[:, :cols], both[:, cols:]
    half = own.shape[0] // 2

    w_y, w_c = flip(w, 8), flip(w, 1)
    own, parts[2] = lax.optimization_barrier((own, parts[2]))
    below, above = z_shift(own, 1), z_shift(own, -1)
    begun = partials(parts, (w, w_c))
    w_y, below, above, own, *begun = lax.optimization_barrier((w_y, below, above, own, *begun))
    w_yc = flip(w_y, 1)
    far_a, far_b = z_shift(above[:half], -1), z_shift(below[half:], 1)
    across = flip(own, 8)

    sums = partials(parts, (w_y, w_yc), begun)
    sums = [sums[0]] + [z_shift(sums[k], -k) for k in range(1, NZ)]
    far_a, far_b, across = after((far_a, far_b, across))
    across_far_a, across_far_b = flip(far_a, 8), flip(far_b, 8)
    (across,) = after((across,), *sums)
    across_below, across_above = z_shift(across, 1), z_shift(across, -1)
    mixed = attention(sums, cos, sin, cache, lengths)

    mixed_c = flip(mixed, 1)
    sources = (own, below, above, across, far_a, far_b)
    sources += (across_far_a, across_far_b, across_below, across_above)
    theirs = terms_of(mixed_c, sources)
    mine = terms_of(*after((mixed,), theirs), sources)
    pieces = (mine, flip(theirs, 1))
    places = ((0, 0, 0), (0, 3, 0), (0, 1, 0), (1, 0, 0), (0, 2, 0), (0, 2, 4))
    places += ((1, 2, 0), (1, 2, 4), (1, 3, 0), (1, 1, 0))
    spots = []
    for core in range(2):
        begin = 0
        for (dy, dz, t0), source in zip(places, sources):
            size = source.shape[0]
            spots.append((core, dy, dz, core, t0, size // owned, begin))
            begin += size
    terms = place(pieces, tuple(spots), block_owner, groups, steps * rows)
    terms = lax.all_to_all(terms, "tp", split_axis=0, concat_axis=0, tiled=True)
    summed = jnp.sum(terms.astype(jnp.float32), axis=0).astype(jnp.bfloat16)
    return summed.reshape(steps, rows, width // groups)


def solution(mesh):
    in_specs = (
        P(None, "fsdp", None),
        P(("fsdp", "tp"), None),
        P(("fsdp", "tp"), None),
        P(),
        P(None, "fsdp", None, "tp"),
        P("fsdp"),
    )
    out_specs = P(None, "fsdp", "tp")
    return jax.shard_map(body, mesh=mesh, in_specs=in_specs, out_specs=out_specs, check_vma=False)
```

```python
import functools
import math

import jax
import jax.numpy as jnp
from jax import lax
from jax.experimental import pallas as pl
from jax.experimental.pallas import tpu as pltpu
from jax.sharding import PartitionSpec as P

HQ = 64
HK = 8
HD = 128
NZ = 4
NX = 4
GROUP = 8
CHUNK = 256
MIB = 1024 * 1024


def z_shift(value, k):
    pairs = [(f, (f // 8) * 8 + ((f // 2 + k) % NZ) * 2 + f % 2) for f in range(16)]
    return lax.ppermute(value, "fsdp", pairs)


def flip(value, bit):
    return lax.ppermute(value, "fsdp", [(f, f ^ bit) for f in range(16)])


def x_shift(value, k):
    return lax.ppermute(value, "tp", [(t, (t // 2 + k) % NX * 2 + t % 2) for t in range(2 * NX)])


def y_flip(value):
    return lax.ppermute(value, "tp", [(t, t ^ 1) for t in range(2 * NX)])


def by_group(array, sections, groups):
    pieces = []
    begin = 0
    for width in sections:
        pieces.append(
            array[:, begin : begin + width].reshape(array.shape[0], groups, width // groups)
        )
        begin = begin + width
    return jnp.concatenate(pieces, axis=2)


def flatten(received):
    return received.reshape(received.shape[0], received.shape[2])


def shuffle_kernel(owner_ref, hidden_ref, *out_refs):
    f = lax.axis_index("fsdp")
    y_lo, z, core = f // 8, lax.rem(f // 2, 4), lax.rem(f, 2)
    rows = hidden_ref.shape[0]
    low = lax.broadcasted_iota(jnp.int32, (rows, 128), 1) < 64

    for k, out_ref in enumerate(out_refs):
        zz = lax.rem(z + k, 4)

        def step(n, carry, zz=zz, out_ref=out_ref):
            q, p = n // 4, lax.rem(n, 4)
            yy = lax.rem(y_lo + q // 2, 2)
            cc = lax.rem(core + lax.rem(q, 2), 2)
            i = yy * 64 + zz * 16 + cc * 8 + 2 * p
            s0, s1 = owner_ref[0, i], owner_ref[0, i + 1]
            a = hidden_ref[:, pl.ds(pl.multiple_of((s0 // 2) * 128, 128), 128)].astype(jnp.float32)
            b = hidden_ref[:, pl.ds(pl.multiple_of((s1 // 2) * 128, 128), 128)].astype(jnp.float32)
            a = pltpu.roll(a, 64 * lax.rem(s0, 2), 1)
            b = pltpu.roll(b, 64 * (1 - lax.rem(s1, 2)), 1)
            out_ref[:, pl.ds(pl.multiple_of(n * 128, 128), 128)] = jnp.where(low, a, b).astype(
                jnp.bfloat16
            )
            return carry

        lax.fori_loop(0, 16, step, 0, unroll=4)


def shuffle(hidden, block_owner):
    rows, width = hidden.shape
    part = jax.ShapeDtypeStruct((rows, width // NZ), jnp.bfloat16)
    return pl.pallas_call(
        shuffle_kernel,
        out_shape=[part] * NZ,
        in_specs=[
            pl.BlockSpec(memory_space=pltpu.SMEM),
            pl.BlockSpec(memory_space=pltpu.VMEM),
        ],
        out_specs=[pl.BlockSpec(memory_space=pltpu.VMEM)] * NZ,
        compiler_params=pltpu.CompilerParams(vmem_limit_bytes=14 * MIB),
        cost_estimate=pl.CostEstimate(
            flops=rows * width * 8, bytes_accessed=4 * rows * width, transcendentals=0
        ),
        name="shuffle",
    )(block_owner, hidden)


def partial_kernel(begun, *refs):
    held, weights = refs[:NZ], refs[NZ : NZ + 2]
    totals = refs[NZ + 2 : 2 * NZ + 2] if begun else ()
    *outs, stacked = refs[NZ + 2 + len(totals) :]
    rows = held[0].shape[0]
    depth = weights[0].shape[0]

    @pl.when(pl.program_id(0) == 0)
    def _():
        for k, h in enumerate(held):
            stacked[pl.ds(k * rows, rows), :] = h[...]

    total = jnp.dot(stacked[:, :depth], weights[0][...], preferred_element_type=jnp.float32)
    total = total + jnp.dot(
        stacked[:, depth:], weights[1][...], preferred_element_type=jnp.float32
    )
    for k, out in enumerate(outs):
        part = total[k * rows : (k + 1) * rows]
        if begun:
            part = part + totals[k][...]
        out[...] = part.astype(out.dtype)


def partials(parts, weights, totals=()):
    rows, width = parts[0].shape
    depth, cols = weights[0].shape
    tile = 256
    begun = len(totals) > 0
    place = 1 if begun else 0
    block = pl.BlockSpec((rows, tile), lambda j: (0, j))
    types = [jnp.float32] + [jnp.bfloat16 if begun else jnp.float32] * (NZ - 1)
    return pl.pallas_call(
        functools.partial(partial_kernel, begun),
        grid=(cols // tile,),
        out_shape=[jax.ShapeDtypeStruct((rows, cols), kind) for kind in types],
        in_specs=[pl.BlockSpec((rows, width // 2), lambda j: (0, place))] * NZ
        + [pl.BlockSpec((depth, tile), lambda j: (0, j))] * 2
        + [block] * len(totals),
        out_specs=[block] * NZ,
        scratch_shapes=[pltpu.VMEM((NZ * rows, width // 2), jnp.bfloat16)],
        compiler_params=pltpu.CompilerParams(vmem_limit_bytes=14 * MIB),
        cost_estimate=pl.CostEstimate(
            flops=NZ * rows * width * cols,
            bytes_accessed=NZ * rows * width + width * cols + 4 * NZ * rows * cols,
            transcendentals=0,
        ),
        name="partials_rest" if begun else "partials",
    )(*parts, *weights, *totals)


def terms_kernel(mixed_ref, *refs):
    *sources, out_ref = refs
    spare = out_ref.shape[1] - mixed_ref.shape[0]
    wide = jnp.pad(mixed_ref[...].astype(jnp.float32), ((0, spare), (0, 0)))
    turned = wide.T.astype(jnp.bfloat16)
    begin = 0
    for source in sources:

        def multiply(n, carry, source=source, begin=begin):
            rows = source[pl.ds(pl.multiple_of(n * CHUNK, CHUNK), CHUNK), :]
            to = pl.ds(pl.multiple_of(begin + n * CHUNK, CHUNK), CHUNK)
            out_ref[to, :] = jnp.dot(rows, turned, preferred_element_type=jnp.float32).astype(
                out_ref.dtype
            )
            return carry

        lax.fori_loop(0, source.shape[0] // CHUNK, multiply, 0)
        begin += source.shape[0]


def terms_of(mixed, sources):
    rows, depth = mixed.shape
    width = sum(source.shape[0] for source in sources)
    lanes = -(-rows // 128) * 128
    vmem = pl.BlockSpec(memory_space=pltpu.VMEM)
    return pl.pallas_call(
        terms_kernel,
        out_shape=jax.ShapeDtypeStruct((width, lanes), jnp.bfloat16),
        in_specs=[vmem] * (1 + len(sources)),
        out_specs=vmem,
        compiler_params=pltpu.CompilerParams(vmem_limit_bytes=20 * MIB),
        cost_estimate=pl.CostEstimate(
            flops=2 * rows * depth * width,
            bytes_accessed=2 * (rows * depth + depth * width + rows * width),
            transcendentals=0,
        ),
        name="terms",
    )(mixed, *sources)


def place_kernel(spots, groups, owner_ref, *refs):
    pieces, firsts, seconds = refs[:-7], refs[-7:-3], refs[-3:-1]
    placed = refs[-1]
    f = lax.axis_index("fsdp")
    y_lo, z, core = f // 8, lax.rem(f // 2, NZ), lax.rem(f, 2)
    width = placed.shape[0]
    owned = width // owner_ref.shape[1]
    for n, dy, dz, dc, t0, blocks, begin in spots:
        first = (
            lax.rem(y_lo + dy, 2) * 64 + lax.rem(z + dz, NZ) * 16 + lax.rem(core + dc, 2) * 8 + t0
        )

        def put(b, carry, n=n, first=first, begin=begin):
            goal = pl.multiple_of(owner_ref[1, first + b] * owned, owned)
            start = pl.multiple_of(begin + b * owned, owned)
            placed[pl.ds(goal, owned), :] = pieces[n][pl.ds(start, owned), :]
            return carry

        lax.fori_loop(0, blocks, put, 0)
    slab = width // groups
    t = lax.axis_index("tp")
    for k in range(NX):
        for j in range(2):
            at = lax.rem(t // 2 + k, NX) * 2 + lax.rem(lax.rem(t, 2) + j, 2)
            turned = placed[pl.ds(pl.multiple_of(at * slab, slab), slab), :].T
            rows = firsts[k].shape[1]
            firsts[k][j] = turned[:rows]
            seconds[j][k] = turned[rows : 2 * rows]


def place(pieces, spots, block_owner, groups, rows):
    width = sum(piece.shape[0] for piece in pieces)
    lanes = pieces[0].shape[1]
    vmem = pl.BlockSpec(memory_space=pltpu.VMEM)
    return pl.pallas_call(
        functools.partial(place_kernel, spots, groups),
        out_shape=[jax.ShapeDtypeStruct((2, rows, width // groups), jnp.bfloat16)] * NX
        + [jax.ShapeDtypeStruct((NX, rows, width // groups), jnp.bfloat16)] * 2,
        in_specs=[pl.BlockSpec(memory_space=pltpu.SMEM)] + [vmem] * len(pieces),
        out_specs=[vmem] * (NX + 2),
        scratch_shapes=[pltpu.VMEM((width, lanes), jnp.bfloat16)],
        compiler_params=pltpu.CompilerParams(vmem_limit_bytes=20 * MIB),
        cost_estimate=pl.CostEstimate(
            flops=0, bytes_accessed=8 * rows * width, transcendentals=0
        ),
        name="place",
    )(block_owner, *pieces)


def turns(lengths):
    half = HD // 2
    position = (lengths[None, :] + jnp.arange(2, dtype=jnp.int32)[:, None]).reshape(-1)
    freq = 1000000.0 ** (-jnp.arange(half, dtype=jnp.float32) * 2.0 / HD)
    angle = position.astype(jnp.float32)[:, None] * freq
    cosine, sine = jnp.cos(angle), jnp.sin(angle)
    return jnp.concatenate([cosine, cosine], axis=1), jnp.concatenate([-sine, sine], axis=1)


def attention_kernel(
    lengths_ref, p0, p1, p2, p3, cos_ref, sin_ref, cache_ref, out_ref, query, keys, values, result
):
    step = pl.program_id(0)
    both = p0.shape[0]
    rows = both // 2
    heads = out_ref.shape[1] // HD
    lanes = 2 * heads
    span = GROUP * lanes

    @pl.when(step == 0)
    def _():
        cosine, sine = cos_ref[...], sin_ref[...]

        def part(begin):
            cut = slice(begin * HD, (begin + 1) * HD)
            total = p0[:, cut] + p1[:, cut].astype(jnp.float32)
            return total + p2[:, cut].astype(jnp.float32) + p3[:, cut].astype(jnp.float32)

        def turn(x):
            return x * cosine + pltpu.roll(x, HD // 2, 1) * sine

        for h in range(heads):
            turned = turn(part(h))
            for s in range(2):
                query[pl.ds(s * heads + h, rows, stride=lanes), :] = turned[
                    s * rows : (s + 1) * rows
                ]
        new_keys, new_values = turn(part(heads)), part(heads + 1)
        for g in range(rows // GROUP):
            for t in range(2):
                to = slice((2 * g + t) * GROUP, (2 * g + t + 1) * GROUP)
                begin = t * rows + g * GROUP
                keys[to] = new_keys[begin : begin + GROUP]
                values[to] = new_values[begin : begin + GROUP]

    factor = 1.0 / math.sqrt(HD)
    nt = (((1,), (1,)), ((), ()))
    at = pl.ds(pl.multiple_of(step * span, span), span)
    fresh_at = pl.ds(pl.multiple_of(step * 2 * GROUP, 2 * GROUP), 2 * GROUP)
    q = query[at, :].astype(jnp.bfloat16)
    fresh = (
        lax.dot_general(
            q, keys[fresh_at, :].astype(jnp.bfloat16), nt, preferred_element_type=jnp.float32
        )
        * factor
    )
    of = lax.broadcasted_iota(jnp.int32, fresh.shape, 0)
    new = lax.broadcasted_iota(jnp.int32, fresh.shape, 1)
    seen = (of // lanes == new % GROUP) & (new // GROUP <= (of // heads) % 2)
    fresh = jnp.where(seen, fresh, -jnp.inf)

    held = cache_ref.shape[2]
    place = lax.broadcasted_iota(jnp.int32, (lanes, held), 1)
    pieces = []
    for r in range(GROUP):
        score = lax.dot_general(
            q[r * lanes : (r + 1) * lanes], cache_ref[0, r], nt, preferred_element_type=jnp.float32
        )
        pieces.append(jnp.where(place < lengths_ref[step * GROUP + r], score * factor, -jnp.inf))
    old = jnp.concatenate(pieces, axis=0)
    top = jnp.maximum(
        jnp.max(old, axis=1, keepdims=True), jnp.max(fresh, axis=1, keepdims=True)
    )
    old_w = jnp.exp(old - top)
    fresh_w = jnp.exp(fresh - top)
    total = jnp.sum(old_w, axis=1, keepdims=True) + jnp.sum(fresh_w, axis=1, keepdims=True)
    scale = 1.0 / total
    old_p = (old_w * scale).astype(jnp.bfloat16)
    fresh_p = (fresh_w * scale).astype(jnp.bfloat16)
    mixed = jnp.concatenate(
        [
            jnp.dot(
                old_p[r * lanes : (r + 1) * lanes],
                cache_ref[1, r],
                preferred_element_type=jnp.float32,
            )
            for r in range(GROUP)
        ],
        axis=0,
    )
    mixed = mixed + jnp.dot(
        fresh_p, values[fresh_at, :].astype(jnp.bfloat16), preferred_element_type=jnp.float32
    )
    result[at, :] = mixed

    @pl.when(step == pl.num_programs(0) - 1)
    def _():
        for h in range(heads):
            for s in range(2):
                out_ref[s * rows : (s + 1) * rows, h * HD : (h + 1) * HD] = result[
                    pl.ds(s * heads + h, rows, stride=lanes), :
                ].astype(out_ref.dtype)


def attention(sums, cos, sin, cache, lengths):
    both, cols = sums[0].shape
    rows = both // 2
    width = cols - 2 * HD
    held = cache.shape[2]
    lanes = 2 * width // HD

    def whole(*shape):
        return pl.BlockSpec(shape, lambda g: (0,) * len(shape))

    return pl.pallas_call(
        attention_kernel,
        grid=(rows // GROUP,),
        out_shape=jax.ShapeDtypeStruct((both, width), jnp.bfloat16),
        in_specs=[pl.BlockSpec(memory_space=pltpu.SMEM)]
        + [whole(both, cols)] * NZ
        + [whole(both, HD)] * 2
        + [pl.BlockSpec((2, GROUP, held, HD), lambda g: (0, g, 0, 0))],
        out_specs=whole(both, width),
        scratch_shapes=[
            pltpu.VMEM((rows * lanes, HD), jnp.float32),
            pltpu.VMEM((both, HD), jnp.float32),
            pltpu.VMEM((both, HD), jnp.float32),
            pltpu.VMEM((rows * lanes, HD), jnp.float32),
        ],
        compiler_params=pltpu.CompilerParams(vmem_limit_bytes=48 * MIB),
        cost_estimate=pl.CostEstimate(
            flops=4 * rows * lanes * held * HD,
            bytes_accessed=16 * rows * held * HD,
            transcendentals=rows * lanes * held,
        ),
        name="attention",
    )(lengths, *sums, cos, sin, cache)


def after(values, *first):
    return lax.optimization_barrier((*values, *first))[: len(values)]


def body(hidden, qkv_rows, o_rows, block_owner, cache, lengths):
    groups = lax.axis_size("tp")
    steps, rows, width = hidden.shape
    owned = qkv_rows.shape[0]
    query_cols = HQ * HD
    kv_cols = HK * HD
    cols = (query_cols + 2 * kv_cols) // groups
    copy = jnp.concatenate([qkv_rows.astype(jnp.bfloat16), o_rows.astype(jnp.bfloat16)], axis=1)
    copy = by_group(copy, (query_cols, kv_cols, kv_cols, query_cols), groups)

    cos, sin = turns(lengths)
    parts = shuffle(hidden.reshape(steps * rows, width), block_owner)
    parts = [parts[0]] + [z_shift(parts[k], k) for k in range(1, NZ)]

    both = flatten(lax.all_to_all(copy, "tp", split_axis=1, concat_axis=0, tiled=True))
    both, cos, sin, parts[1], parts[3] = lax.optimization_barrier(
        (both, cos, sin, parts[1], parts[3])
    )
    w, own = both[:, :cols], both[:, cols:]
    half = own.shape[0] // 2

    w_y, w_c = flip(w, 8), flip(w, 1)
    own, parts[2] = lax.optimization_barrier((own, parts[2]))
    below, above = z_shift(own, 1), z_shift(own, -1)
    begun = partials(parts, (w, w_c))
    w_y, below, above, own, *begun = lax.optimization_barrier((w_y, below, above, own, *begun))
    w_yc = flip(w_y, 1)
    far_a, far_b = z_shift(above[:half], -1), z_shift(below[half:], 1)
    across = flip(own, 8)

    sums = partials(parts, (w_y, w_yc), begun)
    sums = [sums[0]] + [z_shift(sums[k], -k) for k in range(1, NZ)]
    far_a, far_b, across = after((far_a, far_b, across))
    across_far_a, across_far_b = flip(far_a, 8), flip(far_b, 8)
    (across,) = after((across,), *sums)
    across_below, across_above = z_shift(across, 1), z_shift(across, -1)
    mixed = attention(sums, cos, sin, cache, lengths)

    mixed_c = flip(mixed, 1)
    sources = (own, below, above, across, far_a, far_b)
    sources += (across_far_a, across_far_b, across_below, across_above)
    theirs = terms_of(mixed_c, sources)
    mine = terms_of(*after((mixed,), theirs), sources)
    pieces = (mine, flip(theirs, 1))
    places = ((0, 0, 0), (0, 3, 0), (0, 1, 0), (1, 0, 0), (0, 2, 0), (0, 2, 4))
    places += ((1, 2, 0), (1, 2, 4), (1, 3, 0), (1, 1, 0))
    spots = []
    for core in range(2):
        begin = 0
        for (dy, dz, t0), source in zip(places, sources):
            size = source.shape[0]
            spots.append((core, dy, dz, core, t0, size // owned, begin))
            begin += size
    slabs = place(pieces, tuple(spots), block_owner, groups, rows)

    first = [slabs[0]] + [x_shift(slabs[k], k) for k in range(1, NX)]
    second = [slabs[NX], y_flip(slabs[NX + 1])]
    first = sum(value.astype(jnp.float32) for value in first)
    second = sum(value.astype(jnp.float32) for value in second)
    first = first[0] + y_flip(first[1].astype(jnp.bfloat16)).astype(jnp.float32)
    second = [second[0]] + [x_shift(second[k].astype(jnp.bfloat16), k) for k in range(1, NX)]
    second = sum(value.astype(jnp.float32) for value in second)
    return jnp.stack([first, second]).astype(jnp.bfloat16)


def solution(mesh):
    in_specs = (
        P(None, "fsdp", None),
        P(("fsdp", "tp"), None),
        P(("fsdp", "tp"), None),
        P(),
        P(None, "fsdp", None, "tp"),
        P("fsdp"),
    )
    out_specs = P(None, "fsdp", "tp")
    return jax.shard_map(body, mesh=mesh, in_specs=in_specs, out_specs=out_specs, check_vma=False)
```

```python
import functools
import math

import jax
import jax.numpy as jnp
from jax import lax
from jax.experimental import pallas as pl
from jax.experimental.pallas import tpu as pltpu
from jax.sharding import PartitionSpec as P

HQ = 64
HK = 8
HD = 128
NZ = 4
NX = 4
GROUP = 8
CHUNK = 256
MIB = 1024 * 1024


def z_shift(value, k):
    pairs = [(f, (f // 8) * 8 + ((f // 2 + k) % NZ) * 2 + f % 2) for f in range(16)]
    return lax.ppermute(value, "fsdp", pairs)


def flip(value, bit):
    return lax.ppermute(value, "fsdp", [(f, f ^ bit) for f in range(16)])


def x_shift(value, k):
    return lax.ppermute(value, "tp", [(t, (t // 2 + k) % NX * 2 + t % 2) for t in range(2 * NX)])


def y_flip(value):
    return lax.ppermute(value, "tp", [(t, t ^ 1) for t in range(2 * NX)])


def by_group(array, sections, groups):
    pieces = []
    begin = 0
    for width in sections:
        pieces.append(
            array[:, begin : begin + width].reshape(array.shape[0], groups, width // groups)
        )
        begin = begin + width
    return jnp.concatenate(pieces, axis=2)


def flatten(received):
    return received.reshape(received.shape[0], received.shape[2])


def shuffle_kernel(owner_ref, hidden_ref, *out_refs):
    f = lax.axis_index("fsdp")
    y_lo, z, core = f // 8, lax.rem(f // 2, 4), lax.rem(f, 2)
    rows = hidden_ref.shape[0]
    low = lax.broadcasted_iota(jnp.int32, (rows, 128), 1) < 64

    for k, out_ref in enumerate(out_refs):
        zz = lax.rem(z + k, 4)

        def step(n, carry, zz=zz, out_ref=out_ref):
            q, p = n // 4, lax.rem(n, 4)
            yy = lax.rem(y_lo + q // 2, 2)
            cc = lax.rem(core + lax.rem(q, 2), 2)
            i = yy * 64 + zz * 16 + cc * 8 + 2 * p
            s0, s1 = owner_ref[0, i], owner_ref[0, i + 1]
            a = hidden_ref[:, pl.ds(pl.multiple_of((s0 // 2) * 128, 128), 128)].astype(jnp.float32)
            b = hidden_ref[:, pl.ds(pl.multiple_of((s1 // 2) * 128, 128), 128)].astype(jnp.float32)
            a = pltpu.roll(a, 64 * lax.rem(s0, 2), 1)
            b = pltpu.roll(b, 64 * (1 - lax.rem(s1, 2)), 1)
            out_ref[:, pl.ds(pl.multiple_of(n * 128, 128), 128)] = jnp.where(low, a, b).astype(
                jnp.bfloat16
            )
            return carry

        lax.fori_loop(0, 16, step, 0, unroll=4)


def shuffle(hidden, block_owner):
    rows, width = hidden.shape
    part = jax.ShapeDtypeStruct((rows, width // NZ), jnp.bfloat16)
    return pl.pallas_call(
        shuffle_kernel,
        out_shape=[part] * NZ,
        in_specs=[
            pl.BlockSpec(memory_space=pltpu.SMEM),
            pl.BlockSpec(memory_space=pltpu.VMEM),
        ],
        out_specs=[pl.BlockSpec(memory_space=pltpu.VMEM)] * NZ,
        compiler_params=pltpu.CompilerParams(vmem_limit_bytes=14 * MIB),
        cost_estimate=pl.CostEstimate(
            flops=rows * width * 8, bytes_accessed=4 * rows * width, transcendentals=0
        ),
        name="shuffle",
    )(block_owner, hidden)


def partial_kernel(begun, *refs):
    held, weights = refs[:NZ], refs[NZ : NZ + 2]
    totals = refs[NZ + 2 : 2 * NZ + 2] if begun else ()
    *outs, stacked = refs[NZ + 2 + len(totals) :]
    rows = held[0].shape[0]
    depth = weights[0].shape[0]

    @pl.when(pl.program_id(0) == 0)
    def _():
        for k, h in enumerate(held):
            stacked[pl.ds(k * rows, rows), :] = h[...]

    total = jnp.dot(stacked[:, :depth], weights[0][...], preferred_element_type=jnp.float32)
    total = total + jnp.dot(
        stacked[:, depth:], weights[1][...], preferred_element_type=jnp.float32
    )
    for k, out in enumerate(outs):
        part = total[k * rows : (k + 1) * rows]
        if begun:
            part = part + totals[k][...]
        out[...] = part.astype(out.dtype)


def partials(parts, weights, totals=()):
    rows, width = parts[0].shape
    depth, cols = weights[0].shape
    tile = 256
    begun = len(totals) > 0
    place = 1 if begun else 0
    block = pl.BlockSpec((rows, tile), lambda j: (0, j))
    types = [jnp.float32] + [jnp.bfloat16 if begun else jnp.float32] * (NZ - 1)
    return pl.pallas_call(
        functools.partial(partial_kernel, begun),
        grid=(cols // tile,),
        out_shape=[jax.ShapeDtypeStruct((rows, cols), kind) for kind in types],
        in_specs=[pl.BlockSpec((rows, width // 2), lambda j: (0, place))] * NZ
        + [pl.BlockSpec((depth, tile), lambda j: (0, j))] * 2
        + [block] * len(totals),
        out_specs=[block] * NZ,
        scratch_shapes=[pltpu.VMEM((NZ * rows, width // 2), jnp.bfloat16)],
        compiler_params=pltpu.CompilerParams(vmem_limit_bytes=14 * MIB),
        cost_estimate=pl.CostEstimate(
            flops=NZ * rows * width * cols,
            bytes_accessed=NZ * rows * width + width * cols + 4 * NZ * rows * cols,
            transcendentals=0,
        ),
        name="partials_rest" if begun else "partials",
    )(*parts, *weights, *totals)


def terms_kernel(mixed_ref, *refs):
    *sources, out_ref = refs
    spare = out_ref.shape[1] - mixed_ref.shape[0]
    wide = jnp.pad(mixed_ref[...].astype(jnp.float32), ((0, spare), (0, 0)))
    turned = wide.T.astype(jnp.bfloat16)
    begin = 0
    for source in sources:

        def multiply(n, carry, source=source, begin=begin):
            rows = source[pl.ds(pl.multiple_of(n * CHUNK, CHUNK), CHUNK), :]
            to = pl.ds(pl.multiple_of(begin + n * CHUNK, CHUNK), CHUNK)
            out_ref[to, :] = jnp.dot(rows, turned, preferred_element_type=jnp.float32).astype(
                out_ref.dtype
            )
            return carry

        lax.fori_loop(0, source.shape[0] // CHUNK, multiply, 0)
        begin += source.shape[0]


def terms_of(mixed, sources):
    rows, depth = mixed.shape
    width = sum(source.shape[0] for source in sources)
    lanes = -(-rows // 128) * 128
    vmem = pl.BlockSpec(memory_space=pltpu.VMEM)
    return pl.pallas_call(
        terms_kernel,
        out_shape=jax.ShapeDtypeStruct((width, lanes), jnp.bfloat16),
        in_specs=[vmem] * (1 + len(sources)),
        out_specs=vmem,
        compiler_params=pltpu.CompilerParams(vmem_limit_bytes=20 * MIB),
        cost_estimate=pl.CostEstimate(
            flops=2 * rows * depth * width,
            bytes_accessed=2 * (rows * depth + depth * width + rows * width),
            transcendentals=0,
        ),
        name="terms",
    )(mixed, *sources)


def place_kernel(spots, groups, owner_ref, *refs):
    pieces, firsts, seconds = refs[:-7], refs[-7:-3], refs[-3:-1]
    placed = refs[-1]
    f = lax.axis_index("fsdp")
    y_lo, z, core = f // 8, lax.rem(f // 2, NZ), lax.rem(f, 2)
    width = placed.shape[0]
    owned = width // owner_ref.shape[1]
    for n, dy, dz, dc, t0, blocks, begin in spots:
        first = (
            lax.rem(y_lo + dy, 2) * 64 + lax.rem(z + dz, NZ) * 16 + lax.rem(core + dc, 2) * 8 + t0
        )

        def put(b, carry, n=n, first=first, begin=begin):
            goal = pl.multiple_of(owner_ref[1, first + b] * owned, owned)
            start = pl.multiple_of(begin + b * owned, owned)
            placed[pl.ds(goal, owned), :] = pieces[n][pl.ds(start, owned), :]
            return carry

        lax.fori_loop(0, blocks, put, 0)
    slab = width // groups
    t = lax.axis_index("tp")
    for k in range(NX):
        for j in range(2):
            at = lax.rem(t // 2 + k, NX) * 2 + lax.rem(lax.rem(t, 2) + j, 2)
            turned = placed[pl.ds(pl.multiple_of(at * slab, slab), slab), :].T
            rows = firsts[k].shape[1]
            firsts[k][j] = turned[:rows]
            seconds[j][k] = turned[rows : 2 * rows]


def place(pieces, spots, block_owner, groups, rows):
    width = sum(piece.shape[0] for piece in pieces)
    lanes = pieces[0].shape[1]
    vmem = pl.BlockSpec(memory_space=pltpu.VMEM)
    return pl.pallas_call(
        functools.partial(place_kernel, spots, groups),
        out_shape=[jax.ShapeDtypeStruct((2, rows, width // groups), jnp.bfloat16)] * NX
        + [jax.ShapeDtypeStruct((NX, rows, width // groups), jnp.bfloat16)] * 2,
        in_specs=[pl.BlockSpec(memory_space=pltpu.SMEM)] + [vmem] * len(pieces),
        out_specs=[vmem] * (NX + 2),
        scratch_shapes=[pltpu.VMEM((width, lanes), jnp.bfloat16)],
        compiler_params=pltpu.CompilerParams(vmem_limit_bytes=20 * MIB),
        cost_estimate=pl.CostEstimate(
            flops=0, bytes_accessed=8 * rows * width, transcendentals=0
        ),
        name="place",
    )(block_owner, *pieces)


def turns(lengths):
    half = HD // 2
    position = (lengths[None, :] + jnp.arange(2, dtype=jnp.int32)[:, None]).reshape(-1)
    freq = 1000000.0 ** (-jnp.arange(half, dtype=jnp.float32) * 2.0 / HD)
    angle = position.astype(jnp.float32)[:, None] * freq
    cosine, sine = jnp.cos(angle), jnp.sin(angle)
    return jnp.concatenate([cosine, cosine], axis=1), jnp.concatenate([-sine, sine], axis=1)


def attention_kernel(
    lengths_ref, p0, p1, p2, p3, cos_ref, sin_ref, cache_ref, out_ref, query, keys, values, result
):
    step = pl.program_id(0)
    both = p0.shape[0]
    rows = both // 2
    heads = out_ref.shape[1] // HD
    lanes = 2 * heads
    span = GROUP * lanes

    @pl.when(step == 0)
    def _():
        cosine, sine = cos_ref[...], sin_ref[...]

        def part(begin):
            cut = slice(begin * HD, (begin + 1) * HD)
            total = p0[:, cut] + p1[:, cut].astype(jnp.float32)
            return total + p2[:, cut].astype(jnp.float32) + p3[:, cut].astype(jnp.float32)

        def turn(x):
            return x * cosine + pltpu.roll(x, HD // 2, 1) * sine

        for h in range(heads):
            turned = turn(part(h))
            for s in range(2):
                query[pl.ds(s * heads + h, rows, stride=lanes), :] = turned[
                    s * rows : (s + 1) * rows
                ]
        new_keys, new_values = turn(part(heads)), part(heads + 1)
        for g in range(rows // GROUP):
            for t in range(2):
                to = slice((2 * g + t) * GROUP, (2 * g + t + 1) * GROUP)
                begin = t * rows + g * GROUP
                keys[to] = new_keys[begin : begin + GROUP]
                values[to] = new_values[begin : begin + GROUP]

    factor = 1.0 / math.sqrt(HD)
    nt = (((1,), (1,)), ((), ()))
    at = pl.ds(pl.multiple_of(step * span, span), span)
    fresh_at = pl.ds(pl.multiple_of(step * 2 * GROUP, 2 * GROUP), 2 * GROUP)
    q = query[at, :].astype(jnp.bfloat16)
    fresh = (
        lax.dot_general(
            q, keys[fresh_at, :].astype(jnp.bfloat16), nt, preferred_element_type=jnp.float32
        )
        * factor
    )
    of = lax.broadcasted_iota(jnp.int32, fresh.shape, 0)
    new = lax.broadcasted_iota(jnp.int32, fresh.shape, 1)
    seen = (of // lanes == new % GROUP) & (new // GROUP <= (of // heads) % 2)
    fresh = jnp.where(seen, fresh, -jnp.inf)

    held = cache_ref.shape[2]
    place = lax.broadcasted_iota(jnp.int32, (lanes, held), 1)
    pieces = []
    for r in range(GROUP):
        score = lax.dot_general(
            q[r * lanes : (r + 1) * lanes], cache_ref[0, r], nt, preferred_element_type=jnp.float32
        )
        pieces.append(jnp.where(place < lengths_ref[step * GROUP + r], score * factor, -jnp.inf))
    old = jnp.concatenate(pieces, axis=0)
    top = jnp.maximum(
        jnp.max(old, axis=1, keepdims=True), jnp.max(fresh, axis=1, keepdims=True)
    )
    old_w = jnp.exp(old - top)
    fresh_w = jnp.exp(fresh - top)
    total = jnp.sum(old_w, axis=1, keepdims=True) + jnp.sum(fresh_w, axis=1, keepdims=True)
    scale = 1.0 / total
    old_p = (old_w * scale).astype(jnp.bfloat16)
    fresh_p = (fresh_w * scale).astype(jnp.bfloat16)
    mixed = jnp.concatenate(
        [
            jnp.dot(
                old_p[r * lanes : (r + 1) * lanes],
                cache_ref[1, r],
                preferred_element_type=jnp.float32,
            )
            for r in range(GROUP)
        ],
        axis=0,
    )
    mixed = mixed + jnp.dot(
        fresh_p, values[fresh_at, :].astype(jnp.bfloat16), preferred_element_type=jnp.float32
    )
    result[at, :] = mixed

    @pl.when(step == pl.num_programs(0) - 1)
    def _():
        for h in range(heads):
            for s in range(2):
                out_ref[s * rows : (s + 1) * rows, h * HD : (h + 1) * HD] = result[
                    pl.ds(s * heads + h, rows, stride=lanes), :
                ].astype(out_ref.dtype)


def attention(sums, cos, sin, cache, lengths):
    both, cols = sums[0].shape
    rows = both // 2
    width = cols - 2 * HD
    held = cache.shape[2]
    lanes = 2 * width // HD

    def whole(*shape):
        return pl.BlockSpec(shape, lambda g: (0,) * len(shape))

    return pl.pallas_call(
        attention_kernel,
        grid=(rows // GROUP,),
        out_shape=jax.ShapeDtypeStruct((both, width), jnp.bfloat16),
        in_specs=[pl.BlockSpec(memory_space=pltpu.SMEM)]
        + [whole(both, cols)] * NZ
        + [whole(both, HD)] * 2
        + [pl.BlockSpec((2, GROUP, held, HD), lambda g: (0, g, 0, 0))],
        out_specs=whole(both, width),
        scratch_shapes=[
            pltpu.VMEM((rows * lanes, HD), jnp.float32),
            pltpu.VMEM((both, HD), jnp.float32),
            pltpu.VMEM((both, HD), jnp.float32),
            pltpu.VMEM((rows * lanes, HD), jnp.float32),
        ],
        compiler_params=pltpu.CompilerParams(vmem_limit_bytes=48 * MIB),
        cost_estimate=pl.CostEstimate(
            flops=4 * rows * lanes * held * HD,
            bytes_accessed=16 * rows * held * HD,
            transcendentals=rows * lanes * held,
        ),
        name="attention",
    )(lengths, *sums, cos, sin, cache)


def after(values, *first):
    return lax.optimization_barrier((*values, *first))[: len(values)]


def body(hidden, qkv_rows, o_rows, block_owner, cache, lengths):
    groups = lax.axis_size("tp")
    steps, rows, width = hidden.shape
    owned = qkv_rows.shape[0]
    query_cols = HQ * HD
    kv_cols = HK * HD
    qkv_copy = by_group(qkv_rows.astype(jnp.bfloat16), (query_cols, kv_cols, kv_cols), groups)
    out_copy = o_rows.astype(jnp.bfloat16).reshape(owned, groups, query_cols // groups)

    cos, sin = turns(lengths)
    parts = shuffle(hidden.reshape(steps * rows, width), block_owner)
    parts = [parts[0]] + [z_shift(parts[k], k) for k in range(1, NZ)]

    w = flatten(lax.all_to_all(qkv_copy, "tp", split_axis=1, concat_axis=0, tiled=True))
    w_y, w_c = flip(w, 8), flip(w, 1)
    out_copy, parts[1], parts[3], cos, sin = after(
        (out_copy, parts[1], parts[3], cos, sin), w
    )
    own = flatten(lax.all_to_all(out_copy, "tp", split_axis=1, concat_axis=0, tiled=True))
    half = own.shape[0] // 2
    own, parts[2], w_c = lax.optimization_barrier((own, parts[2], w_c))
    below, above = z_shift(own, 1), z_shift(own, -1)
    begun = partials(parts, (w, w_c))
    w_y, below, above, own, *begun = lax.optimization_barrier((w_y, below, above, own, *begun))
    w_yc = flip(w_y, 1)
    far_a, far_b = z_shift(above[:half], -1), z_shift(below[half:], 1)
    across = flip(own, 8)

    sums = partials(parts, (w_y, w_yc), begun)
    sums = [sums[0]] + [z_shift(sums[k], -k) for k in range(1, NZ)]
    far_a, far_b, across = after((far_a, far_b, across))
    across_far_a, across_far_b = flip(far_a, 8), flip(far_b, 8)
    (across,) = after((across,), *sums)
    across_below, across_above = z_shift(across, 1), z_shift(across, -1)
    mixed = attention(sums, cos, sin, cache, lengths)

    mixed_c = flip(mixed, 1)
    sources = (own, below, above, across, far_a, far_b)
    sources += (across_far_a, across_far_b, across_below, across_above)
    theirs = terms_of(mixed_c, sources)
    mine = terms_of(*after((mixed,), theirs), sources)
    pieces = (mine, flip(theirs, 1))
    places = ((0, 0, 0), (0, 3, 0), (0, 1, 0), (1, 0, 0), (0, 2, 0), (0, 2, 4))
    places += ((1, 2, 0), (1, 2, 4), (1, 3, 0), (1, 1, 0))
    spots = []
    for core in range(2):
        begin = 0
        for (dy, dz, t0), source in zip(places, sources):
            size = source.shape[0]
            spots.append((core, dy, dz, core, t0, size // owned, begin))
            begin += size
    slabs = place(pieces, tuple(spots), block_owner, groups, rows)

    first = [slabs[0]] + [x_shift(slabs[k], k) for k in range(1, NX)]
    second = [slabs[NX], y_flip(slabs[NX + 1])]
    first = sum(value.astype(jnp.float32) for value in first)
    second = sum(value.astype(jnp.float32) for value in second)
    first = first[0] + y_flip(first[1].astype(jnp.bfloat16)).astype(jnp.float32)
    second = [second[0]] + [x_shift(second[k].astype(jnp.bfloat16), k) for k in range(1, NX)]
    second = sum(value.astype(jnp.float32) for value in second)
    return jnp.stack([first, second]).astype(jnp.bfloat16)


def solution(mesh):
    in_specs = (
        P(None, "fsdp", None),
        P(("fsdp", "tp"), None),
        P(("fsdp", "tp"), None),
        P(),
        P(None, "fsdp", None, "tp"),
        P("fsdp"),
    )
    out_specs = P(None, "fsdp", "tp")
    return jax.shard_map(body, mesh=mesh, in_specs=in_specs, out_specs=out_specs, check_vma=False)
```

```python
import functools
import math

import jax
import jax.numpy as jnp
from jax import lax
from jax.experimental import pallas as pl
from jax.experimental.pallas import tpu as pltpu
from jax.sharding import PartitionSpec as P

HQ = 64
HK = 8
HD = 128
NZ = 4
NX = 4
GROUP = 8
CHUNK = 512
MIB = 1024 * 1024


def z_shift(value, k):
    pairs = [(f, (f // 8) * 8 + ((f // 2 + k) % NZ) * 2 + f % 2) for f in range(16)]
    return lax.ppermute(value, "fsdp", pairs)


def flip(value, bit):
    return lax.ppermute(value, "fsdp", [(f, f ^ bit) for f in range(16)])


def x_shift(value, k):
    return lax.ppermute(value, "tp", [(t, (t // 2 + k) % NX * 2 + t % 2) for t in range(2 * NX)])


def y_flip(value):
    return lax.ppermute(value, "tp", [(t, t ^ 1) for t in range(2 * NX)])


def slabs_kernel(query, key, value, back, out_ref):
    begin = 0
    for ref in (query, key, value, back):
        width = ref.shape[1] // out_ref.shape[0]
        for g in range(out_ref.shape[0]):
            part = ref[:, g * width : (g + 1) * width]
            out_ref[g, :, begin : begin + width] = part.astype(out_ref.dtype)
        begin += width


def slabs_of(qkv_rows, o_rows, groups):
    owned = qkv_rows.shape[0]
    query_cols = HQ * HD
    each = 2
    wide, narrow = each * query_cols // groups, each * HK * HD // groups
    keys_at = query_cols // narrow
    values_at = keys_at + HK * HD // narrow
    cols = (2 * wide + 2 * narrow) // each
    return pl.pallas_call(
        slabs_kernel,
        grid=(groups // each,),
        out_shape=jax.ShapeDtypeStruct((groups, owned, cols), jnp.bfloat16),
        in_specs=[
            pl.BlockSpec((owned, wide), lambda g: (0, g)),
            pl.BlockSpec((owned, narrow), lambda g: (0, keys_at + g)),
            pl.BlockSpec((owned, narrow), lambda g: (0, values_at + g)),
            pl.BlockSpec((owned, wide), lambda g: (0, g)),
        ],
        out_specs=pl.BlockSpec((each, owned, cols), lambda g: (g, 0, 0)),
        compiler_params=pltpu.CompilerParams(vmem_limit_bytes=60 * MIB),
        cost_estimate=pl.CostEstimate(
            flops=0, bytes_accessed=6 * groups * owned * cols, transcendentals=0
        ),
        name="slabs",
    )(qkv_rows, qkv_rows, qkv_rows, o_rows)


def shuffle_kernel(owner_ref, hidden_ref, *out_refs):
    f = lax.axis_index("fsdp")
    y_lo, z, core = f // 8, lax.rem(f // 2, 4), lax.rem(f, 2)
    rows = hidden_ref.shape[0]
    low = lax.broadcasted_iota(jnp.int32, (rows, 128), 1) < 64

    for k, out_ref in enumerate(out_refs):
        zz = lax.rem(z + k, 4)

        def step(n, carry, zz=zz, out_ref=out_ref):
            q, p = n // 4, lax.rem(n, 4)
            yy = lax.rem(y_lo + q // 2, 2)
            cc = lax.rem(core + lax.rem(q, 2), 2)
            i = yy * 64 + zz * 16 + cc * 8 + 2 * p
            s0, s1 = owner_ref[0, i], owner_ref[0, i + 1]
            a = hidden_ref[:, pl.ds(pl.multiple_of((s0 // 2) * 128, 128), 128)].astype(jnp.float32)
            b = hidden_ref[:, pl.ds(pl.multiple_of((s1 // 2) * 128, 128), 128)].astype(jnp.float32)
            a = pltpu.roll(a, 64 * lax.rem(s0, 2), 1)
            b = pltpu.roll(b, 64 * (1 - lax.rem(s1, 2)), 1)
            out_ref[:, pl.ds(pl.multiple_of(n * 128, 128), 128)] = jnp.where(low, a, b).astype(
                jnp.bfloat16
            )
            return carry

        lax.fori_loop(0, 16, step, 0, unroll=8)


def shuffle(hidden, block_owner):
    rows, width = hidden.shape
    part = jax.ShapeDtypeStruct((rows, width // NZ), jnp.bfloat16)
    return pl.pallas_call(
        shuffle_kernel,
        out_shape=[part] * NZ,
        in_specs=[
            pl.BlockSpec(memory_space=pltpu.SMEM),
            pl.BlockSpec(memory_space=pltpu.VMEM),
        ],
        out_specs=[pl.BlockSpec(memory_space=pltpu.VMEM)] * NZ,
        compiler_params=pltpu.CompilerParams(vmem_limit_bytes=14 * MIB),
        cost_estimate=pl.CostEstimate(
            flops=rows * width * 8, bytes_accessed=4 * rows * width, transcendentals=0
        ),
        name="shuffle",
    )(block_owner, hidden)


def partial_kernel(begun, *refs):
    held, weights = refs[:NZ], refs[NZ : NZ + 2]
    totals = refs[NZ + 2 : 2 * NZ + 2] if begun else ()
    *outs, stacked = refs[NZ + 2 + len(totals) :]
    rows = held[0].shape[0]
    depth = weights[0].shape[0]

    @pl.when(pl.program_id(0) == 0)
    def _():
        for k, h in enumerate(held):
            stacked[pl.ds(k * rows, rows), :] = h[...]

    total = jnp.dot(stacked[:, :depth], weights[0][...], preferred_element_type=jnp.float32)
    total = total + jnp.dot(
        stacked[:, depth:], weights[1][...], preferred_element_type=jnp.float32
    )
    for k, out in enumerate(outs):
        part = total[k * rows : (k + 1) * rows]
        if begun:
            part = part + totals[k][...]
        out[...] = part.astype(out.dtype)


def partials(parts, weights, totals=()):
    rows, width = parts[0].shape
    depth, cols = weights[0].shape
    tile = 256
    begun = len(totals) > 0
    place = 1 if begun else 0
    block = pl.BlockSpec((rows, tile), lambda j: (0, j))
    types = [jnp.float32] + [jnp.bfloat16 if begun else jnp.float32] * (NZ - 1)
    return pl.pallas_call(
        functools.partial(partial_kernel, begun),
        grid=(cols // tile,),
        out_shape=[jax.ShapeDtypeStruct((rows, cols), kind) for kind in types],
        in_specs=[pl.BlockSpec((rows, width // 2), lambda j: (0, place))] * NZ
        + [pl.BlockSpec((depth, tile), lambda j: (0, j))] * 2
        + [block] * len(totals),
        out_specs=[block] * NZ,
        scratch_shapes=[pltpu.VMEM((NZ * rows, width // 2), jnp.bfloat16)],
        compiler_params=pltpu.CompilerParams(vmem_limit_bytes=14 * MIB),
        cost_estimate=pl.CostEstimate(
            flops=NZ * rows * width * cols,
            bytes_accessed=NZ * rows * width + width * cols + 4 * NZ * rows * cols,
            transcendentals=0,
        ),
        name="partials_rest" if begun else "partials",
    )(*parts, *weights, *totals)


def terms_kernel(mixed_ref, *refs):
    *sources, out_ref = refs
    spare = out_ref.shape[1] - mixed_ref.shape[0]
    wide = jnp.pad(mixed_ref[...].astype(jnp.float32), ((0, spare), (0, 0)))
    turned = wide.T.astype(jnp.bfloat16)
    begin = 0
    for source in sources:
        size = source.shape[0]
        chunk = min(CHUNK, size)

        def multiply(n, carry, source=source, begin=begin, chunk=chunk):
            rows = source[pl.ds(pl.multiple_of(n * chunk, chunk), chunk), :]
            to = pl.ds(pl.multiple_of(begin + n * chunk, chunk), chunk)
            out_ref[to, :] = jnp.dot(rows, turned, preferred_element_type=jnp.float32).astype(
                out_ref.dtype
            )
            return carry

        lax.fori_loop(0, size // chunk, multiply, 0)
        begin += size


def terms_of(mixed, sources):
    rows, depth = mixed.shape
    width = sum(source.shape[0] for source in sources)
    lanes = -(-rows // 128) * 128
    vmem = pl.BlockSpec(memory_space=pltpu.VMEM)
    return pl.pallas_call(
        terms_kernel,
        out_shape=jax.ShapeDtypeStruct((width, lanes), jnp.bfloat16),
        in_specs=[vmem] * (1 + len(sources)),
        out_specs=vmem,
        compiler_params=pltpu.CompilerParams(vmem_limit_bytes=20 * MIB),
        cost_estimate=pl.CostEstimate(
            flops=2 * rows * depth * width,
            bytes_accessed=2 * (rows * depth + depth * width + rows * width),
            transcendentals=0,
        ),
        name="terms",
    )(mixed, *sources)


def place_kernel(spots, groups, owner_ref, *refs):
    pieces, firsts, seconds = refs[:-7], refs[-7:-3], refs[-3:-1]
    placed = refs[-1]
    f = lax.axis_index("fsdp")
    y_lo, z, core = f // 8, lax.rem(f // 2, NZ), lax.rem(f, 2)
    width = placed.shape[0]
    owned = width // owner_ref.shape[1]
    for n, dy, dz, dc, t0, blocks, begin in spots:
        first = (
            lax.rem(y_lo + dy, 2) * 64 + lax.rem(z + dz, NZ) * 16 + lax.rem(core + dc, 2) * 8 + t0
        )

        def put(b, carry, n=n, first=first, begin=begin):
            goal = pl.multiple_of(owner_ref[1, first + b] * owned, owned)
            start = pl.multiple_of(begin + b * owned, owned)
            placed[pl.ds(goal, owned), :] = pieces[n][pl.ds(start, owned), :]
            return carry

        lax.fori_loop(0, blocks, put, 0)
    slab = width // groups
    t = lax.axis_index("tp")
    for k in range(NX):
        for j in range(2):
            at = lax.rem(t // 2 + k, NX) * 2 + lax.rem(lax.rem(t, 2) + j, 2)
            turned = placed[pl.ds(pl.multiple_of(at * slab, slab), slab), :].T
            rows = firsts[k].shape[1]
            firsts[k][j] = turned[:rows]
            seconds[j][k] = turned[rows : 2 * rows]


def place(pieces, spots, block_owner, groups, rows):
    width = sum(piece.shape[0] for piece in pieces)
    lanes = pieces[0].shape[1]
    vmem = pl.BlockSpec(memory_space=pltpu.VMEM)
    return pl.pallas_call(
        functools.partial(place_kernel, spots, groups),
        out_shape=[jax.ShapeDtypeStruct((2, rows, width // groups), jnp.bfloat16)] * NX
        + [jax.ShapeDtypeStruct((NX, rows, width // groups), jnp.bfloat16)] * 2,
        in_specs=[pl.BlockSpec(memory_space=pltpu.SMEM)] + [vmem] * len(pieces),
        out_specs=[vmem] * (NX + 2),
        scratch_shapes=[pltpu.VMEM((width, lanes), jnp.bfloat16)],
        compiler_params=pltpu.CompilerParams(vmem_limit_bytes=20 * MIB),
        cost_estimate=pl.CostEstimate(
            flops=0, bytes_accessed=8 * rows * width, transcendentals=0
        ),
        name="place",
    )(block_owner, *pieces)


def turns(lengths):
    half = HD // 2
    position = (lengths[None, :] + jnp.arange(2, dtype=jnp.int32)[:, None]).reshape(-1)
    freq = 1000000.0 ** (-jnp.arange(half, dtype=jnp.float32) * 2.0 / HD)
    angle = position.astype(jnp.float32)[:, None] * freq
    cosine, sine = jnp.cos(angle), jnp.sin(angle)
    return jnp.concatenate([cosine, cosine], axis=1), jnp.concatenate([-sine, sine], axis=1)


def attention_kernel(
    lengths_ref, p0, p1, p2, p3, cos_ref, sin_ref, cache_ref, out_ref, query, keys, values, result
):
    step = pl.program_id(0)
    both = p0.shape[0]
    rows = both // 2
    heads = out_ref.shape[1] // HD
    lanes = 2 * heads
    span = GROUP * lanes

    @pl.when(step == 0)
    def _():
        cosine, sine = cos_ref[...], sin_ref[...]

        def part(begin):
            cut = slice(begin * HD, (begin + 1) * HD)
            total = p0[:, cut] + p1[:, cut].astype(jnp.float32)
            return total + p2[:, cut].astype(jnp.float32) + p3[:, cut].astype(jnp.float32)

        def turn(x):
            return x * cosine + pltpu.roll(x, HD // 2, 1) * sine

        for h in range(heads):
            turned = turn(part(h))
            for s in range(2):
                query[pl.ds(s * heads + h, rows, stride=lanes), :] = turned[
                    s * rows : (s + 1) * rows
                ]
        new_keys, new_values = turn(part(heads)), part(heads + 1)
        for g in range(rows // GROUP):
            for t in range(2):
                to = slice((2 * g + t) * GROUP, (2 * g + t + 1) * GROUP)
                begin = t * rows + g * GROUP
                keys[to] = new_keys[begin : begin + GROUP]
                values[to] = new_values[begin : begin + GROUP]

    factor = 1.0 / math.sqrt(HD)
    nt = (((1,), (1,)), ((), ()))
    at = pl.ds(pl.multiple_of(step * span, span), span)
    fresh_at = pl.ds(pl.multiple_of(step * 2 * GROUP, 2 * GROUP), 2 * GROUP)
    q = query[at, :].astype(jnp.bfloat16)
    fresh = (
        lax.dot_general(
            q, keys[fresh_at, :].astype(jnp.bfloat16), nt, preferred_element_type=jnp.float32
        )
        * factor
    )
    of = lax.broadcasted_iota(jnp.int32, fresh.shape, 0)
    new = lax.broadcasted_iota(jnp.int32, fresh.shape, 1)
    seen = (of // lanes == new % GROUP) & (new // GROUP <= (of // heads) % 2)
    fresh = jnp.where(seen, fresh, -jnp.inf)

    held = cache_ref.shape[2]
    place = lax.broadcasted_iota(jnp.int32, (lanes, held), 1)
    pieces = []
    for r in range(GROUP):
        score = lax.dot_general(
            q[r * lanes : (r + 1) * lanes], cache_ref[0, r], nt, preferred_element_type=jnp.float32
        )
        pieces.append(jnp.where(place < lengths_ref[step * GROUP + r], score * factor, -jnp.inf))
    old = jnp.concatenate(pieces, axis=0)
    top = jnp.maximum(
        jnp.max(old, axis=1, keepdims=True), jnp.max(fresh, axis=1, keepdims=True)
    )
    old_w = jnp.exp(old - top)
    fresh_w = jnp.exp(fresh - top)
    total = jnp.sum(old_w, axis=1, keepdims=True) + jnp.sum(fresh_w, axis=1, keepdims=True)
    scale = 1.0 / total
    old_p = (old_w * scale).astype(jnp.bfloat16)
    fresh_p = (fresh_w * scale).astype(jnp.bfloat16)
    mixed = jnp.concatenate(
        [
            jnp.dot(
                old_p[r * lanes : (r + 1) * lanes],
                cache_ref[1, r],
                preferred_element_type=jnp.float32,
            )
            for r in range(GROUP)
        ],
        axis=0,
    )
    mixed = mixed + jnp.dot(
        fresh_p, values[fresh_at, :].astype(jnp.bfloat16), preferred_element_type=jnp.float32
    )
    result[at, :] = mixed

    @pl.when(step == pl.num_programs(0) - 1)
    def _():
        for h in range(heads):
            for s in range(2):
                out_ref[s * rows : (s + 1) * rows, h * HD : (h + 1) * HD] = result[
                    pl.ds(s * heads + h, rows, stride=lanes), :
                ].astype(out_ref.dtype)


def attention(sums, cos, sin, cache, lengths):
    both, cols = sums[0].shape
    rows = both // 2
    width = cols - 2 * HD
    held = cache.shape[2]
    lanes = 2 * width // HD

    def whole(*shape):
        return pl.BlockSpec(shape, lambda g: (0,) * len(shape))

    return pl.pallas_call(
        attention_kernel,
        grid=(rows // GROUP,),
        out_shape=jax.ShapeDtypeStruct((both, width), jnp.bfloat16),
        in_specs=[pl.BlockSpec(memory_space=pltpu.SMEM)]
        + [whole(both, cols)] * NZ
        + [whole(both, HD)] * 2
        + [pl.BlockSpec((2, GROUP, held, HD), lambda g: (0, g, 0, 0))],
        out_specs=whole(both, width),
        scratch_shapes=[
            pltpu.VMEM((rows * lanes, HD), jnp.float32),
            pltpu.VMEM((both, HD), jnp.float32),
            pltpu.VMEM((both, HD), jnp.float32),
            pltpu.VMEM((rows * lanes, HD), jnp.float32),
        ],
        compiler_params=pltpu.CompilerParams(vmem_limit_bytes=48 * MIB),
        cost_estimate=pl.CostEstimate(
            flops=4 * rows * lanes * held * HD,
            bytes_accessed=16 * rows * held * HD,
            transcendentals=rows * lanes * held,
        ),
        name="attention",
    )(lengths, *sums, cos, sin, cache)


def after(values, *first):
    return lax.optimization_barrier((*values, *first))[: len(values)]


def body(hidden, qkv_rows, o_rows, block_owner, cache, lengths):
    groups = lax.axis_size("tp")
    steps, rows, width = hidden.shape
    owned = qkv_rows.shape[0]
    query_cols = HQ * HD
    kv_cols = HK * HD
    cols = (query_cols + 2 * kv_cols) // groups
    copy = slabs_of(qkv_rows, o_rows, groups)

    cos, sin = turns(lengths)
    parts = shuffle(hidden.reshape(steps * rows, width), block_owner)
    parts = [parts[0]] + [z_shift(parts[k], k) for k in range(1, NZ)]

    both = lax.all_to_all(copy, "tp", split_axis=0, concat_axis=0, tiled=True)
    both = both.reshape(groups * owned, -1)
    both, cos, sin, parts[1], parts[3] = lax.optimization_barrier(
        (both, cos, sin, parts[1], parts[3])
    )
    w, own = both[:, :cols], both[:, cols:]
    half = own.shape[0] // 2

    w_y, w_c = flip(w, 8), flip(w, 1)
    own, parts[2] = lax.optimization_barrier((own, parts[2]))
    below, above = z_shift(own, 1), z_shift(own, -1)
    begun = partials(parts, (w, w_c))
    w_y, below, above, own, *begun = lax.optimization_barrier((w_y, below, above, own, *begun))
    w_yc = flip(w_y, 1)
    far_a, far_b = z_shift(above[:half], -1), z_shift(below[half:], 1)
    across = flip(own, 8)

    sums = partials(parts, (w_y, w_yc), begun)
    sums = [sums[0]] + [z_shift(sums[k], -k) for k in range(1, NZ)]
    far_a, far_b, across = after((far_a, far_b, across))
    across_far_a, across_far_b = flip(far_a, 8), flip(far_b, 8)
    (across,) = after((across,), *sums)
    across_below, across_above = z_shift(across, 1), z_shift(across, -1)
    mixed = attention(sums, cos, sin, cache, lengths)

    mixed_c = flip(mixed, 1)
    sources = (own, below, above, across, far_a, far_b)
    sources += (across_far_a, across_far_b, across_below, across_above)
    theirs = terms_of(mixed_c, sources)
    mine = terms_of(*after((mixed,), theirs), sources)
    pieces = (mine, flip(theirs, 1))
    places = ((0, 0, 0), (0, 3, 0), (0, 1, 0), (1, 0, 0), (0, 2, 0), (0, 2, 4))
    places += ((1, 2, 0), (1, 2, 4), (1, 3, 0), (1, 1, 0))
    spots = []
    for core in range(2):
        begin = 0
        for (dy, dz, t0), source in zip(places, sources):
            size = source.shape[0]
            spots.append((core, dy, dz, core, t0, size // owned, begin))
            begin += size
    slabs = place(pieces, tuple(spots), block_owner, groups, rows)

    first = [slabs[0]] + [x_shift(slabs[k], k) for k in range(1, NX)]
    second = [slabs[NX], y_flip(slabs[NX + 1])]
    first = sum(value.astype(jnp.float32) for value in first)
    second = sum(value.astype(jnp.float32) for value in second)
    first = first[0] + y_flip(first[1].astype(jnp.bfloat16)).astype(jnp.float32)
    second = [second[0]] + [x_shift(second[k].astype(jnp.bfloat16), k) for k in range(1, NX)]
    second = sum(value.astype(jnp.float32) for value in second)
    return jnp.stack([first, second]).astype(jnp.bfloat16)


def solution(mesh):
    in_specs = (
        P(None, "fsdp", None),
        P(("fsdp", "tp"), None),
        P(("fsdp", "tp"), None),
        P(),
        P(None, "fsdp", None, "tp"),
        P("fsdp"),
    )
    out_specs = P(None, "fsdp", "tp")
    return jax.shard_map(body, mesh=mesh, in_specs=in_specs, out_specs=out_specs, check_vma=False)
```

```python
import functools
import math

import jax
import jax.numpy as jnp
from jax import lax
from jax.experimental import pallas as pl
from jax.experimental.pallas import tpu as pltpu
from jax.sharding import PartitionSpec as P

HQ = 64
HK = 8
HD = 128
NZ = 4
NX = 4
GROUP = 8
CHUNK = 512
MIB = 1024 * 1024


def z_shift(value, k):
    pairs = [(f, (f // 8) * 8 + ((f // 2 + k) % NZ) * 2 + f % 2) for f in range(16)]
    return lax.ppermute(value, "fsdp", pairs)


def flip(value, bit):
    return lax.ppermute(value, "fsdp", [(f, f ^ bit) for f in range(16)])


def x_shift(value, k):
    return lax.ppermute(value, "tp", [(t, (t // 2 + k) % NX * 2 + t % 2) for t in range(2 * NX)])


def y_flip(value):
    return lax.ppermute(value, "tp", [(t, t ^ 1) for t in range(2 * NX)])


def slabs_kernel(query, key, value, back, out_ref):
    begin = 0
    for ref in (query, key, value, back):
        width = ref.shape[1] // out_ref.shape[0]
        for g in range(out_ref.shape[0]):
            part = ref[:, g * width : (g + 1) * width]
            out_ref[g, :, begin : begin + width] = part.astype(out_ref.dtype)
        begin += width


def slabs_of(qkv_rows, o_rows, groups):
    owned = qkv_rows.shape[0]
    query_cols = HQ * HD
    each = 2
    wide, narrow = each * query_cols // groups, each * HK * HD // groups
    keys_at = query_cols // narrow
    values_at = keys_at + HK * HD // narrow
    cols = (2 * wide + 2 * narrow) // each
    return pl.pallas_call(
        slabs_kernel,
        grid=(groups // each,),
        out_shape=jax.ShapeDtypeStruct((groups, owned, cols), jnp.bfloat16),
        in_specs=[
            pl.BlockSpec((owned, wide), lambda g: (0, g)),
            pl.BlockSpec((owned, narrow), lambda g: (0, keys_at + g)),
            pl.BlockSpec((owned, narrow), lambda g: (0, values_at + g)),
            pl.BlockSpec((owned, wide), lambda g: (0, g)),
        ],
        out_specs=pl.BlockSpec((each, owned, cols), lambda g: (g, 0, 0)),
        compiler_params=pltpu.CompilerParams(vmem_limit_bytes=60 * MIB),
        cost_estimate=pl.CostEstimate(
            flops=0, bytes_accessed=6 * groups * owned * cols, transcendentals=0
        ),
        name="slabs",
    )(qkv_rows, qkv_rows, qkv_rows, o_rows)


def shuffle_kernel(owner_ref, hidden_ref, *out_refs):
    f = lax.axis_index("fsdp")
    y_lo, z, core = f // 8, lax.rem(f // 2, 4), lax.rem(f, 2)
    rows = hidden_ref.shape[0]
    low = lax.broadcasted_iota(jnp.int32, (rows, 128), 1) < 64

    for k, out_ref in enumerate(out_refs):
        zz = lax.rem(z + k, 4)

        def step(n, carry, zz=zz, out_ref=out_ref):
            q, p = n // 4, lax.rem(n, 4)
            yy = lax.rem(y_lo + q // 2, 2)
            cc = lax.rem(core + lax.rem(q, 2), 2)
            i = yy * 64 + zz * 16 + cc * 8 + 2 * p
            s0, s1 = owner_ref[0, i], owner_ref[0, i + 1]
            a = hidden_ref[:, pl.ds(pl.multiple_of((s0 // 2) * 128, 128), 128)].astype(jnp.float32)
            b = hidden_ref[:, pl.ds(pl.multiple_of((s1 // 2) * 128, 128), 128)].astype(jnp.float32)
            a = pltpu.roll(a, 64 * lax.rem(s0, 2), 1)
            b = pltpu.roll(b, 64 * (1 - lax.rem(s1, 2)), 1)
            out_ref[:, pl.ds(pl.multiple_of(n * 128, 128), 128)] = jnp.where(low, a, b).astype(
                jnp.bfloat16
            )
            return carry

        lax.fori_loop(0, 16, step, 0, unroll=8)


def shuffle(hidden, block_owner):
    rows, width = hidden.shape
    part = jax.ShapeDtypeStruct((rows, width // NZ), jnp.bfloat16)
    return pl.pallas_call(
        shuffle_kernel,
        out_shape=[part] * NZ,
        in_specs=[
            pl.BlockSpec(memory_space=pltpu.SMEM),
            pl.BlockSpec(memory_space=pltpu.VMEM),
        ],
        out_specs=[pl.BlockSpec(memory_space=pltpu.VMEM)] * NZ,
        compiler_params=pltpu.CompilerParams(vmem_limit_bytes=14 * MIB),
        cost_estimate=pl.CostEstimate(
            flops=rows * width * 8, bytes_accessed=4 * rows * width, transcendentals=0
        ),
        name="shuffle",
    )(block_owner, hidden)


def partial_kernel(begun, *refs):
    held, weights = refs[:NZ], refs[NZ : NZ + 2]
    totals = refs[NZ + 2 : 2 * NZ + 2] if begun else ()
    *outs, stacked = refs[NZ + 2 + len(totals) :]
    rows = held[0].shape[0]
    depth = weights[0].shape[0]

    @pl.when(pl.program_id(0) == 0)
    def _():
        for k, h in enumerate(held):
            stacked[pl.ds(k * rows, rows), :] = h[...]

    total = jnp.dot(stacked[:, :depth], weights[0][...], preferred_element_type=jnp.float32)
    total = total + jnp.dot(
        stacked[:, depth:], weights[1][...], preferred_element_type=jnp.float32
    )
    for k, out in enumerate(outs):
        part = total[k * rows : (k + 1) * rows]
        if begun:
            part = part + totals[k][...]
        out[...] = part.astype(out.dtype)


def partials(parts, weights, totals=()):
    rows, width = parts[0].shape
    depth, cols = weights[0].shape
    tile = 256
    begun = len(totals) > 0
    place = 1 if begun else 0
    block = pl.BlockSpec((rows, tile), lambda j: (0, j))
    types = [jnp.float32] + [jnp.bfloat16 if begun else jnp.float32] * (NZ - 1)
    return pl.pallas_call(
        functools.partial(partial_kernel, begun),
        grid=(cols // tile,),
        out_shape=[jax.ShapeDtypeStruct((rows, cols), kind) for kind in types],
        in_specs=[pl.BlockSpec((rows, width // 2), lambda j: (0, place))] * NZ
        + [pl.BlockSpec((depth, tile), lambda j: (0, j))] * 2
        + [block] * len(totals),
        out_specs=[block] * NZ,
        scratch_shapes=[pltpu.VMEM((NZ * rows, width // 2), jnp.bfloat16)],
        compiler_params=pltpu.CompilerParams(vmem_limit_bytes=14 * MIB),
        cost_estimate=pl.CostEstimate(
            flops=NZ * rows * width * cols,
            bytes_accessed=NZ * rows * width + width * cols + 4 * NZ * rows * cols,
            transcendentals=0,
        ),
        name="partials_rest" if begun else "partials",
    )(*parts, *weights, *totals)


def terms_kernel(mixed_ref, *refs):
    *sources, out_ref = refs
    spare = out_ref.shape[1] - mixed_ref.shape[0]
    wide = jnp.pad(mixed_ref[...].astype(jnp.float32), ((0, spare), (0, 0)))
    turned = wide.T.astype(jnp.bfloat16)
    begin = 0
    for source in sources:
        size = source.shape[0]
        chunk = min(CHUNK, size)

        def multiply(n, carry, source=source, begin=begin, chunk=chunk):
            rows = source[pl.ds(pl.multiple_of(n * chunk, chunk), chunk), :]
            to = pl.ds(pl.multiple_of(begin + n * chunk, chunk), chunk)
            out_ref[to, :] = jnp.dot(rows, turned, preferred_element_type=jnp.float32).astype(
                out_ref.dtype
            )
            return carry

        lax.fori_loop(0, size // chunk, multiply, 0)
        begin += size


def terms_of(mixed, sources):
    rows, depth = mixed.shape
    width = sum(source.shape[0] for source in sources)
    lanes = -(-rows // 128) * 128
    vmem = pl.BlockSpec(memory_space=pltpu.VMEM)
    return pl.pallas_call(
        terms_kernel,
        out_shape=jax.ShapeDtypeStruct((width, lanes), jnp.bfloat16),
        in_specs=[vmem] * (1 + len(sources)),
        out_specs=vmem,
        compiler_params=pltpu.CompilerParams(vmem_limit_bytes=20 * MIB),
        cost_estimate=pl.CostEstimate(
            flops=2 * rows * depth * width,
            bytes_accessed=2 * (rows * depth + depth * width + rows * width),
            transcendentals=0,
        ),
        name="terms",
    )(mixed, *sources)


def place_kernel(spots, groups, owner_ref, *refs):
    pieces, firsts, seconds = refs[:-7], refs[-7:-3], refs[-3:-1]
    placed = refs[-1]
    f = lax.axis_index("fsdp")
    y_lo, z, core = f // 8, lax.rem(f // 2, NZ), lax.rem(f, 2)
    width = placed.shape[0]
    owned = width // owner_ref.shape[1]
    for n, dy, dz, dc, t0, blocks, begin in spots:
        first = (
            lax.rem(y_lo + dy, 2) * 64 + lax.rem(z + dz, NZ) * 16 + lax.rem(core + dc, 2) * 8 + t0
        )

        def put(b, carry, n=n, first=first, begin=begin):
            goal = pl.multiple_of(owner_ref[1, first + b] * owned, owned)
            start = pl.multiple_of(begin + b * owned, owned)
            placed[pl.ds(goal, owned), :] = pieces[n][pl.ds(start, owned), :]
            return carry

        lax.fori_loop(0, blocks, put, 0)
    slab = width // groups
    t = lax.axis_index("tp")
    for k in range(NX):
        for j in range(2):
            at = lax.rem(t // 2 + k, NX) * 2 + lax.rem(lax.rem(t, 2) + j, 2)
            turned = placed[pl.ds(pl.multiple_of(at * slab, slab), slab), :].T
            rows = firsts[k].shape[1]
            firsts[k][j] = turned[:rows]
            seconds[j][k] = turned[rows : 2 * rows]


def place(pieces, spots, block_owner, groups, rows):
    width = sum(piece.shape[0] for piece in pieces)
    lanes = pieces[0].shape[1]
    vmem = pl.BlockSpec(memory_space=pltpu.VMEM)
    return pl.pallas_call(
        functools.partial(place_kernel, spots, groups),
        out_shape=[jax.ShapeDtypeStruct((2, rows, width // groups), jnp.bfloat16)] * NX
        + [jax.ShapeDtypeStruct((NX, rows, width // groups), jnp.bfloat16)] * 2,
        in_specs=[pl.BlockSpec(memory_space=pltpu.SMEM)] + [vmem] * len(pieces),
        out_specs=[vmem] * (NX + 2),
        scratch_shapes=[pltpu.VMEM((width, lanes), jnp.bfloat16)],
        compiler_params=pltpu.CompilerParams(vmem_limit_bytes=20 * MIB),
        cost_estimate=pl.CostEstimate(
            flops=0, bytes_accessed=8 * rows * width, transcendentals=0
        ),
        name="place",
    )(block_owner, *pieces)


def turns(lengths):
    half = HD // 2
    position = (lengths[None, :] + jnp.arange(2, dtype=jnp.int32)[:, None]).reshape(-1)
    freq = 1000000.0 ** (-jnp.arange(half, dtype=jnp.float32) * 2.0 / HD)
    angle = position.astype(jnp.float32)[:, None] * freq
    cosine, sine = jnp.cos(angle), jnp.sin(angle)
    return jnp.concatenate([cosine, cosine], axis=1), jnp.concatenate([-sine, sine], axis=1)


def attention_kernel(
    lengths_ref, p0, p1, p2, p3, cos_ref, sin_ref, cache_ref, out_ref, query, keys, values, result
):
    step = pl.program_id(0)
    both = p0.shape[0]
    rows = both // 2
    heads = out_ref.shape[1] // HD
    lanes = 2 * heads
    span = GROUP * lanes

    @pl.when(step == 0)
    def _():
        cosine, sine = cos_ref[...], sin_ref[...]

        def part(begin):
            cut = slice(begin * HD, (begin + 1) * HD)
            total = p0[:, cut] + p1[:, cut].astype(jnp.float32)
            return total + p2[:, cut].astype(jnp.float32) + p3[:, cut].astype(jnp.float32)

        def turn(x):
            return x * cosine + pltpu.roll(x, HD // 2, 1) * sine

        for h in range(heads):
            turned = turn(part(h))
            for s in range(2):
                query[pl.ds(s * heads + h, rows, stride=lanes), :] = turned[
                    s * rows : (s + 1) * rows
                ]
        new_keys, new_values = turn(part(heads)), part(heads + 1)
        for g in range(rows // GROUP):
            for t in range(2):
                to = slice((2 * g + t) * GROUP, (2 * g + t + 1) * GROUP)
                begin = t * rows + g * GROUP
                keys[to] = new_keys[begin : begin + GROUP]
                values[to] = new_values[begin : begin + GROUP]

    factor = 1.0 / math.sqrt(HD)
    nt = (((1,), (1,)), ((), ()))
    at = pl.ds(pl.multiple_of(step * span, span), span)
    fresh_at = pl.ds(pl.multiple_of(step * 2 * GROUP, 2 * GROUP), 2 * GROUP)
    q = query[at, :].astype(jnp.bfloat16)
    fresh = (
        lax.dot_general(
            q, keys[fresh_at, :].astype(jnp.bfloat16), nt, preferred_element_type=jnp.float32
        )
        * factor
    )
    of = lax.broadcasted_iota(jnp.int32, fresh.shape, 0)
    new = lax.broadcasted_iota(jnp.int32, fresh.shape, 1)
    seen = (of // lanes == new % GROUP) & (new // GROUP <= (of // heads) % 2)
    fresh = jnp.where(seen, fresh, -jnp.inf)

    held = cache_ref.shape[2]
    place = lax.broadcasted_iota(jnp.int32, (lanes, held), 1)
    pieces = []
    for r in range(GROUP):
        score = lax.dot_general(
            q[r * lanes : (r + 1) * lanes], cache_ref[0, r], nt, preferred_element_type=jnp.float32
        )
        pieces.append(jnp.where(place < lengths_ref[step * GROUP + r], score * factor, -jnp.inf))
    old = jnp.concatenate(pieces, axis=0)
    top = jnp.maximum(
        jnp.max(old, axis=1, keepdims=True), jnp.max(fresh, axis=1, keepdims=True)
    )
    old_w = jnp.exp(old - top)
    fresh_w = jnp.exp(fresh - top)
    total = jnp.sum(old_w, axis=1, keepdims=True) + jnp.sum(fresh_w, axis=1, keepdims=True)
    scale = 1.0 / total
    old_p = (old_w * scale).astype(jnp.bfloat16)
    fresh_p = (fresh_w * scale).astype(jnp.bfloat16)
    mixed = jnp.concatenate(
        [
            jnp.dot(
                old_p[r * lanes : (r + 1) * lanes],
                cache_ref[1, r],
                preferred_element_type=jnp.float32,
            )
            for r in range(GROUP)
        ],
        axis=0,
    )
    mixed = mixed + jnp.dot(
        fresh_p, values[fresh_at, :].astype(jnp.bfloat16), preferred_element_type=jnp.float32
    )
    result[at, :] = mixed

    @pl.when(step == pl.num_programs(0) - 1)
    def _():
        for h in range(heads):
            for s in range(2):
                out_ref[s * rows : (s + 1) * rows, h * HD : (h + 1) * HD] = result[
                    pl.ds(s * heads + h, rows, stride=lanes), :
                ].astype(out_ref.dtype)


def attention(sums, cos, sin, cache, lengths):
    both, cols = sums[0].shape
    rows = both // 2
    width = cols - 2 * HD
    held = cache.shape[2]
    lanes = 2 * width // HD

    def whole(*shape):
        return pl.BlockSpec(shape, lambda g: (0,) * len(shape))

    return pl.pallas_call(
        attention_kernel,
        grid=(rows // GROUP,),
        out_shape=jax.ShapeDtypeStruct((both, width), jnp.bfloat16),
        in_specs=[pl.BlockSpec(memory_space=pltpu.SMEM)]
        + [whole(both, cols)] * NZ
        + [whole(both, HD)] * 2
        + [pl.BlockSpec((2, GROUP, held, HD), lambda g: (0, g, 0, 0))],
        out_specs=whole(both, width),
        scratch_shapes=[
            pltpu.VMEM((rows * lanes, HD), jnp.float32),
            pltpu.VMEM((both, HD), jnp.float32),
            pltpu.VMEM((both, HD), jnp.float32),
            pltpu.VMEM((rows * lanes, HD), jnp.float32),
        ],
        compiler_params=pltpu.CompilerParams(vmem_limit_bytes=48 * MIB),
        cost_estimate=pl.CostEstimate(
            flops=4 * rows * lanes * held * HD,
            bytes_accessed=16 * rows * held * HD,
            transcendentals=rows * lanes * held,
        ),
        name="attention",
    )(lengths, *sums, cos, sin, cache)


def after(values, *first):
    return lax.optimization_barrier((*values, *first))[: len(values)]


def body(hidden, qkv_rows, o_rows, block_owner, cache, lengths):
    groups = lax.axis_size("tp")
    steps, rows, width = hidden.shape
    owned = qkv_rows.shape[0]
    query_cols = HQ * HD
    kv_cols = HK * HD
    cols = (query_cols + 2 * kv_cols) // groups
    copy = slabs_of(qkv_rows, o_rows, groups)

    cos, sin = turns(lengths)
    parts = shuffle(hidden.reshape(steps * rows, width), block_owner)
    parts = [parts[0]] + [z_shift(parts[k], k) for k in range(1, NZ)]

    both = lax.all_to_all(copy, "tp", split_axis=0, concat_axis=0, tiled=True)
    both = both.reshape(groups * owned, -1)
    both, cos, sin, parts[1], parts[3] = lax.optimization_barrier(
        (both, cos, sin, parts[1], parts[3])
    )
    w, own = both[:, :cols], both[:, cols:]
    half = own.shape[0] // 2

    w_y, w_c = flip(w, 8), flip(w, 1)
    own, parts[2] = lax.optimization_barrier((own, parts[2]))
    below, above = z_shift(own, 1), z_shift(own, -1)
    begun = partials(parts, (w, w_c))
    w_y, below, above, own, *begun = lax.optimization_barrier((w_y, below, above, own, *begun))
    w_yc = flip(w_y, 1)
    far_a, far_b = z_shift(above[:half], -1), z_shift(below[half:], 1)
    across = flip(own, 8)

    sums = partials(parts, (w_y, w_yc), begun)
    sums = [sums[0]] + [z_shift(sums[k], -k) for k in range(1, NZ)]
    far_a, far_b, across = after((far_a, far_b, across))
    across_far_a, across_far_b = flip(far_a, 8), flip(far_b, 8)
    (across,) = after((across,), sums[1], sums[2])
    across_below, across_above = z_shift(across, 1), z_shift(across, -1)
    mixed = attention(sums, cos, sin, cache, lengths)

    mixed_c = flip(mixed, 1)
    sources = (own, below, above, across, far_a, far_b)
    sources += (across_far_a, across_far_b, across_below, across_above)
    theirs = terms_of(mixed_c, sources)
    mine = terms_of(*after((mixed,), theirs), sources)
    pieces = (mine, flip(theirs, 1))
    places = ((0, 0, 0), (0, 3, 0), (0, 1, 0), (1, 0, 0), (0, 2, 0), (0, 2, 4))
    places += ((1, 2, 0), (1, 2, 4), (1, 3, 0), (1, 1, 0))
    spots = []
    for core in range(2):
        begin = 0
        for (dy, dz, t0), source in zip(places, sources):
            size = source.shape[0]
            spots.append((core, dy, dz, core, t0, size // owned, begin))
            begin += size
    slabs = place(pieces, tuple(spots), block_owner, groups, rows)

    first = [slabs[0]] + [x_shift(slabs[k], k) for k in range(1, NX)]
    second = [slabs[NX], y_flip(slabs[NX + 1])]
    first = sum(value.astype(jnp.float32) for value in first)
    second = sum(value.astype(jnp.float32) for value in second)
    first = first[0] + y_flip(first[1].astype(jnp.bfloat16)).astype(jnp.float32)
    second = [second[0]] + [x_shift(second[k].astype(jnp.bfloat16), k) for k in range(1, NX)]
    second = sum(value.astype(jnp.float32) for value in second)
    return jnp.stack([first, second]).astype(jnp.bfloat16)


def solution(mesh):
    in_specs = (
        P(None, "fsdp", None),
        P(("fsdp", "tp"), None),
        P(("fsdp", "tp"), None),
        P(),
        P(None, "fsdp", None, "tp"),
        P("fsdp"),
    )
    out_specs = P(None, "fsdp", "tp")
    return jax.shard_map(body, mesh=mesh, in_specs=in_specs, out_specs=out_specs, check_vma=False)
```

```python
import functools
import math

import jax
import jax.numpy as jnp
from jax import lax
from jax.experimental import pallas as pl
from jax.experimental.pallas import tpu as pltpu
from jax.sharding import PartitionSpec as P

HQ = 64
HK = 8
HD = 128
NZ = 4
NX = 4
GROUP = 8
CHUNK = 512
MIB = 1024 * 1024


def z_shift(value, k):
    pairs = [(f, (f // 8) * 8 + ((f // 2 + k) % NZ) * 2 + f % 2) for f in range(16)]
    return lax.ppermute(value, "fsdp", pairs)


def flip(value, bit):
    return lax.ppermute(value, "fsdp", [(f, f ^ bit) for f in range(16)])


def x_shift(value, k):
    return lax.ppermute(value, "tp", [(t, (t // 2 + k) % NX * 2 + t % 2) for t in range(2 * NX)])


def y_flip(value):
    return lax.ppermute(value, "tp", [(t, t ^ 1) for t in range(2 * NX)])


def slabs_kernel(query, key, value, back, out_ref):
    begin = 0
    for ref in (query, key, value, back):
        width = ref.shape[1] // out_ref.shape[0]
        for g in range(out_ref.shape[0]):
            part = ref[:, g * width : (g + 1) * width]
            out_ref[g, :, begin : begin + width] = part.astype(out_ref.dtype)
        begin += width


def slabs_of(qkv_rows, o_rows, groups):
    owned = qkv_rows.shape[0]
    query_cols = HQ * HD
    each = 2
    wide, narrow = each * query_cols // groups, each * HK * HD // groups
    keys_at = query_cols // narrow
    values_at = keys_at + HK * HD // narrow
    cols = (2 * wide + 2 * narrow) // each
    return pl.pallas_call(
        slabs_kernel,
        grid=(groups // each,),
        out_shape=jax.ShapeDtypeStruct((groups, owned, cols), jnp.bfloat16),
        in_specs=[
            pl.BlockSpec((owned, wide), lambda g: (0, g)),
            pl.BlockSpec((owned, narrow), lambda g: (0, keys_at + g)),
            pl.BlockSpec((owned, narrow), lambda g: (0, values_at + g)),
            pl.BlockSpec((owned, wide), lambda g: (0, g)),
        ],
        out_specs=pl.BlockSpec((each, owned, cols), lambda g: (g, 0, 0)),
        compiler_params=pltpu.CompilerParams(vmem_limit_bytes=60 * MIB),
        cost_estimate=pl.CostEstimate(
            flops=0, bytes_accessed=6 * groups * owned * cols, transcendentals=0
        ),
        name="slabs",
    )(qkv_rows, qkv_rows, qkv_rows, o_rows)


def shuffle_kernel(owner_ref, hidden_ref, *out_refs):
    f = lax.axis_index("fsdp")
    y_lo, z, core = f // 8, lax.rem(f // 2, 4), lax.rem(f, 2)
    rows = hidden_ref.shape[0]
    low = lax.broadcasted_iota(jnp.int32, (rows, 128), 1) < 64

    for k, out_ref in enumerate(out_refs):
        zz = lax.rem(z + k, 4)

        def step(n, carry, zz=zz, out_ref=out_ref):
            q, p = n // 4, lax.rem(n, 4)
            yy = lax.rem(y_lo + q // 2, 2)
            cc = lax.rem(core + lax.rem(q, 2), 2)
            i = yy * 64 + zz * 16 + cc * 8 + 2 * p
            s0, s1 = owner_ref[0, i], owner_ref[0, i + 1]
            a = hidden_ref[:, pl.ds(pl.multiple_of((s0 // 2) * 128, 128), 128)].astype(jnp.float32)
            b = hidden_ref[:, pl.ds(pl.multiple_of((s1 // 2) * 128, 128), 128)].astype(jnp.float32)
            a = pltpu.roll(a, 64 * lax.rem(s0, 2), 1)
            b = pltpu.roll(b, 64 * (1 - lax.rem(s1, 2)), 1)
            out_ref[:, pl.ds(pl.multiple_of(n * 128, 128), 128)] = jnp.where(low, a, b).astype(
                jnp.bfloat16
            )
            return carry

        lax.fori_loop(0, 16, step, 0, unroll=8)


def shuffle(hidden, block_owner):
    rows, width = hidden.shape
    part = jax.ShapeDtypeStruct((rows, width // NZ), jnp.bfloat16)
    return pl.pallas_call(
        shuffle_kernel,
        out_shape=[part] * NZ,
        in_specs=[
            pl.BlockSpec(memory_space=pltpu.SMEM),
            pl.BlockSpec(memory_space=pltpu.VMEM),
        ],
        out_specs=[pl.BlockSpec(memory_space=pltpu.VMEM)] * NZ,
        compiler_params=pltpu.CompilerParams(vmem_limit_bytes=14 * MIB),
        cost_estimate=pl.CostEstimate(
            flops=rows * width * 8, bytes_accessed=4 * rows * width, transcendentals=0
        ),
        name="shuffle",
    )(block_owner, hidden)


def partial_kernel(begun, *refs):
    held, weights = refs[:NZ], refs[NZ : NZ + 2]
    totals = refs[NZ + 2 : 2 * NZ + 2] if begun else ()
    *outs, stacked = refs[NZ + 2 + len(totals) :]
    rows = held[0].shape[0]
    depth = weights[0].shape[0]

    @pl.when(pl.program_id(0) == 0)
    def _():
        for k, h in enumerate(held):
            stacked[pl.ds(k * rows, rows), :] = h[...]

    total = jnp.dot(stacked[:, :depth], weights[0][...], preferred_element_type=jnp.float32)
    total = total + jnp.dot(
        stacked[:, depth:], weights[1][...], preferred_element_type=jnp.float32
    )
    for k, out in enumerate(outs):
        part = total[k * rows : (k + 1) * rows]
        if begun:
            part = part + totals[k][...]
        out[...] = part.astype(out.dtype)


def partials(parts, weights, totals=()):
    rows, width = parts[0].shape
    depth, cols = weights[0].shape
    tile = 256
    begun = len(totals) > 0
    place = 1 if begun else 0
    block = pl.BlockSpec((rows, tile), lambda j: (0, j))
    types = [jnp.float32] + [jnp.bfloat16 if begun else jnp.float32] * (NZ - 1)
    return pl.pallas_call(
        functools.partial(partial_kernel, begun),
        grid=(cols // tile,),
        out_shape=[jax.ShapeDtypeStruct((rows, cols), kind) for kind in types],
        in_specs=[pl.BlockSpec((rows, width // 2), lambda j: (0, place))] * NZ
        + [pl.BlockSpec((depth, tile), lambda j: (0, j))] * 2
        + [block] * len(totals),
        out_specs=[block] * NZ,
        scratch_shapes=[pltpu.VMEM((NZ * rows, width // 2), jnp.bfloat16)],
        compiler_params=pltpu.CompilerParams(vmem_limit_bytes=14 * MIB),
        cost_estimate=pl.CostEstimate(
            flops=NZ * rows * width * cols,
            bytes_accessed=NZ * rows * width + width * cols + 4 * NZ * rows * cols,
            transcendentals=0,
        ),
        name="partials_rest" if begun else "partials",
    )(*parts, *weights, *totals)


def terms_kernel(mixed_ref, *refs):
    *sources, out_ref = refs
    spare = out_ref.shape[1] - mixed_ref.shape[0]
    wide = jnp.pad(mixed_ref[...].astype(jnp.float32), ((0, spare), (0, 0)))
    turned = wide.T.astype(jnp.bfloat16)
    begin = 0
    for source in sources:
        size = source.shape[0]
        chunk = min(CHUNK, size)

        def multiply(n, carry, source=source, begin=begin, chunk=chunk):
            rows = source[pl.ds(pl.multiple_of(n * chunk, chunk), chunk), :]
            to = pl.ds(pl.multiple_of(begin + n * chunk, chunk), chunk)
            out_ref[to, :] = jnp.dot(rows, turned, preferred_element_type=jnp.float32).astype(
                out_ref.dtype
            )
            return carry

        lax.fori_loop(0, size // chunk, multiply, 0)
        begin += size


def terms_of(mixed, sources):
    rows, depth = mixed.shape
    width = sum(source.shape[0] for source in sources)
    lanes = -(-rows // 128) * 128
    vmem = pl.BlockSpec(memory_space=pltpu.VMEM)
    return pl.pallas_call(
        terms_kernel,
        out_shape=jax.ShapeDtypeStruct((width, lanes), jnp.bfloat16),
        in_specs=[vmem] * (1 + len(sources)),
        out_specs=vmem,
        compiler_params=pltpu.CompilerParams(vmem_limit_bytes=20 * MIB),
        cost_estimate=pl.CostEstimate(
            flops=2 * rows * depth * width,
            bytes_accessed=2 * (rows * depth + depth * width + rows * width),
            transcendentals=0,
        ),
        name="terms",
    )(mixed, *sources)


def place_kernel(spots, groups, owner_ref, *refs):
    pieces, firsts, seconds = refs[:-7], refs[-7:-3], refs[-3:-1]
    placed = refs[-1]
    f = lax.axis_index("fsdp")
    y_lo, z, core = f // 8, lax.rem(f // 2, NZ), lax.rem(f, 2)
    width = placed.shape[0]
    owned = width // owner_ref.shape[1]
    for n, dy, dz, dc, t0, blocks, begin in spots:
        first = (
            lax.rem(y_lo + dy, 2) * 64 + lax.rem(z + dz, NZ) * 16 + lax.rem(core + dc, 2) * 8 + t0
        )

        def put(b, carry, n=n, first=first, begin=begin):
            goal = pl.multiple_of(owner_ref[1, first + b] * owned, owned)
            start = pl.multiple_of(begin + b * owned, owned)
            placed[pl.ds(goal, owned), :] = pieces[n][pl.ds(start, owned), :]
            return carry

        lax.fori_loop(0, blocks, put, 0)
    slab = width // groups
    t = lax.axis_index("tp")
    for k in range(NX):
        for j in range(2):
            at = lax.rem(t // 2 + k, NX) * 2 + lax.rem(lax.rem(t, 2) + j, 2)
            turned = placed[pl.ds(pl.multiple_of(at * slab, slab), slab), :].T
            rows = firsts[k].shape[1]
            firsts[k][j] = turned[:rows]
            seconds[j][k] = turned[rows : 2 * rows]


def place(pieces, spots, block_owner, groups, rows):
    width = sum(piece.shape[0] for piece in pieces)
    lanes = pieces[0].shape[1]
    vmem = pl.BlockSpec(memory_space=pltpu.VMEM)
    return pl.pallas_call(
        functools.partial(place_kernel, spots, groups),
        out_shape=[jax.ShapeDtypeStruct((2, rows, width // groups), jnp.bfloat16)] * NX
        + [jax.ShapeDtypeStruct((NX, rows, width // groups), jnp.bfloat16)] * 2,
        in_specs=[pl.BlockSpec(memory_space=pltpu.SMEM)] + [vmem] * len(pieces),
        out_specs=[vmem] * (NX + 2),
        scratch_shapes=[pltpu.VMEM((width, lanes), jnp.bfloat16)],
        compiler_params=pltpu.CompilerParams(vmem_limit_bytes=20 * MIB),
        cost_estimate=pl.CostEstimate(
            flops=0, bytes_accessed=8 * rows * width, transcendentals=0
        ),
        name="place",
    )(block_owner, *pieces)


def turns(lengths):
    half = HD // 2
    position = (lengths[None, :] + jnp.arange(2, dtype=jnp.int32)[:, None]).reshape(-1)
    freq = 1000000.0 ** (-jnp.arange(half, dtype=jnp.float32) * 2.0 / HD)
    angle = position.astype(jnp.float32)[:, None] * freq
    cosine, sine = jnp.cos(angle), jnp.sin(angle)
    return jnp.concatenate([cosine, cosine], axis=1), jnp.concatenate([-sine, sine], axis=1)


def attention_kernel(
    lengths_ref, p0, p1, p2, p3, cos_ref, sin_ref, cache_ref, out_ref, query, keys, values, result
):
    step = pl.program_id(0)
    both = p0.shape[0]
    rows = both // 2
    heads = out_ref.shape[1] // HD
    lanes = 2 * heads
    span = GROUP * lanes

    @pl.when(step == 0)
    def _():
        cosine, sine = cos_ref[...], sin_ref[...]

        def part(begin):
            cut = slice(begin * HD, (begin + 1) * HD)
            total = p0[:, cut] + p1[:, cut].astype(jnp.float32)
            return total + p2[:, cut].astype(jnp.float32) + p3[:, cut].astype(jnp.float32)

        def turn(x):
            return x * cosine + pltpu.roll(x, HD // 2, 1) * sine

        for h in range(heads):
            turned = turn(part(h))
            for s in range(2):
                query[pl.ds(s * heads + h, rows, stride=lanes), :] = turned[
                    s * rows : (s + 1) * rows
                ]
        new_keys, new_values = turn(part(heads)), part(heads + 1)
        for g in range(rows // GROUP):
            for t in range(2):
                to = slice((2 * g + t) * GROUP, (2 * g + t + 1) * GROUP)
                begin = t * rows + g * GROUP
                keys[to] = new_keys[begin : begin + GROUP]
                values[to] = new_values[begin : begin + GROUP]

    factor = 1.0 / math.sqrt(HD)
    nt = (((1,), (1,)), ((), ()))
    at = pl.ds(pl.multiple_of(step * span, span), span)
    fresh_at = pl.ds(pl.multiple_of(step * 2 * GROUP, 2 * GROUP), 2 * GROUP)
    q = query[at, :].astype(jnp.bfloat16)
    fresh = (
        lax.dot_general(
            q, keys[fresh_at, :].astype(jnp.bfloat16), nt, preferred_element_type=jnp.float32
        )
        * factor
    )
    of = lax.broadcasted_iota(jnp.int32, fresh.shape, 0)
    new = lax.broadcasted_iota(jnp.int32, fresh.shape, 1)
    seen = (of // lanes == new % GROUP) & (new // GROUP <= (of // heads) % 2)
    fresh = jnp.where(seen, fresh, -jnp.inf)

    held = cache_ref.shape[2]
    place = lax.broadcasted_iota(jnp.int32, (lanes, held), 1)
    pieces = []
    for r in range(GROUP):
        score = lax.dot_general(
            q[r * lanes : (r + 1) * lanes], cache_ref[0, r], nt, preferred_element_type=jnp.float32
        )
        pieces.append(jnp.where(place < lengths_ref[step * GROUP + r], score * factor, -jnp.inf))
    old = jnp.concatenate(pieces, axis=0)
    top = jnp.maximum(
        jnp.max(old, axis=1, keepdims=True), jnp.max(fresh, axis=1, keepdims=True)
    )
    old_w = jnp.exp(old - top)
    fresh_w = jnp.exp(fresh - top)
    total = jnp.sum(old_w, axis=1, keepdims=True) + jnp.sum(fresh_w, axis=1, keepdims=True)
    scale = 1.0 / total
    old_p = (old_w * scale).astype(jnp.bfloat16)
    fresh_p = (fresh_w * scale).astype(jnp.bfloat16)
    mixed = jnp.concatenate(
        [
            jnp.dot(
                old_p[r * lanes : (r + 1) * lanes],
                cache_ref[1, r],
                preferred_element_type=jnp.float32,
            )
            for r in range(GROUP)
        ],
        axis=0,
    )
    mixed = mixed + jnp.dot(
        fresh_p, values[fresh_at, :].astype(jnp.bfloat16), preferred_element_type=jnp.float32
    )
    result[at, :] = mixed

    @pl.when(step == pl.num_programs(0) - 1)
    def _():
        for h in range(heads):
            for s in range(2):
                out_ref[s * rows : (s + 1) * rows, h * HD : (h + 1) * HD] = result[
                    pl.ds(s * heads + h, rows, stride=lanes), :
                ].astype(out_ref.dtype)


def attention(sums, cos, sin, cache, lengths):
    both, cols = sums[0].shape
    rows = both // 2
    width = cols - 2 * HD
    held = cache.shape[2]
    lanes = 2 * width // HD

    def whole(*shape):
        return pl.BlockSpec(shape, lambda g: (0,) * len(shape))

    return pl.pallas_call(
        attention_kernel,
        grid=(rows // GROUP,),
        out_shape=jax.ShapeDtypeStruct((both, width), jnp.bfloat16),
        in_specs=[pl.BlockSpec(memory_space=pltpu.SMEM)]
        + [whole(both, cols)] * NZ
        + [whole(both, HD)] * 2
        + [pl.BlockSpec((2, GROUP, held, HD), lambda g: (0, g, 0, 0))],
        out_specs=whole(both, width),
        scratch_shapes=[
            pltpu.VMEM((rows * lanes, HD), jnp.float32),
            pltpu.VMEM((both, HD), jnp.float32),
            pltpu.VMEM((both, HD), jnp.float32),
            pltpu.VMEM((rows * lanes, HD), jnp.float32),
        ],
        compiler_params=pltpu.CompilerParams(vmem_limit_bytes=48 * MIB),
        cost_estimate=pl.CostEstimate(
            flops=4 * rows * lanes * held * HD,
            bytes_accessed=16 * rows * held * HD,
            transcendentals=rows * lanes * held,
        ),
        name="attention",
    )(lengths, *sums, cos, sin, cache)


def after(values, *first):
    return lax.optimization_barrier((*values, *first))[: len(values)]


def body(hidden, qkv_rows, o_rows, block_owner, cache, lengths):
    groups = lax.axis_size("tp")
    steps, rows, width = hidden.shape
    owned = qkv_rows.shape[0]
    query_cols = HQ * HD
    kv_cols = HK * HD
    cols = (query_cols + 2 * kv_cols) // groups
    copy = slabs_of(qkv_rows, o_rows, groups)

    cos, sin = turns(lengths)
    parts = shuffle(hidden.reshape(steps * rows, width), block_owner)
    parts = [parts[0]] + [z_shift(parts[k], k) for k in range(1, NZ)]

    both = lax.all_to_all(copy, "tp", split_axis=0, concat_axis=0, tiled=True)
    both = both.reshape(groups * owned, -1)
    w, own = both[:, :cols], both[:, cols:]
    half = own.shape[0] // 2

    w_y, w_c = flip(w, 8), flip(w, 1)
    own, cos, sin, *parts = lax.optimization_barrier((own, cos, sin, *parts))
    below, above = z_shift(own, 1), z_shift(own, -1)
    begun = partials(parts, (w, w_c))
    below, above, *begun = lax.optimization_barrier((below, above, *begun))
    above_a, below_b = above[:half], below[half:]
    w_y, own, above_a, below_b = lax.optimization_barrier((w_y, own, above_a, below_b))
    w_yc = flip(w_y, 1)
    far_a, far_b = z_shift(above_a, -1), z_shift(below_b, 1)
    across = flip(own, 8)

    sums = partials(parts, (w_y, w_yc), begun)
    sums = [sums[0]] + [z_shift(sums[k], -k) for k in range(1, NZ)]
    far_a, far_b, across = after((far_a, far_b, across))
    across_far_a, across_far_b = flip(far_a, 8), flip(far_b, 8)
    (across,) = after((across,), *sums)
    across_below, across_above = z_shift(across, 1), z_shift(across, -1)
    mixed = attention(sums, cos, sin, cache, lengths)

    mixed_c = flip(mixed, 1)
    sources = (own, below, above, across, far_a, far_b)
    sources += (across_far_a, across_far_b, across_below, across_above)
    theirs = terms_of(mixed_c, sources)
    mine = terms_of(*after((mixed,), theirs), sources)
    pieces = (mine, flip(theirs, 1))
    places = ((0, 0, 0), (0, 3, 0), (0, 1, 0), (1, 0, 0), (0, 2, 0), (0, 2, 4))
    places += ((1, 2, 0), (1, 2, 4), (1, 3, 0), (1, 1, 0))
    spots = []
    for core in range(2):
        begin = 0
        for (dy, dz, t0), source in zip(places, sources):
            size = source.shape[0]
            spots.append((core, dy, dz, core, t0, size // owned, begin))
            begin += size
    slabs = place(pieces, tuple(spots), block_owner, groups, rows)

    first = [slabs[0]] + [x_shift(slabs[k], k) for k in range(1, NX)]
    second = [slabs[NX], y_flip(slabs[NX + 1])]
    first = sum(value.astype(jnp.float32) for value in first)
    second = sum(value.astype(jnp.float32) for value in second)
    first = first[0] + y_flip(first[1].astype(jnp.bfloat16)).astype(jnp.float32)
    second = [second[0]] + [x_shift(second[k].astype(jnp.bfloat16), k) for k in range(1, NX)]
    second = sum(value.astype(jnp.float32) for value in second)
    return jnp.stack([first, second]).astype(jnp.bfloat16)


def solution(mesh):
    in_specs = (
        P(None, "fsdp", None),
        P(("fsdp", "tp"), None),
        P(("fsdp", "tp"), None),
        P(),
        P(None, "fsdp", None, "tp"),
        P("fsdp"),
    )
    out_specs = P(None, "fsdp", "tp")
    return jax.shard_map(body, mesh=mesh, in_specs=in_specs, out_specs=out_specs, check_vma=False)
```

```python
import functools
import math

import jax
import jax.numpy as jnp
from jax import lax
from jax.experimental import pallas as pl
from jax.experimental.pallas import tpu as pltpu
from jax.sharding import PartitionSpec as P

HQ = 64
HK = 8
HD = 128
NZ = 4
NX = 4
GROUP = 8
CHUNK = 512
MIB = 1024 * 1024


def z_shift(value, k):
    pairs = [(f, (f // 8) * 8 + ((f // 2 + k) % NZ) * 2 + f % 2) for f in range(16)]
    return lax.ppermute(value, "fsdp", pairs)


def flip(value, bit):
    return lax.ppermute(value, "fsdp", [(f, f ^ bit) for f in range(16)])


def x_shift(value, k):
    return lax.ppermute(value, "tp", [(t, (t // 2 + k) % NX * 2 + t % 2) for t in range(2 * NX)])


def y_flip(value):
    return lax.ppermute(value, "tp", [(t, t ^ 1) for t in range(2 * NX)])


def slabs_kernel(query, key, value, back, out_ref):
    begin = 0
    for ref in (query, key, value, back):
        width = ref.shape[1] // out_ref.shape[0]
        for g in range(out_ref.shape[0]):
            part = ref[:, g * width : (g + 1) * width]
            out_ref[g, :, begin : begin + width] = part.astype(out_ref.dtype)
        begin += width


def slabs_of(qkv_rows, o_rows, groups):
    owned = qkv_rows.shape[0]
    query_cols = HQ * HD
    each = 2
    wide, narrow = each * query_cols // groups, each * HK * HD // groups
    keys_at = query_cols // narrow
    values_at = keys_at + HK * HD // narrow
    cols = (2 * wide + 2 * narrow) // each
    return pl.pallas_call(
        slabs_kernel,
        grid=(groups // each,),
        out_shape=jax.ShapeDtypeStruct((groups, owned, cols), jnp.bfloat16),
        in_specs=[
            pl.BlockSpec((owned, wide), lambda g: (0, g)),
            pl.BlockSpec((owned, narrow), lambda g: (0, keys_at + g)),
            pl.BlockSpec((owned, narrow), lambda g: (0, values_at + g)),
            pl.BlockSpec((owned, wide), lambda g: (0, g)),
        ],
        out_specs=pl.BlockSpec((each, owned, cols), lambda g: (g, 0, 0)),
        compiler_params=pltpu.CompilerParams(vmem_limit_bytes=60 * MIB),
        cost_estimate=pl.CostEstimate(
            flops=0, bytes_accessed=6 * groups * owned * cols, transcendentals=0
        ),
        name="slabs",
    )(qkv_rows, qkv_rows, qkv_rows, o_rows)


def shuffle_kernel(owner_ref, hidden_ref, *out_refs):
    f = lax.axis_index("fsdp")
    y_lo, z, core = f // 8, lax.rem(f // 2, 4), lax.rem(f, 2)
    rows = hidden_ref.shape[0]
    low = lax.broadcasted_iota(jnp.int32, (rows, 128), 1) < 64

    for k, out_ref in enumerate(out_refs):
        zz = lax.rem(z + k, 4)

        def step(n, carry, zz=zz, out_ref=out_ref):
            q, p = n // 4, lax.rem(n, 4)
            yy = lax.rem(y_lo + q // 2, 2)
            cc = lax.rem(core + lax.rem(q, 2), 2)
            i = yy * 64 + zz * 16 + cc * 8 + 2 * p
            s0, s1 = owner_ref[0, i], owner_ref[0, i + 1]
            a = hidden_ref[:, pl.ds(pl.multiple_of((s0 // 2) * 128, 128), 128)].astype(jnp.float32)
            b = hidden_ref[:, pl.ds(pl.multiple_of((s1 // 2) * 128, 128), 128)].astype(jnp.float32)
            a = pltpu.roll(a, 64 * lax.rem(s0, 2), 1)
            b = pltpu.roll(b, 64 * (1 - lax.rem(s1, 2)), 1)
            out_ref[:, pl.ds(pl.multiple_of(n * 128, 128), 128)] = jnp.where(low, a, b).astype(
                jnp.bfloat16
            )
            return carry

        lax.fori_loop(0, 16, step, 0, unroll=8)


def shuffle(hidden, block_owner):
    rows, width = hidden.shape
    part = jax.ShapeDtypeStruct((rows, width // NZ), jnp.bfloat16)
    return pl.pallas_call(
        shuffle_kernel,
        out_shape=[part] * NZ,
        in_specs=[
            pl.BlockSpec(memory_space=pltpu.SMEM),
            pl.BlockSpec(memory_space=pltpu.VMEM),
        ],
        out_specs=[pl.BlockSpec(memory_space=pltpu.VMEM)] * NZ,
        compiler_params=pltpu.CompilerParams(vmem_limit_bytes=14 * MIB),
        cost_estimate=pl.CostEstimate(
            flops=rows * width * 8, bytes_accessed=4 * rows * width, transcendentals=0
        ),
        name="shuffle",
    )(block_owner, hidden)


def partial_kernel(begun, *refs):
    held, weights = refs[:NZ], refs[NZ : NZ + 2]
    totals = refs[NZ + 2 : 2 * NZ + 2] if begun else ()
    *outs, stacked = refs[NZ + 2 + len(totals) :]
    rows = held[0].shape[0]
    depth = weights[0].shape[0]

    @pl.when(pl.program_id(0) == 0)
    def _():
        for k, h in enumerate(held):
            stacked[pl.ds(k * rows, rows), :] = h[...]

    total = jnp.dot(stacked[:, :depth], weights[0][...], preferred_element_type=jnp.float32)
    total = total + jnp.dot(
        stacked[:, depth:], weights[1][...], preferred_element_type=jnp.float32
    )
    for k, out in enumerate(outs):
        part = total[k * rows : (k + 1) * rows]
        if begun:
            part = part + totals[k][...]
        out[...] = part.astype(out.dtype)


def partials(parts, weights, totals=()):
    rows, width = parts[0].shape
    depth, cols = weights[0].shape
    tile = 256
    begun = len(totals) > 0
    place = 1 if begun else 0
    block = pl.BlockSpec((rows, tile), lambda j: (0, j))
    types = [jnp.float32] + [jnp.bfloat16 if begun else jnp.float32] * (NZ - 1)
    return pl.pallas_call(
        functools.partial(partial_kernel, begun),
        grid=(cols // tile,),
        out_shape=[jax.ShapeDtypeStruct((rows, cols), kind) for kind in types],
        in_specs=[pl.BlockSpec((rows, width // 2), lambda j: (0, place))] * NZ
        + [pl.BlockSpec((depth, tile), lambda j: (0, j))] * 2
        + [block] * len(totals),
        out_specs=[block] * NZ,
        scratch_shapes=[pltpu.VMEM((NZ * rows, width // 2), jnp.bfloat16)],
        compiler_params=pltpu.CompilerParams(vmem_limit_bytes=14 * MIB),
        cost_estimate=pl.CostEstimate(
            flops=NZ * rows * width * cols,
            bytes_accessed=NZ * rows * width + width * cols + 4 * NZ * rows * cols,
            transcendentals=0,
        ),
        name="partials_rest" if begun else "partials",
    )(*parts, *weights, *totals)


def terms_kernel(mixed_ref, *refs):
    *sources, out_ref = refs
    spare = out_ref.shape[1] - mixed_ref.shape[0]
    wide = jnp.pad(mixed_ref[...].astype(jnp.float32), ((0, spare), (0, 0)))
    turned = wide.T.astype(jnp.bfloat16)
    begin = 0
    for source in sources:
        size = source.shape[0]
        chunk = min(CHUNK, size)

        def multiply(n, carry, source=source, begin=begin, chunk=chunk):
            rows = source[pl.ds(pl.multiple_of(n * chunk, chunk), chunk), :]
            to = pl.ds(pl.multiple_of(begin + n * chunk, chunk), chunk)
            out_ref[to, :] = jnp.dot(rows, turned, preferred_element_type=jnp.float32).astype(
                out_ref.dtype
            )
            return carry

        lax.fori_loop(0, size // chunk, multiply, 0)
        begin += size


def terms_of(mixed, sources):
    rows, depth = mixed.shape
    width = sum(source.shape[0] for source in sources)
    lanes = -(-rows // 128) * 128
    vmem = pl.BlockSpec(memory_space=pltpu.VMEM)
    return pl.pallas_call(
        terms_kernel,
        out_shape=jax.ShapeDtypeStruct((width, lanes), jnp.bfloat16),
        in_specs=[vmem] * (1 + len(sources)),
        out_specs=vmem,
        compiler_params=pltpu.CompilerParams(vmem_limit_bytes=20 * MIB),
        cost_estimate=pl.CostEstimate(flops=0, bytes_accessed=rows, transcendentals=0),
        name="terms",
    )(mixed, *sources)


def place_kernel(spots, groups, owner_ref, *refs):
    pieces, firsts, seconds = refs[:-7], refs[-7:-3], refs[-3:-1]
    placed = refs[-1]
    f = lax.axis_index("fsdp")
    y_lo, z, core = f // 8, lax.rem(f // 2, NZ), lax.rem(f, 2)
    width = placed.shape[0]
    owned = width // owner_ref.shape[1]
    for n, dy, dz, dc, blocks, begin in spots:
        first = lax.rem(y_lo + dy, 2) * 64 + lax.rem(z + dz, NZ) * 16 + lax.rem(core + dc, 2) * 8

        def put(b, carry, n=n, first=first, begin=begin):
            goal = pl.multiple_of(owner_ref[1, first + b] * owned, owned)
            start = pl.multiple_of(begin + b * owned, owned)
            placed[pl.ds(goal, owned), :] = pieces[n][pl.ds(start, owned), :]
            return carry

        lax.fori_loop(0, blocks, put, 0)
    slab = width // groups
    t = lax.axis_index("tp")
    for k in range(NX):
        for j in range(2):
            at = lax.rem(t // 2 + k, NX) * 2 + lax.rem(lax.rem(t, 2) + j, 2)
            turned = placed[pl.ds(pl.multiple_of(at * slab, slab), slab), :].T
            rows = firsts[k].shape[1]
            firsts[k][j] = turned[:rows]
            seconds[j][k] = turned[rows : 2 * rows]


def place(pieces, spots, block_owner, groups, rows):
    width = sum(piece.shape[0] for piece in pieces)
    lanes = pieces[0].shape[1]
    vmem = pl.BlockSpec(memory_space=pltpu.VMEM)
    return pl.pallas_call(
        functools.partial(place_kernel, spots, groups),
        out_shape=[jax.ShapeDtypeStruct((2, rows, width // groups), jnp.bfloat16)] * NX
        + [jax.ShapeDtypeStruct((NX, rows, width // groups), jnp.bfloat16)] * 2,
        in_specs=[pl.BlockSpec(memory_space=pltpu.SMEM)] + [vmem] * len(pieces),
        out_specs=[vmem] * (NX + 2),
        scratch_shapes=[pltpu.VMEM((width, lanes), jnp.bfloat16)],
        compiler_params=pltpu.CompilerParams(vmem_limit_bytes=20 * MIB),
        cost_estimate=pl.CostEstimate(
            flops=0, bytes_accessed=8 * rows * width, transcendentals=0
        ),
        name="place",
    )(block_owner, *pieces)


def turns(lengths):
    half = HD // 2
    position = (lengths[None, :] + jnp.arange(2, dtype=jnp.int32)[:, None]).reshape(-1)
    freq = 1000000.0 ** (-jnp.arange(half, dtype=jnp.float32) * 2.0 / HD)
    angle = position.astype(jnp.float32)[:, None] * freq
    cosine, sine = jnp.cos(angle), jnp.sin(angle)
    return jnp.concatenate([cosine, cosine], axis=1), jnp.concatenate([-sine, sine], axis=1)


def attention_kernel(
    lengths_ref, p0, p1, p2, p3, cos_ref, sin_ref, cache_ref, out_ref, query, keys, values, result
):
    step = pl.program_id(0)
    both = p0.shape[0]
    rows = both // 2
    heads = out_ref.shape[1] // HD
    lanes = 2 * heads
    span = GROUP * lanes

    @pl.when(step == 0)
    def _():
        cosine, sine = cos_ref[...], sin_ref[...]

        def part(begin):
            cut = slice(begin * HD, (begin + 1) * HD)
            total = p0[:, cut] + p1[:, cut].astype(jnp.float32)
            return total + p2[:, cut].astype(jnp.float32) + p3[:, cut].astype(jnp.float32)

        def turn(x):
            return x * cosine + pltpu.roll(x, HD // 2, 1) * sine

        for h in range(heads):
            turned = turn(part(h))
            for s in range(2):
                query[pl.ds(s * heads + h, rows, stride=lanes), :] = turned[
                    s * rows : (s + 1) * rows
                ]
        new_keys, new_values = turn(part(heads)), part(heads + 1)
        for g in range(rows // GROUP):
            for t in range(2):
                to = slice((2 * g + t) * GROUP, (2 * g + t + 1) * GROUP)
                begin = t * rows + g * GROUP
                keys[to] = new_keys[begin : begin + GROUP]
                values[to] = new_values[begin : begin + GROUP]

    factor = 1.0 / math.sqrt(HD)
    nt = (((1,), (1,)), ((), ()))
    at = pl.ds(pl.multiple_of(step * span, span), span)
    fresh_at = pl.ds(pl.multiple_of(step * 2 * GROUP, 2 * GROUP), 2 * GROUP)
    q = query[at, :].astype(jnp.bfloat16)
    fresh = (
        lax.dot_general(
            q, keys[fresh_at, :].astype(jnp.bfloat16), nt, preferred_element_type=jnp.float32
        )
        * factor
    )
    of = lax.broadcasted_iota(jnp.int32, fresh.shape, 0)
    new = lax.broadcasted_iota(jnp.int32, fresh.shape, 1)
    seen = (of // lanes == new % GROUP) & (new // GROUP <= (of // heads) % 2)
    fresh = jnp.where(seen, fresh, -jnp.inf)

    held = cache_ref.shape[2]
    place = lax.broadcasted_iota(jnp.int32, (lanes, held), 1)
    pieces = []
    for r in range(GROUP):
        score = lax.dot_general(
            q[r * lanes : (r + 1) * lanes], cache_ref[0, r], nt, preferred_element_type=jnp.float32
        )
        pieces.append(jnp.where(place < lengths_ref[step * GROUP + r], score * factor, -jnp.inf))
    old = jnp.concatenate(pieces, axis=0)
    top = jnp.maximum(
        jnp.max(old, axis=1, keepdims=True), jnp.max(fresh, axis=1, keepdims=True)
    )
    old_w = jnp.exp(old - top)
    fresh_w = jnp.exp(fresh - top)
    total = jnp.sum(old_w, axis=1, keepdims=True) + jnp.sum(fresh_w, axis=1, keepdims=True)
    scale = 1.0 / total
    old_p = (old_w * scale).astype(jnp.bfloat16)
    fresh_p = (fresh_w * scale).astype(jnp.bfloat16)
    mixed = jnp.concatenate(
        [
            jnp.dot(
                old_p[r * lanes : (r + 1) * lanes],
                cache_ref[1, r],
                preferred_element_type=jnp.float32,
            )
            for r in range(GROUP)
        ],
        axis=0,
    )
    mixed = mixed + jnp.dot(
        fresh_p, values[fresh_at, :].astype(jnp.bfloat16), preferred_element_type=jnp.float32
    )
    result[at, :] = mixed

    @pl.when(step == pl.num_programs(0) - 1)
    def _():
        for h in range(heads):
            for s in range(2):
                out_ref[s * rows : (s + 1) * rows, h * HD : (h + 1) * HD] = result[
                    pl.ds(s * heads + h, rows, stride=lanes), :
                ].astype(out_ref.dtype)


def attention(sums, cos, sin, cache, lengths):
    both, cols = sums[0].shape
    rows = both // 2
    width = cols - 2 * HD
    held = cache.shape[2]
    lanes = 2 * width // HD

    def whole(*shape):
        return pl.BlockSpec(shape, lambda g: (0,) * len(shape))

    return pl.pallas_call(
        attention_kernel,
        grid=(rows // GROUP,),
        out_shape=jax.ShapeDtypeStruct((both, width), jnp.bfloat16),
        in_specs=[pl.BlockSpec(memory_space=pltpu.SMEM)]
        + [whole(both, cols)] * NZ
        + [whole(both, HD)] * 2
        + [pl.BlockSpec((2, GROUP, held, HD), lambda g: (0, g, 0, 0))],
        out_specs=whole(both, width),
        scratch_shapes=[
            pltpu.VMEM((rows * lanes, HD), jnp.float32),
            pltpu.VMEM((both, HD), jnp.float32),
            pltpu.VMEM((both, HD), jnp.float32),
            pltpu.VMEM((rows * lanes, HD), jnp.float32),
        ],
        compiler_params=pltpu.CompilerParams(vmem_limit_bytes=48 * MIB),
        cost_estimate=pl.CostEstimate(
            flops=4 * rows * lanes * held * HD,
            bytes_accessed=16 * rows * held * HD,
            transcendentals=rows * lanes * held,
        ),
        name="attention",
    )(lengths, *sums, cos, sin, cache)


def after(values, *first):
    return lax.optimization_barrier((*values, *first))[: len(values)]


def body(hidden, qkv_rows, o_rows, block_owner, cache, lengths):
    groups = lax.axis_size("tp")
    steps, rows, width = hidden.shape
    owned = qkv_rows.shape[0]
    query_cols = HQ * HD
    kv_cols = HK * HD
    cols = (query_cols + 2 * kv_cols) // groups
    copy = slabs_of(qkv_rows, o_rows, groups)

    cos, sin = turns(lengths)
    parts = shuffle(hidden.reshape(steps * rows, width), block_owner)
    parts = [parts[0]] + [z_shift(parts[k], k) for k in range(1, NZ)]

    both = lax.all_to_all(copy, "tp", split_axis=0, concat_axis=0, tiled=True)
    both = both.reshape(groups * owned, -1)
    w, own = both[:, :cols], both[:, cols:]
    half = own.shape[0] // 2

    w_y, w_c = flip(w, 8), flip(w, 1)
    own, cos, sin, *parts = lax.optimization_barrier((own, cos, sin, *parts))
    below, above = z_shift(own, 1), z_shift(own, -1)
    begun = partials(parts, (w, w_c))
    below, above, *begun = lax.optimization_barrier((below, above, *begun))
    above_a, below_b = above[:half], below[half:]
    w_y, own, above_a, below_b = lax.optimization_barrier((w_y, own, above_a, below_b))
    w_yc = flip(w_y, 1)
    far_a, far_b = z_shift(above_a, -1), z_shift(below_b, 1)
    across = flip(own, 8)

    sums = partials(parts, (w_y, w_yc), begun)
    sums = [sums[0]] + [z_shift(sums[k], -k) for k in range(1, NZ)]
    far_a, far_b, across = after((far_a, far_b, across))
    far = jnp.concatenate([far_a, far_b])
    across_far = flip(far, 8)
    (across,) = after((across,), *sums)
    across_below, across_above = z_shift(across, 1), z_shift(across, -1)
    mixed = attention(sums, cos, sin, cache, lengths)

    mixed_c = flip(mixed, 1)
    sources = (own, below, above, across, far, across_far, across_below, across_above)
    parts_of = (sources[:5], sources[5:])
    theirs = [terms_of(mixed_c, part) for part in parts_of]
    mine = terms_of(*after((mixed,), *theirs), sources)
    pieces = (mine, *(flip(value, 1) for value in theirs))
    places = ((0, 0), (0, 3), (0, 1), (1, 0), (0, 2), (1, 2), (1, 3), (1, 1))
    spots = []
    for core in range(2):
        begin, piece = 0, core
        for n, ((dy, dz), source) in enumerate(zip(places, sources)):
            if core == 1 and n == len(parts_of[0]):
                begin, piece = 0, 2
            size = source.shape[0]
            spots.append((piece, dy, dz, core, size // owned, begin))
            begin += size
    slabs = place(pieces, tuple(spots), block_owner, groups, rows)

    first = [slabs[0]] + [x_shift(slabs[k], k) for k in range(1, NX)]
    second = [slabs[NX], y_flip(slabs[NX + 1])]
    first = sum(value.astype(jnp.float32) for value in first)
    second = sum(value.astype(jnp.float32) for value in second)
    first = first[0] + y_flip(first[1].astype(jnp.bfloat16)).astype(jnp.float32)
    second = [second[0]] + [x_shift(second[k].astype(jnp.bfloat16), k) for k in range(1, NX)]
    second = sum(value.astype(jnp.float32) for value in second)
    return jnp.stack([first, second]).astype(jnp.bfloat16)


def solution(mesh):
    in_specs = (
        P(None, "fsdp", None),
        P(("fsdp", "tp"), None),
        P(("fsdp", "tp"), None),
        P(),
        P(None, "fsdp", None, "tp"),
        P("fsdp"),
    )
    out_specs = P(None, "fsdp", "tp")
    return jax.shard_map(body, mesh=mesh, in_specs=in_specs, out_specs=out_specs, check_vma=False)
```

```python
import functools
import math

import jax
import jax.numpy as jnp
from jax import lax
from jax.experimental import pallas as pl
from jax.experimental.pallas import tpu as pltpu
from jax.sharding import PartitionSpec as P

HQ = 64
HK = 8
HD = 128
NZ = 4
NX = 4
GROUP = 8
CHUNK = 512
MIB = 1024 * 1024


def z_shift(value, k):
    pairs = [(f, (f // 8) * 8 + ((f // 2 + k) % NZ) * 2 + f % 2) for f in range(16)]
    return lax.ppermute(value, "fsdp", pairs)


def flip(value, bit):
    return lax.ppermute(value, "fsdp", [(f, f ^ bit) for f in range(16)])


def x_shift(value, k):
    return lax.ppermute(value, "tp", [(t, (t // 2 + k) % NX * 2 + t % 2) for t in range(2 * NX)])


def y_flip(value):
    return lax.ppermute(value, "tp", [(t, t ^ 1) for t in range(2 * NX)])


def slabs_kernel(query, key, value, back, out_ref):
    begin = 0
    for ref in (query, key, value, back):
        width = ref.shape[1] // out_ref.shape[0]
        for g in range(out_ref.shape[0]):
            part = ref[:, g * width : (g + 1) * width]
            out_ref[g, :, begin : begin + width] = part.astype(out_ref.dtype)
        begin += width


def slabs_of(qkv_rows, o_rows, groups):
    owned = qkv_rows.shape[0]
    query_cols = HQ * HD
    each = 1
    wide, narrow = each * query_cols // groups, each * HK * HD // groups
    keys_at = query_cols // narrow
    values_at = keys_at + HK * HD // narrow
    cols = (2 * wide + 2 * narrow) // each
    return pl.pallas_call(
        slabs_kernel,
        grid=(groups // each,),
        out_shape=jax.ShapeDtypeStruct((groups, owned, cols), jnp.bfloat16),
        in_specs=[
            pl.BlockSpec((owned, wide), lambda g: (0, g)),
            pl.BlockSpec((owned, narrow), lambda g: (0, keys_at + g)),
            pl.BlockSpec((owned, narrow), lambda g: (0, values_at + g)),
            pl.BlockSpec((owned, wide), lambda g: (0, g)),
        ],
        out_specs=pl.BlockSpec((each, owned, cols), lambda g: (g, 0, 0)),
        compiler_params=pltpu.CompilerParams(vmem_limit_bytes=60 * MIB),
        cost_estimate=pl.CostEstimate(
            flops=0, bytes_accessed=6 * groups * owned * cols, transcendentals=0
        ),
        name="slabs",
    )(qkv_rows, qkv_rows, qkv_rows, o_rows)


def shuffle_kernel(owner_ref, hidden_ref, *out_refs):
    f = lax.axis_index("fsdp")
    y_lo, z, core = f // 8, lax.rem(f // 2, 4), lax.rem(f, 2)
    rows = hidden_ref.shape[0]
    low = lax.broadcasted_iota(jnp.int32, (rows, 128), 1) < 64

    for k, out_ref in enumerate(out_refs):
        zz = lax.rem(z + k, 4)

        def step(n, carry, zz=zz, out_ref=out_ref):
            q, p = n // 4, lax.rem(n, 4)
            yy = lax.rem(y_lo + q // 2, 2)
            cc = lax.rem(core + lax.rem(q, 2), 2)
            i = yy * 64 + zz * 16 + cc * 8 + 2 * p
            s0, s1 = owner_ref[0, i], owner_ref[0, i + 1]
            a = hidden_ref[:, pl.ds(pl.multiple_of((s0 // 2) * 128, 128), 128)].astype(jnp.float32)
            b = hidden_ref[:, pl.ds(pl.multiple_of((s1 // 2) * 128, 128), 128)].astype(jnp.float32)
            a = pltpu.roll(a, 64 * lax.rem(s0, 2), 1)
            b = pltpu.roll(b, 64 * (1 - lax.rem(s1, 2)), 1)
            out_ref[:, pl.ds(pl.multiple_of(n * 128, 128), 128)] = jnp.where(low, a, b).astype(
                jnp.bfloat16
            )
            return carry

        lax.fori_loop(0, 16, step, 0, unroll=8)


def shuffle(hidden, block_owner):
    rows, width = hidden.shape
    part = jax.ShapeDtypeStruct((rows, width // NZ), jnp.bfloat16)
    return pl.pallas_call(
        shuffle_kernel,
        out_shape=[part] * NZ,
        in_specs=[
            pl.BlockSpec(memory_space=pltpu.SMEM),
            pl.BlockSpec(memory_space=pltpu.VMEM),
        ],
        out_specs=[pl.BlockSpec(memory_space=pltpu.VMEM)] * NZ,
        compiler_params=pltpu.CompilerParams(vmem_limit_bytes=14 * MIB),
        cost_estimate=pl.CostEstimate(
            flops=rows * width * 8, bytes_accessed=4 * rows * width, transcendentals=0
        ),
        name="shuffle",
    )(block_owner, hidden)


def partial_kernel(begun, *refs):
    held, weights = refs[:NZ], refs[NZ : NZ + 2]
    totals = refs[NZ + 2 : 2 * NZ + 2] if begun else ()
    *outs, stacked = refs[NZ + 2 + len(totals) :]
    rows = held[0].shape[0]
    depth = weights[0].shape[0]

    @pl.when(pl.program_id(0) == 0)
    def _():
        for k, h in enumerate(held):
            stacked[pl.ds(k * rows, rows), :] = h[...]

    total = jnp.dot(stacked[:, :depth], weights[0][...], preferred_element_type=jnp.float32)
    total = total + jnp.dot(
        stacked[:, depth:], weights[1][...], preferred_element_type=jnp.float32
    )
    for k, out in enumerate(outs):
        part = total[k * rows : (k + 1) * rows]
        if begun:
            part = part + totals[k][...]
        out[...] = part.astype(out.dtype)


def partials(parts, weights, totals=()):
    rows, width = parts[0].shape
    depth, cols = weights[0].shape
    tile = 256
    begun = len(totals) > 0
    place = 1 if begun else 0
    block = pl.BlockSpec((rows, tile), lambda j: (0, j))
    types = [jnp.float32] + [jnp.bfloat16 if begun else jnp.float32] * (NZ - 1)
    return pl.pallas_call(
        functools.partial(partial_kernel, begun),
        grid=(cols // tile,),
        out_shape=[jax.ShapeDtypeStruct((rows, cols), kind) for kind in types],
        in_specs=[pl.BlockSpec((rows, width // 2), lambda j: (0, place))] * NZ
        + [pl.BlockSpec((depth, tile), lambda j: (0, j))] * 2
        + [block] * len(totals),
        out_specs=[block] * NZ,
        scratch_shapes=[pltpu.VMEM((NZ * rows, width // 2), jnp.bfloat16)],
        compiler_params=pltpu.CompilerParams(vmem_limit_bytes=14 * MIB),
        cost_estimate=pl.CostEstimate(
            flops=NZ * rows * width * cols,
            bytes_accessed=NZ * rows * width + width * cols + 4 * NZ * rows * cols,
            transcendentals=0,
        ),
        name="partials_rest" if begun else "partials",
    )(*parts, *weights, *totals)


def terms_kernel(mixed_ref, *refs):
    *sources, out_ref = refs
    spare = out_ref.shape[1] - mixed_ref.shape[0]
    wide = jnp.pad(mixed_ref[...].astype(jnp.float32), ((0, spare), (0, 0)))
    turned = wide.T.astype(jnp.bfloat16)
    begin = 0
    for source in sources:
        size = source.shape[0]
        chunk = min(CHUNK, size)

        def multiply(n, carry, source=source, begin=begin, chunk=chunk):
            rows = source[pl.ds(pl.multiple_of(n * chunk, chunk), chunk), :]
            to = pl.ds(pl.multiple_of(begin + n * chunk, chunk), chunk)
            out_ref[to, :] = jnp.dot(rows, turned, preferred_element_type=jnp.float32).astype(
                out_ref.dtype
            )
            return carry

        lax.fori_loop(0, size // chunk, multiply, 0)
        begin += size


def terms_of(mixed, sources):
    rows, depth = mixed.shape
    width = sum(source.shape[0] for source in sources)
    lanes = -(-rows // 128) * 128
    vmem = pl.BlockSpec(memory_space=pltpu.VMEM)
    return pl.pallas_call(
        terms_kernel,
        out_shape=jax.ShapeDtypeStruct((width, lanes), jnp.bfloat16),
        in_specs=[vmem] * (1 + len(sources)),
        out_specs=vmem,
        compiler_params=pltpu.CompilerParams(vmem_limit_bytes=20 * MIB),
        cost_estimate=pl.CostEstimate(flops=0, bytes_accessed=rows, transcendentals=0),
        name="terms",
    )(mixed, *sources)


def place_kernel(spots, groups, owner_ref, *refs):
    pieces, firsts, seconds = refs[:-7], refs[-7:-3], refs[-3:-1]
    placed = refs[-1]
    f = lax.axis_index("fsdp")
    y_lo, z, core = f // 8, lax.rem(f // 2, NZ), lax.rem(f, 2)
    width = placed.shape[0]
    owned = width // owner_ref.shape[1]
    for n, dy, dz, dc, blocks, begin in spots:
        first = lax.rem(y_lo + dy, 2) * 64 + lax.rem(z + dz, NZ) * 16 + lax.rem(core + dc, 2) * 8

        def put(b, carry, n=n, first=first, begin=begin):
            goal = pl.multiple_of(owner_ref[1, first + b] * owned, owned)
            start = pl.multiple_of(begin + b * owned, owned)
            placed[pl.ds(goal, owned), :] = pieces[n][pl.ds(start, owned), :]
            return carry

        lax.fori_loop(0, blocks, put, 0)
    slab = width // groups
    t = lax.axis_index("tp")
    for k in range(NX):
        for j in range(2):
            at = lax.rem(t // 2 + k, NX) * 2 + lax.rem(lax.rem(t, 2) + j, 2)
            turned = placed[pl.ds(pl.multiple_of(at * slab, slab), slab), :].T
            rows = firsts[k].shape[1]
            firsts[k][j] = turned[:rows]
            seconds[j][k] = turned[rows : 2 * rows]


def place(pieces, spots, block_owner, groups, rows):
    width = sum(piece.shape[0] for piece in pieces)
    lanes = pieces[0].shape[1]
    vmem = pl.BlockSpec(memory_space=pltpu.VMEM)
    return pl.pallas_call(
        functools.partial(place_kernel, spots, groups),
        out_shape=[jax.ShapeDtypeStruct((2, rows, width // groups), jnp.bfloat16)] * NX
        + [jax.ShapeDtypeStruct((NX, rows, width // groups), jnp.bfloat16)] * 2,
        in_specs=[pl.BlockSpec(memory_space=pltpu.SMEM)] + [vmem] * len(pieces),
        out_specs=[vmem] * (NX + 2),
        scratch_shapes=[pltpu.VMEM((width, lanes), jnp.bfloat16)],
        compiler_params=pltpu.CompilerParams(vmem_limit_bytes=20 * MIB),
        cost_estimate=pl.CostEstimate(
            flops=0, bytes_accessed=8 * rows * width, transcendentals=0
        ),
        name="place",
    )(block_owner, *pieces)


def turns(lengths):
    half = HD // 2
    position = (lengths[None, :] + jnp.arange(2, dtype=jnp.int32)[:, None]).reshape(-1)
    freq = 1000000.0 ** (-jnp.arange(half, dtype=jnp.float32) * 2.0 / HD)
    angle = position.astype(jnp.float32)[:, None] * freq
    cosine, sine = jnp.cos(angle), jnp.sin(angle)
    return jnp.concatenate([cosine, cosine], axis=1), jnp.concatenate([-sine, sine], axis=1)


def attention_kernel(
    lengths_ref, p0, p1, p2, p3, cos_ref, sin_ref, cache_ref, out_ref, query, keys, values, result
):
    step = pl.program_id(0)
    both = p0.shape[0]
    rows = both // 2
    heads = out_ref.shape[1] // HD
    lanes = 2 * heads
    span = GROUP * lanes

    @pl.when(step == 0)
    def _():
        cosine, sine = cos_ref[...], sin_ref[...]

        def part(begin):
            cut = slice(begin * HD, (begin + 1) * HD)
            total = p0[:, cut] + p1[:, cut].astype(jnp.float32)
            return total + p2[:, cut].astype(jnp.float32) + p3[:, cut].astype(jnp.float32)

        def turn(x):
            return x * cosine + pltpu.roll(x, HD // 2, 1) * sine

        for h in range(heads):
            turned = turn(part(h))
            for s in range(2):
                query[pl.ds(s * heads + h, rows, stride=lanes), :] = turned[
                    s * rows : (s + 1) * rows
                ]
        new_keys, new_values = turn(part(heads)), part(heads + 1)
        for g in range(rows // GROUP):
            for t in range(2):
                to = slice((2 * g + t) * GROUP, (2 * g + t + 1) * GROUP)
                begin = t * rows + g * GROUP
                keys[to] = new_keys[begin : begin + GROUP]
                values[to] = new_values[begin : begin + GROUP]

    factor = 1.0 / math.sqrt(HD)
    nt = (((1,), (1,)), ((), ()))
    at = pl.ds(pl.multiple_of(step * span, span), span)
    fresh_at = pl.ds(pl.multiple_of(step * 2 * GROUP, 2 * GROUP), 2 * GROUP)
    q = query[at, :].astype(jnp.bfloat16)
    fresh = (
        lax.dot_general(
            q, keys[fresh_at, :].astype(jnp.bfloat16), nt, preferred_element_type=jnp.float32
        )
        * factor
    )
    of = lax.broadcasted_iota(jnp.int32, fresh.shape, 0)
    new = lax.broadcasted_iota(jnp.int32, fresh.shape, 1)
    seen = (of // lanes == new % GROUP) & (new // GROUP <= (of // heads) % 2)
    fresh = jnp.where(seen, fresh, -jnp.inf)

    held = cache_ref.shape[2]
    place = lax.broadcasted_iota(jnp.int32, (lanes, held), 1)
    pieces = []
    for r in range(GROUP):
        score = lax.dot_general(
            q[r * lanes : (r + 1) * lanes], cache_ref[0, r], nt, preferred_element_type=jnp.float32
        )
        pieces.append(jnp.where(place < lengths_ref[step * GROUP + r], score * factor, -jnp.inf))
    old = jnp.concatenate(pieces, axis=0)
    top = jnp.maximum(
        jnp.max(old, axis=1, keepdims=True), jnp.max(fresh, axis=1, keepdims=True)
    )
    old_w = jnp.exp(old - top)
    fresh_w = jnp.exp(fresh - top)
    total = jnp.sum(old_w, axis=1, keepdims=True) + jnp.sum(fresh_w, axis=1, keepdims=True)
    scale = 1.0 / total
    old_p = (old_w * scale).astype(jnp.bfloat16)
    fresh_p = (fresh_w * scale).astype(jnp.bfloat16)
    mixed = jnp.concatenate(
        [
            jnp.dot(
                old_p[r * lanes : (r + 1) * lanes],
                cache_ref[1, r],
                preferred_element_type=jnp.float32,
            )
            for r in range(GROUP)
        ],
        axis=0,
    )
    mixed = mixed + jnp.dot(
        fresh_p, values[fresh_at, :].astype(jnp.bfloat16), preferred_element_type=jnp.float32
    )
    result[at, :] = mixed

    @pl.when(step == pl.num_programs(0) - 1)
    def _():
        for h in range(heads):
            for s in range(2):
                out_ref[s * rows : (s + 1) * rows, h * HD : (h + 1) * HD] = result[
                    pl.ds(s * heads + h, rows, stride=lanes), :
                ].astype(out_ref.dtype)


def attention(sums, cos, sin, cache, lengths):
    both, cols = sums[0].shape
    rows = both // 2
    width = cols - 2 * HD
    held = cache.shape[2]
    lanes = 2 * width // HD

    def whole(*shape):
        return pl.BlockSpec(shape, lambda g: (0,) * len(shape))

    return pl.pallas_call(
        attention_kernel,
        grid=(rows // GROUP,),
        out_shape=jax.ShapeDtypeStruct((both, width), jnp.bfloat16),
        in_specs=[pl.BlockSpec(memory_space=pltpu.SMEM)]
        + [whole(both, cols)] * NZ
        + [whole(both, HD)] * 2
        + [pl.BlockSpec((2, GROUP, held, HD), lambda g: (0, g, 0, 0))],
        out_specs=whole(both, width),
        scratch_shapes=[
            pltpu.VMEM((rows * lanes, HD), jnp.float32),
            pltpu.VMEM((both, HD), jnp.float32),
            pltpu.VMEM((both, HD), jnp.float32),
            pltpu.VMEM((rows * lanes, HD), jnp.float32),
        ],
        compiler_params=pltpu.CompilerParams(vmem_limit_bytes=48 * MIB),
        cost_estimate=pl.CostEstimate(
            flops=4 * rows * lanes * held * HD,
            bytes_accessed=16 * rows * held * HD,
            transcendentals=rows * lanes * held,
        ),
        name="attention",
    )(lengths, *sums, cos, sin, cache)


def after(values, *first):
    return lax.optimization_barrier((*values, *first))[: len(values)]


def body(hidden, qkv_rows, o_rows, block_owner, cache, lengths):
    groups = lax.axis_size("tp")
    steps, rows, width = hidden.shape
    owned = qkv_rows.shape[0]
    query_cols = HQ * HD
    kv_cols = HK * HD
    cols = (query_cols + 2 * kv_cols) // groups
    copy = slabs_of(qkv_rows, o_rows, groups)

    cos, sin = turns(lengths)
    parts = shuffle(hidden.reshape(steps * rows, width), block_owner)
    parts = [parts[0]] + [z_shift(parts[k], k) for k in range(1, NZ)]

    both = lax.all_to_all(copy, "tp", split_axis=0, concat_axis=0, tiled=True)
    both = both.reshape(groups * owned, -1)
    w, own = both[:, :cols], both[:, cols:]
    half = own.shape[0] // 2

    w_y, w_c = flip(w, 8), flip(w, 1)
    own, cos, sin, *parts = lax.optimization_barrier((own, cos, sin, *parts))
    below, above = z_shift(own, 1), z_shift(own, -1)
    begun = partials(parts, (w, w_c))
    below, above, *begun = lax.optimization_barrier((below, above, *begun))
    above_a, below_b = above[:half], below[half:]
    w_y, own, above_a, below_b = lax.optimization_barrier((w_y, own, above_a, below_b))
    w_yc = flip(w_y, 1)
    far_a, far_b = z_shift(above_a, -1), z_shift(below_b, 1)
    across = flip(own, 8)

    sums = partials(parts, (w_y, w_yc), begun)
    sums = [sums[0]] + [z_shift(sums[k], -k) for k in range(1, NZ)]
    far_a, far_b, across = after((far_a, far_b, across))
    far = jnp.concatenate([far_a, far_b])
    across_far = flip(far, 8)
    (across,) = after((across,), *sums)
    across_below, across_above = z_shift(across, 1), z_shift(across, -1)
    mixed = attention(sums, cos, sin, cache, lengths)

    mixed_c = flip(mixed, 1)
    sources = (own, below, above, across, far, across_far, across_below, across_above)
    parts_of = (sources[:5], sources[5:])
    early, late = parts_of
    theirs = [terms_of(mixed_c, early)]
    mine = [terms_of(*after((mixed,), theirs[0]), early)]
    theirs.append(terms_of(*after((mixed_c,), mine[0]), late))
    mine.append(terms_of(*after((mixed,), theirs[1]), late))
    pieces = (*mine, *(flip(value, 1) for value in theirs))
    places = ((0, 0), (0, 3), (0, 1), (1, 0), (0, 2), (1, 2), (1, 3), (1, 1))
    spots = []
    for core in range(2):
        begin, piece = 0, 2 * core
        for n, ((dy, dz), source) in enumerate(zip(places, sources)):
            if n == len(parts_of[0]):
                begin, piece = 0, 2 * core + 1
            size = source.shape[0]
            spots.append((piece, dy, dz, core, size // owned, begin))
            begin += size
    slabs = place(pieces, tuple(spots), block_owner, groups, rows)

    first = [slabs[0]] + [x_shift(slabs[k], k) for k in range(1, NX)]
    second = [slabs[NX], y_flip(slabs[NX + 1])]
    first = sum(value.astype(jnp.float32) for value in first)
    second = sum(value.astype(jnp.float32) for value in second)
    first = first[0] + y_flip(first[1].astype(jnp.bfloat16)).astype(jnp.float32)
    second = [second[0]] + [x_shift(second[k].astype(jnp.bfloat16), k) for k in range(1, NX)]
    second = sum(value.astype(jnp.float32) for value in second)
    return jnp.stack([first, second]).astype(jnp.bfloat16)


def solution(mesh):
    in_specs = (
        P(None, "fsdp", None),
        P(("fsdp", "tp"), None),
        P(("fsdp", "tp"), None),
        P(),
        P(None, "fsdp", None, "tp"),
        P("fsdp"),
    )
    out_specs = P(None, "fsdp", "tp")
    return jax.shard_map(body, mesh=mesh, in_specs=in_specs, out_specs=out_specs, check_vma=False)
```

```python
import functools
import math

import jax
import jax.numpy as jnp
from jax import lax
from jax.experimental import pallas as pl
from jax.experimental.pallas import tpu as pltpu
from jax.sharding import PartitionSpec as P

HQ = 64
HK = 8
HD = 128
NZ = 4
NX = 4
GROUP = 8
CHUNK = 512
MIB = 1024 * 1024


def z_shift(value, k):
    pairs = [(f, (f // 8) * 8 + ((f // 2 + k) % NZ) * 2 + f % 2) for f in range(16)]
    return lax.ppermute(value, "fsdp", pairs)


def flip(value, bit):
    return lax.ppermute(value, "fsdp", [(f, f ^ bit) for f in range(16)])


def x_shift(value, k):
    return lax.ppermute(value, "tp", [(t, (t // 2 + k) % NX * 2 + t % 2) for t in range(2 * NX)])


def y_flip(value):
    return lax.ppermute(value, "tp", [(t, t ^ 1) for t in range(2 * NX)])


def slabs_kernel(query, key, value, back, out_ref):
    begin = 0
    for ref in (query, key, value, back):
        width = ref.shape[1] // out_ref.shape[0]
        for g in range(out_ref.shape[0]):
            part = ref[:, g * width : (g + 1) * width]
            out_ref[g, :, begin : begin + width] = part.astype(out_ref.dtype)
        begin += width


def slabs_of(qkv_rows, o_rows, groups):
    owned = qkv_rows.shape[0]
    query_cols = HQ * HD
    each = 4
    wide, narrow = each * query_cols // groups, each * HK * HD // groups
    keys_at = query_cols // narrow
    values_at = keys_at + HK * HD // narrow
    cols = (2 * wide + 2 * narrow) // each
    return pl.pallas_call(
        slabs_kernel,
        grid=(groups // each,),
        out_shape=jax.ShapeDtypeStruct((groups, owned, cols), jnp.bfloat16),
        in_specs=[
            pl.BlockSpec((owned, wide), lambda g: (0, g)),
            pl.BlockSpec((owned, narrow), lambda g: (0, keys_at + g)),
            pl.BlockSpec((owned, narrow), lambda g: (0, values_at + g)),
            pl.BlockSpec((owned, wide), lambda g: (0, g)),
        ],
        out_specs=pl.BlockSpec((each, owned, cols), lambda g: (g, 0, 0)),
        compiler_params=pltpu.CompilerParams(vmem_limit_bytes=60 * MIB),
        cost_estimate=pl.CostEstimate(
            flops=0, bytes_accessed=6 * groups * owned * cols, transcendentals=0
        ),
        name="slabs",
    )(qkv_rows, qkv_rows, qkv_rows, o_rows)


def shuffle_kernel(owner_ref, hidden_ref, *out_refs):
    f = lax.axis_index("fsdp")
    y_lo, z, core = f // 8, lax.rem(f // 2, 4), lax.rem(f, 2)
    rows = hidden_ref.shape[0]
    low = lax.broadcasted_iota(jnp.int32, (rows, 128), 1) < 64

    for k, out_ref in enumerate(out_refs):
        zz = lax.rem(z + k, 4)

        def step(n, carry, zz=zz, out_ref=out_ref):
            q, p = n // 4, lax.rem(n, 4)
            yy = lax.rem(y_lo + q // 2, 2)
            cc = lax.rem(core + lax.rem(q, 2), 2)
            i = yy * 64 + zz * 16 + cc * 8 + 2 * p
            s0, s1 = owner_ref[0, i], owner_ref[0, i + 1]
            a = hidden_ref[:, pl.ds(pl.multiple_of((s0 // 2) * 128, 128), 128)].astype(jnp.float32)
            b = hidden_ref[:, pl.ds(pl.multiple_of((s1 // 2) * 128, 128), 128)].astype(jnp.float32)
            a = pltpu.roll(a, 64 * lax.rem(s0, 2), 1)
            b = pltpu.roll(b, 64 * (1 - lax.rem(s1, 2)), 1)
            out_ref[:, pl.ds(pl.multiple_of(n * 128, 128), 128)] = jnp.where(low, a, b).astype(
                jnp.bfloat16
            )
            return carry

        lax.fori_loop(0, 16, step, 0, unroll=8)


def shuffle(hidden, block_owner):
    rows, width = hidden.shape
    part = jax.ShapeDtypeStruct((rows, width // NZ), jnp.bfloat16)
    return pl.pallas_call(
        shuffle_kernel,
        out_shape=[part] * NZ,
        in_specs=[
            pl.BlockSpec(memory_space=pltpu.SMEM),
            pl.BlockSpec(memory_space=pltpu.VMEM),
        ],
        out_specs=[pl.BlockSpec(memory_space=pltpu.VMEM)] * NZ,
        compiler_params=pltpu.CompilerParams(vmem_limit_bytes=14 * MIB),
        cost_estimate=pl.CostEstimate(
            flops=rows * width * 8, bytes_accessed=4 * rows * width, transcendentals=0
        ),
        name="shuffle",
    )(block_owner, hidden)


def partial_kernel(begun, *refs):
    held, weights = refs[:NZ], refs[NZ : NZ + 2]
    totals = refs[NZ + 2 : 2 * NZ + 2] if begun else ()
    *outs, stacked = refs[NZ + 2 + len(totals) :]
    rows = held[0].shape[0]
    depth = weights[0].shape[0]

    @pl.when(pl.program_id(0) == 0)
    def _():
        for k, h in enumerate(held):
            stacked[pl.ds(k * rows, rows), :] = h[...]

    total = jnp.dot(stacked[:, :depth], weights[0][...], preferred_element_type=jnp.float32)
    total = total + jnp.dot(
        stacked[:, depth:], weights[1][...], preferred_element_type=jnp.float32
    )
    for k, out in enumerate(outs):
        part = total[k * rows : (k + 1) * rows]
        if begun:
            part = part + totals[k][...]
        out[...] = part.astype(out.dtype)


def partials(parts, weights, totals=()):
    rows, width = parts[0].shape
    depth, cols = weights[0].shape
    tile = 256
    begun = len(totals) > 0
    place = 1 if begun else 0
    block = pl.BlockSpec((rows, tile), lambda j: (0, j))
    types = [jnp.float32] + [jnp.bfloat16 if begun else jnp.float32] * (NZ - 1)
    return pl.pallas_call(
        functools.partial(partial_kernel, begun),
        grid=(cols // tile,),
        out_shape=[jax.ShapeDtypeStruct((rows, cols), kind) for kind in types],
        in_specs=[pl.BlockSpec((rows, width // 2), lambda j: (0, place))] * NZ
        + [pl.BlockSpec((depth, tile), lambda j: (0, j))] * 2
        + [block] * len(totals),
        out_specs=[block] * NZ,
        scratch_shapes=[pltpu.VMEM((NZ * rows, width // 2), jnp.bfloat16)],
        compiler_params=pltpu.CompilerParams(vmem_limit_bytes=14 * MIB),
        cost_estimate=pl.CostEstimate(
            flops=NZ * rows * width * cols,
            bytes_accessed=NZ * rows * width + width * cols + 4 * NZ * rows * cols,
            transcendentals=0,
        ),
        name="partials_rest" if begun else "partials",
    )(*parts, *weights, *totals)


def terms_kernel(mixed_ref, *refs):
    *sources, out_ref = refs
    spare = out_ref.shape[1] - mixed_ref.shape[0]
    wide = jnp.pad(mixed_ref[...].astype(jnp.float32), ((0, spare), (0, 0)))
    turned = wide.T.astype(jnp.bfloat16)
    begin = 0
    for source in sources:
        size = source.shape[0]
        chunk = min(CHUNK, size)

        def multiply(n, carry, source=source, begin=begin, chunk=chunk):
            rows = source[pl.ds(pl.multiple_of(n * chunk, chunk), chunk), :]
            to = pl.ds(pl.multiple_of(begin + n * chunk, chunk), chunk)
            out_ref[to, :] = jnp.dot(rows, turned, preferred_element_type=jnp.float32).astype(
                out_ref.dtype
            )
            return carry

        lax.fori_loop(0, size // chunk, multiply, 0)
        begin += size


def terms_of(mixed, sources):
    rows, depth = mixed.shape
    width = sum(source.shape[0] for source in sources)
    lanes = -(-rows // 128) * 128
    vmem = pl.BlockSpec(memory_space=pltpu.VMEM)
    return pl.pallas_call(
        terms_kernel,
        out_shape=jax.ShapeDtypeStruct((width, lanes), jnp.bfloat16),
        in_specs=[vmem] * (1 + len(sources)),
        out_specs=vmem,
        compiler_params=pltpu.CompilerParams(vmem_limit_bytes=20 * MIB),
        cost_estimate=pl.CostEstimate(flops=0, bytes_accessed=rows, transcendentals=0),
        name="terms",
    )(mixed, *sources)


def place_kernel(spots, groups, owner_ref, *refs):
    pieces, firsts, seconds = refs[:-7], refs[-7:-3], refs[-3:-1]
    placed = refs[-1]
    f = lax.axis_index("fsdp")
    y_lo, z, core = f // 8, lax.rem(f // 2, NZ), lax.rem(f, 2)
    width = placed.shape[0]
    owned = width // owner_ref.shape[1]
    for n, dy, dz, dc, blocks, begin in spots:
        first = lax.rem(y_lo + dy, 2) * 64 + lax.rem(z + dz, NZ) * 16 + lax.rem(core + dc, 2) * 8

        def put(b, carry, n=n, first=first, begin=begin):
            goal = pl.multiple_of(owner_ref[1, first + b] * owned, owned)
            start = pl.multiple_of(begin + b * owned, owned)
            placed[pl.ds(goal, owned), :] = pieces[n][pl.ds(start, owned), :]
            return carry

        lax.fori_loop(0, blocks, put, 0)
    slab = width // groups
    t = lax.axis_index("tp")
    for k in range(NX):
        for j in range(2):
            at = lax.rem(t // 2 + k, NX) * 2 + lax.rem(lax.rem(t, 2) + j, 2)
            turned = placed[pl.ds(pl.multiple_of(at * slab, slab), slab), :].T
            rows = firsts[k].shape[1]
            firsts[k][j] = turned[:rows]
            seconds[j][k] = turned[rows : 2 * rows]


def place(pieces, spots, block_owner, groups, rows):
    width = sum(piece.shape[0] for piece in pieces)
    lanes = pieces[0].shape[1]
    vmem = pl.BlockSpec(memory_space=pltpu.VMEM)
    return pl.pallas_call(
        functools.partial(place_kernel, spots, groups),
        out_shape=[jax.ShapeDtypeStruct((2, rows, width // groups), jnp.bfloat16)] * NX
        + [jax.ShapeDtypeStruct((NX, rows, width // groups), jnp.bfloat16)] * 2,
        in_specs=[pl.BlockSpec(memory_space=pltpu.SMEM)] + [vmem] * len(pieces),
        out_specs=[vmem] * (NX + 2),
        scratch_shapes=[pltpu.VMEM((width, lanes), jnp.bfloat16)],
        compiler_params=pltpu.CompilerParams(vmem_limit_bytes=20 * MIB),
        cost_estimate=pl.CostEstimate(
            flops=0, bytes_accessed=8 * rows * width, transcendentals=0
        ),
        name="place",
    )(block_owner, *pieces)


def turns(lengths):
    half = HD // 2
    position = (lengths[None, :] + jnp.arange(2, dtype=jnp.int32)[:, None]).reshape(-1)
    freq = 1000000.0 ** (-jnp.arange(half, dtype=jnp.float32) * 2.0 / HD)
    angle = position.astype(jnp.float32)[:, None] * freq
    cosine, sine = jnp.cos(angle), jnp.sin(angle)
    return jnp.concatenate([cosine, cosine], axis=1), jnp.concatenate([-sine, sine], axis=1)


def attention_kernel(
    lengths_ref, p0, p1, p2, p3, cos_ref, sin_ref, cache_ref, out_ref, query, keys, values, result
):
    step = pl.program_id(0)
    both = p0.shape[0]
    rows = both // 2
    heads = out_ref.shape[1] // HD
    lanes = 2 * heads
    span = GROUP * lanes

    @pl.when(step == 0)
    def _():
        cosine, sine = cos_ref[...], sin_ref[...]

        def part(begin):
            cut = slice(begin * HD, (begin + 1) * HD)
            total = p0[:, cut] + p1[:, cut].astype(jnp.float32)
            return total + p2[:, cut].astype(jnp.float32) + p3[:, cut].astype(jnp.float32)

        def turn(x):
            return x * cosine + pltpu.roll(x, HD // 2, 1) * sine

        for h in range(heads):
            turned = turn(part(h))
            for s in range(2):
                query[pl.ds(s * heads + h, rows, stride=lanes), :] = turned[
                    s * rows : (s + 1) * rows
                ]
        new_keys, new_values = turn(part(heads)), part(heads + 1)
        for g in range(rows // GROUP):
            for t in range(2):
                to = slice((2 * g + t) * GROUP, (2 * g + t + 1) * GROUP)
                begin = t * rows + g * GROUP
                keys[to] = new_keys[begin : begin + GROUP]
                values[to] = new_values[begin : begin + GROUP]

    factor = 1.0 / math.sqrt(HD)
    nt = (((1,), (1,)), ((), ()))
    at = pl.ds(pl.multiple_of(step * span, span), span)
    fresh_at = pl.ds(pl.multiple_of(step * 2 * GROUP, 2 * GROUP), 2 * GROUP)
    q = query[at, :].astype(jnp.bfloat16)
    fresh = (
        lax.dot_general(
            q, keys[fresh_at, :].astype(jnp.bfloat16), nt, preferred_element_type=jnp.float32
        )
        * factor
    )
    of = lax.broadcasted_iota(jnp.int32, fresh.shape, 0)
    new = lax.broadcasted_iota(jnp.int32, fresh.shape, 1)
    seen = (of // lanes == new % GROUP) & (new // GROUP <= (of // heads) % 2)
    fresh = jnp.where(seen, fresh, -jnp.inf)

    held = cache_ref.shape[2]
    place = lax.broadcasted_iota(jnp.int32, (lanes, held), 1)
    pieces = []
    for r in range(GROUP):
        score = lax.dot_general(
            q[r * lanes : (r + 1) * lanes], cache_ref[0, r], nt, preferred_element_type=jnp.float32
        )
        pieces.append(jnp.where(place < lengths_ref[step * GROUP + r], score * factor, -jnp.inf))
    old = jnp.concatenate(pieces, axis=0)
    top = jnp.maximum(
        jnp.max(old, axis=1, keepdims=True), jnp.max(fresh, axis=1, keepdims=True)
    )
    old_w = jnp.exp(old - top)
    fresh_w = jnp.exp(fresh - top)
    total = jnp.sum(old_w, axis=1, keepdims=True) + jnp.sum(fresh_w, axis=1, keepdims=True)
    scale = 1.0 / total
    old_p = (old_w * scale).astype(jnp.bfloat16)
    fresh_p = (fresh_w * scale).astype(jnp.bfloat16)
    mixed = jnp.concatenate(
        [
            jnp.dot(
                old_p[r * lanes : (r + 1) * lanes],
                cache_ref[1, r],
                preferred_element_type=jnp.float32,
            )
            for r in range(GROUP)
        ],
        axis=0,
    )
    mixed = mixed + jnp.dot(
        fresh_p, values[fresh_at, :].astype(jnp.bfloat16), preferred_element_type=jnp.float32
    )
    result[at, :] = mixed

    @pl.when(step == pl.num_programs(0) - 1)
    def _():
        for h in range(heads):
            for s in range(2):
                out_ref[s * rows : (s + 1) * rows, h * HD : (h + 1) * HD] = result[
                    pl.ds(s * heads + h, rows, stride=lanes), :
                ].astype(out_ref.dtype)


def attention(sums, cos, sin, cache, lengths):
    both, cols = sums[0].shape
    rows = both // 2
    width = cols - 2 * HD
    held = cache.shape[2]
    lanes = 2 * width // HD

    def whole(*shape):
        return pl.BlockSpec(shape, lambda g: (0,) * len(shape))

    return pl.pallas_call(
        attention_kernel,
        grid=(rows // GROUP,),
        out_shape=jax.ShapeDtypeStruct((both, width), jnp.bfloat16),
        in_specs=[pl.BlockSpec(memory_space=pltpu.SMEM)]
        + [whole(both, cols)] * NZ
        + [whole(both, HD)] * 2
        + [pl.BlockSpec((2, GROUP, held, HD), lambda g: (0, g, 0, 0))],
        out_specs=whole(both, width),
        scratch_shapes=[
            pltpu.VMEM((rows * lanes, HD), jnp.float32),
            pltpu.VMEM((both, HD), jnp.float32),
            pltpu.VMEM((both, HD), jnp.float32),
            pltpu.VMEM((rows * lanes, HD), jnp.float32),
        ],
        compiler_params=pltpu.CompilerParams(vmem_limit_bytes=48 * MIB),
        cost_estimate=pl.CostEstimate(
            flops=4 * rows * lanes * held * HD,
            bytes_accessed=16 * rows * held * HD,
            transcendentals=rows * lanes * held,
        ),
        name="attention",
    )(lengths, *sums, cos, sin, cache)


def after(values, *first):
    return lax.optimization_barrier((*values, *first))[: len(values)]


def body(hidden, qkv_rows, o_rows, block_owner, cache, lengths):
    groups = lax.axis_size("tp")
    steps, rows, width = hidden.shape
    owned = qkv_rows.shape[0]
    query_cols = HQ * HD
    kv_cols = HK * HD
    cols = (query_cols + 2 * kv_cols) // groups
    copy = slabs_of(qkv_rows, o_rows, groups)

    cos, sin = turns(lengths)
    parts = shuffle(hidden.reshape(steps * rows, width), block_owner)
    parts = [parts[0]] + [z_shift(parts[k], k) for k in range(1, NZ)]

    both = lax.all_to_all(copy, "tp", split_axis=0, concat_axis=0, tiled=True)
    both = both.reshape(groups * owned, -1)
    w, own = both[:, :cols], both[:, cols:]
    half = own.shape[0] // 2

    w_y, w_c = flip(w, 8), flip(w, 1)
    own, cos, sin, *parts = lax.optimization_barrier((own, cos, sin, *parts))
    below, above = z_shift(own, 1), z_shift(own, -1)
    begun = partials(parts, (w, w_c))
    below, above, *begun = lax.optimization_barrier((below, above, *begun))
    above_a, below_b = above[:half], below[half:]
    w_y, own, above_a, below_b = lax.optimization_barrier((w_y, own, above_a, below_b))
    w_yc = flip(w_y, 1)
    far_a, far_b = z_shift(above_a, -1), z_shift(below_b, 1)
    across = flip(own, 8)

    sums = partials(parts, (w_y, w_yc), begun)
    sums = [sums[0]] + [z_shift(sums[k], -k) for k in range(1, NZ)]
    far_a, far_b, across = after((far_a, far_b, across))
    far = jnp.concatenate([far_a, far_b])
    across_far = flip(far, 8)
    (across,) = after((across,), *sums)
    across_below, across_above = z_shift(across, 1), z_shift(across, -1)
    mixed = attention(sums, cos, sin, cache, lengths)

    mixed_c = flip(mixed, 1)
    sources = (own, below, above, across, far, across_far, across_below, across_above)
    parts_of = (sources[:5], sources[5:])
    theirs = [terms_of(mixed_c, part) for part in parts_of]
    mine = terms_of(*after((mixed,), *theirs), sources)
    pieces = (mine, *(flip(value, 1) for value in theirs))
    places = ((0, 0), (0, 3), (0, 1), (1, 0), (0, 2), (1, 2), (1, 3), (1, 1))
    spots = []
    for core in range(2):
        begin, piece = 0, core
        for n, ((dy, dz), source) in enumerate(zip(places, sources)):
            if core == 1 and n == len(parts_of[0]):
                begin, piece = 0, 2
            size = source.shape[0]
            spots.append((piece, dy, dz, core, size // owned, begin))
            begin += size
    slabs = place(pieces, tuple(spots), block_owner, groups, rows)

    first = [slabs[0]] + [x_shift(slabs[k], k) for k in range(1, NX)]
    second = [slabs[NX], y_flip(slabs[NX + 1])]
    first = sum(value.astype(jnp.float32) for value in first)
    second = sum(value.astype(jnp.float32) for value in second)
    first = first[0] + y_flip(first[1].astype(jnp.bfloat16)).astype(jnp.float32)
    second = [second[0]] + [x_shift(second[k].astype(jnp.bfloat16), k) for k in range(1, NX)]
    second = sum(value.astype(jnp.float32) for value in second)
    return jnp.stack([first, second]).astype(jnp.bfloat16)


def solution(mesh):
    in_specs = (
        P(None, "fsdp", None),
        P(("fsdp", "tp"), None),
        P(("fsdp", "tp"), None),
        P(),
        P(None, "fsdp", None, "tp"),
        P("fsdp"),
    )
    out_specs = P(None, "fsdp", "tp")
    return jax.shard_map(body, mesh=mesh, in_specs=in_specs, out_specs=out_specs, check_vma=False)
```
